32 devices in a mesh: subj: 2 (over core), slab: 16 (over z, y, x).
Axes of the slice: x: 2, y: 2, z: 4, core: 2. Of those that a mesh axis runs over, the one named last changes fastest.
Arguments:
- template: float32 [64, 128, 512], P('slab', 'subj'), may hold values from -6 to 6
- subject: float32 [2, 64, 128, 512], P('subj', 'slab'), may hold values from -6 to 6
- velocity: float32 [2, 2, 3, 64, 128, 512], P('subj', None, None, 'slab'), may hold values from -0.6 to 0.6
Outputs:
- velocity_grad: float32 [2, 2, 3, 64, 128, 512], P('subj', None, None, 'slab')
- template_grad: float32 [64, 128, 512], P('slab', 'subj')
The draws below stay inside these ranges and needn't reach their ends.
All inputs are finite; a program needn't handle non-finite values.
Results may differ from the reference program's by a relative error of at most 0.0003.
Values sent between devices are 32-bit elements; how exact they have to be, the bound alone decides.
No kernel may reach another device: no remote copies, remote signals or barrier semaphores. Data moves between devices by JAX's collectives and lax.ppermute only.
A program may use at most 128 MiB of HBM per device.

```python
import jax
import jax.numpy as jnp
from jax import lax

NY = 128
NX = 512
TS = 2
SW = 3
NSUBJ = 2
NZ = 64


def block_scale(own_key, dims, cuts, least, largest):
    loudness, own = 1.0, jax.random.fold_in(own_key, 6)
    for dim, shards_of in cuts:
        steps = jnp.exp(jax.random.uniform(jax.random.fold_in(own, dim), (shards_of,), jnp.float32, least / len(cuts), largest / len(cuts)))
        loudness = loudness * jnp.repeat(steps, dims[dim] // shards_of).reshape([-1 if axis == dim else 1 for axis in range(len(dims))])
    return loudness


def scatter_about(own_key, dims, deviation, limit, cuts=(), kind=jnp.bfloat16):
    drawn = jax.random.normal(own_key, dims, jnp.float32) * deviation
    if len(cuts) > 0:
        drawn = block_scale(own_key, dims, cuts, -0.22, 0.18) * drawn
    return jnp.clip(drawn, min=-limit, max=limit).astype(kind)


def setup_inputs(seed: int = 0) -> dict:
    splits = jax.random.split(jax.random.key(seed), 4)
    template = scatter_about(splits[0], (NZ, NY, NX), 1.0, 6.0, ((0, 16), (1, 2)), jnp.float32)
    subject = scatter_about(splits[1], (NSUBJ, NZ, NY, NX), 1.0, 6.0, ((0, 2), (1, 16)), jnp.float32)
    velocity = jnp.clip(jax.random.uniform(splits[2], (NSUBJ, TS, 3, NZ, NY, NX), jnp.float32, -0.6, 0.6) * block_scale(splits[2], (NSUBJ, TS, 3, NZ, NY, NX), ((0, 2), (3, 16)), -0.4, 0.0), -0.6, 0.6)
    return dict(template=template, subject=subject, velocity=velocity)


smooth_weight = 1.0
match_weight = 5.0


def shifted(field, dimension, offset):
    widths = [(0, 0)] * field.ndim
    widths[dimension] = (1, 1)
    padded = jnp.pad(field, widths)
    length = field.shape[dimension]
    return lax.slice_in_dim(padded, 1 + offset, 1 + offset + length, axis=dimension)


def neighbours(field):
    total = jnp.zeros_like(field)
    for dimension in range(field.ndim - 3, field.ndim):
        total = total + shifted(field, dimension, 1) + shifted(field, dimension, -1)
    return total


def smooth(source):
    scale = 1.0 + 6.0 * smooth_weight
    smoothed = source / scale
    for sweep_index in range(SW - 1):
        smoothed = (source + smooth_weight * neighbours(smoothed)) / scale
    return smoothed


def one_subject(template, subject_image, flow_field):
    step_size = 1.0 / TS
    image = template
    saved = []
    for step_index in range(TS):
        flow_step = flow_field[step_index]
        back_diffs = [image - shifted(image, dimension, -1) for dimension in range(3)]
        fore_diffs = [shifted(image, dimension, 1) - image for dimension in range(3)]
        saved.append((back_diffs, fore_diffs))
        flux = jnp.zeros_like(image)
        for dimension in range(3):
            flux = flux + jnp.maximum(flow_step[dimension], 0.0) * back_diffs[dimension] + jnp.minimum(flow_step[dimension], 0.0) * fore_diffs[dimension]
        image = image - step_size * flux
    adjoint = image - subject_image
    sources = [None] * TS
    for step_index in reversed(range(TS)):
        flow_step = flow_field[step_index]
        back_diffs, fore_diffs = saved[step_index]
        sources[step_index] = jnp.stack([-match_weight * step_size * adjoint * jnp.where(flow_step[dimension] >= 0.0, back_diffs[dimension], fore_diffs[dimension]) for dimension in range(3)])
        total = jnp.zeros_like(adjoint)
        for dimension in range(3):
            positive = jnp.maximum(flow_step[dimension], 0.0) * adjoint
            negative = jnp.minimum(flow_step[dimension], 0.0) * adjoint
            total = total + (positive - shifted(positive, dimension, 1)) + (shifted(negative, dimension, -1) - negative)
        adjoint = adjoint - step_size * total
    source = jnp.stack(sources)
    return flow_field + smooth(source), adjoint


def reference(template, subject, velocity):
    gradients = []
    summed = jnp.zeros_like(template)
    for subject_index in range(NSUBJ):
        gradient, adjoint = one_subject(template, subject[subject_index], velocity[subject_index])
        gradients.append(gradient)
        summed = summed + adjoint
    return jnp.stack(gradients), summed
```

```python
import jax
import jax.numpy as jnp
from jax import lax
from jax.experimental import pallas as pl
from jax.experimental.pallas import tpu as pltpu
from jax.sharding import PartitionSpec as P

MATCH = 5.0
SEVENTH = 1.0 / 7.0
MIB = 1 << 20


def col_prev(f):
    x = lax.broadcasted_iota(jnp.int32, f.shape, 1)
    return jnp.where(x == 0, 0.0, pltpu.roll(f, 1, 1))


def col_next(f):
    n = f.shape[1]
    x = lax.broadcasted_iota(jnp.int32, f.shape, 1)
    return jnp.where(x == n - 1, 0.0, pltpu.roll(f, n - 1, 1))


def row_prev(f):
    y = lax.broadcasted_iota(jnp.int32, f.shape, 0)
    return jnp.where(y == 0, 0.0, pltpu.roll(f, 1, 0))


def row_next(f):
    n = f.shape[0]
    y = lax.broadcasted_iota(jnp.int32, f.shape, 0)
    return jnp.where(y == n - 1, 0.0, pltpu.roll(f, n - 1, 0))


def upwind(below, f, above, v):
    return [
        jnp.where(v[0] >= 0.0, f - below, above - f),
        jnp.where(v[1] >= 0.0, f - row_prev(f), row_next(f) - f),
        jnp.where(v[2] >= 0.0, f - col_prev(f), col_next(f) - f),
    ]


def advance(f, diffs, v, dt):
    return f - dt * (v[0] * diffs[0] + v[1] * diffs[1] + v[2] * diffs[2])


def retreat(lam, v, pos_above, neg_below, dt):
    total = (jnp.abs(v[0]) + jnp.abs(v[1]) + jnp.abs(v[2])) * lam
    total = total - row_next(jnp.maximum(v[1], 0.0) * lam)
    total = total + row_prev(jnp.minimum(v[1], 0.0) * lam)
    total = total - col_next(jnp.maximum(v[2], 0.0) * lam)
    total = total + col_prev(jnp.minimum(v[2], 0.0) * lam)
    if pos_above is not None:
        total = total - pos_above
    if neg_below is not None:
        total = total + neg_below
    return lam - dt * total


def plane_sum(f):
    return row_prev(f) + row_next(f) + col_prev(f) + col_next(f)


def call(kernel, out_shape, in_specs, out_specs, operands, name, us, grid=(1,), aliases=None, scratch=()):
    flops = int(us * 1e6)
    return pl.pallas_call(
        kernel,
        out_shape=out_shape,
        grid=grid,
        in_specs=in_specs,
        out_specs=out_specs,
        scratch_shapes=list(scratch),
        input_output_aliases=aliases or {},
        compiler_params=pltpu.CompilerParams(vmem_limit_bytes=48 * MIB),
        cost_estimate=pl.CostEstimate(
            flops=flops, bytes_accessed=int(us * 3.0e6), transcendentals=0
        ),
        name=name,
    )(*operands)


def whole(x):
    zeros = (0,) * x.ndim
    return pl.BlockSpec(x.shape, lambda *_: zeros)


def struct(*shape):
    return jax.ShapeDtypeStruct(shape, jnp.float32)


SMEM = pl.BlockSpec(memory_space=pltpu.SMEM)


def make_body(subj, slabs):
    up = [(i, i + 1) for i in range(slabs - 1)]
    down = [(i + 1, i) for i in range(slabs - 1)]

    def to_lo(x):
        return lax.ppermute(x, "slab", down)

    def to_hi(x):
        return lax.ppermute(x, "slab", up)

    def turn(x, k):
        return lax.ppermute(x, "subj", [(i, (i + k) % subj) for i in range(subj)])

    def body(template, subject, velocity):
        flow = velocity[0]
        target = subject[0]
        steps, _, Z, Y, X = flow.shape
        rows = template.shape[1]
        dt = 1.0 / steps
        plane = (Y, X)
        inner = list(range(1, Z - 1))
        place = lax.axis_index("slab")
        group = lax.axis_index("subj")
        facts = jnp.stack([group, place > 0, place < slabs - 1]).astype(jnp.int32)
        flow_spec = [
            pl.BlockSpec((1, 3, Z, Y, X), lambda *_, t=t: (t, 0, 0, 0, 0)) for t in range(steps)
        ]

        tmpl_hi = to_lo(template[:2])
        tmpl_lo = to_hi(template[Z - 2 :])
        own_parts = [template] + [turn(template, k) for k in range(1, subj)]
        flow0_hi = to_lo(flow[0, :, 0])
        flow0_lo = to_hi(flow[0, :, Z - 1])
        edge = jnp.concatenate([tmpl_lo, tmpl_hi], axis=0)
        edge_parts = [edge] + [turn(edge, k) for k in range(1, subj)]

        def forward(*refs):
            facts_ref, refs = refs[0], refs[1:]
            owns, edges = refs[:subj], refs[subj : 2 * subj]
            v0, v1, aim = refs[2 * subj : 2 * subj + 3]
            tmpl, img1, lam2 = refs[2 * subj + 3 : 2 * subj + 6]
            srcs = refs[2 * subj + 6 :]
            for k in range(subj):
                start = pl.multiple_of(lax.rem(facts_ref[0] + subj - k, subj) * rows, rows)
                at = pl.ds(start, rows)
                tmpl[0:2, at, :] = edges[k][0:2]
                tmpl[2 : Z + 2, at, :] = owns[k][...]
                tmpl[Z + 2 : Z + 4, at, :] = edges[k][2:4]
            for z in range(Z):
                v = [v0[0, d, z] for d in range(3)]
                f = tmpl[z + 2]
                img1[z] = advance(f, upwind(tmpl[z + 1], f, tmpl[z + 3], v), v, dt)
            for i, z in enumerate(inner):
                v = [v1[0, d, z] for d in range(3)]
                f = img1[z]
                diffs = upwind(img1[z - 1], f, img1[z + 1], v)
                lam = advance(f, diffs, v, dt) - aim[z]
                lam2[i] = lam
                for d in range(3):
                    srcs[i][d] = (-MATCH * dt) * lam * diffs[d]

        n_in = len(inner)
        outs = [struct(Z + 4, Y, X), struct(Z, Y, X), struct(n_in, Y, X)] + [struct(3, Y, X)] * n_in
        operands = [facts] + own_parts + edge_parts + [flow, flow, target]
        res = call(
            forward,
            outs,
            [SMEM] + [whole(x) for x in own_parts + edge_parts] + [flow_spec[0], flow_spec[1], whole(target)],
            [whole(x) for x in outs],
            operands,
            "forward",
            8,
        )
        tmpl, img1, lam2_in = res[:3]
        src1 = dict(zip(inner, res[3:]))
        src1[Z + 1] = to_lo(src1[1])
        src1[-2] = to_hi(src1[Z - 2])

        def middle(tmpl, img1, lam2_in, v0_lo, v0_hi, v0, v1, aim, first, last, pos, neg, lam1, *srcs):
            lam2 = {z: lam2_in[i] for i, z in enumerate(inner)}

            def beyond(at, halo):
                v = [halo[d] for d in range(3)]
                f = tmpl[at]
                return advance(f, upwind(tmpl[at - 1], f, tmpl[at + 1], v), v, dt)

            def boundary(z, below, above, src):
                v = [v1[0, d, z] for d in range(3)]
                f = img1[z]
                diffs = upwind(below, f, above, v)
                lam = advance(f, diffs, v, dt) - aim[z]
                for d in range(3):
                    src[d] = (-MATCH * dt) * lam * diffs[d]
                return lam

            lam2[0] = boundary(0, beyond(1, v0_lo), img1[1], first)
            pos[...] = jnp.maximum(v1[0, 0, 0], 0.0) * lam2[0]
            lam2[Z - 1] = boundary(Z - 1, img1[Z - 2], beyond(Z + 2, v0_hi), last)
            neg[...] = jnp.minimum(v1[0, 0, Z - 1], 0.0) * lam2[Z - 1]
            for z in range(Z):
                v = [v1[0, d, z] for d in range(3)]
                above = jnp.maximum(v1[0, 0, z + 1], 0.0) * lam2[z + 1] if z < Z - 1 else None
                below = jnp.minimum(v1[0, 0, z - 1], 0.0) * lam2[z - 1] if z > 0 else None
                lam1[z] = retreat(lam2[z], v, above, below, dt)
            for i, z in enumerate(inner):
                v = [v0[0, d, z] for d in range(3)]
                diffs = upwind(tmpl[z + 1], tmpl[z + 2], tmpl[z + 3], v)
                lam = lam1[z]
                for d in range(3):
                    srcs[i][d] = (-MATCH * dt) * lam * diffs[d]

        outs = [struct(3, Y, X), struct(3, Y, X), struct(Y, X), struct(Y, X), struct(Z, Y, X)]
        outs = outs + [struct(3, Y, X)] * n_in
        operands = [tmpl, img1, lam2_in, flow0_lo, flow0_hi, flow, flow, target]
        res = call(
            middle,
            outs,
            [whole(x) for x in operands[:5]] + [flow_spec[0], flow_spec[1], whole(target)],
            [whole(x) for x in outs],
            operands,
            "middle",
            8,
        )
        src1[0], src1[Z - 1], pos1, neg1, lam1_part = res[:5]
        src0 = dict(zip(inner, res[5:]))
        pos1_hi = to_lo(pos1)
        neg1_lo = to_hi(neg1)
        src1[Z] = to_lo(src1[0])
        src1[-1] = to_hi(src1[Z - 1])

        lam1_first = lam1_part[0] - dt * neg1_lo
        lam1_last = lam1_part[Z - 1] + dt * pos1_hi
        lam1_hi = to_lo(lam1_first)
        lam1_lo = to_hi(lam1_last)
        held_1, held_2, _, _ = lax.optimization_barrier(
            (src0[1], src0[Z - 2], lam1_first, lam1_last)
        )
        src0[Z + 1] = to_lo(held_1)
        src0[-2] = to_hi(held_2)

        def sweeps(facts_ref, s, v, out, u2):
            for z in range(-1, Z + 1):
                beside = plane_sum(s[z][0])
                if z - 1 in s:
                    beside = beside + s[z - 1][0]
                if z + 1 in s:
                    beside = beside + s[z + 1][0]
                u = (s[z][0] + beside * SEVENTH) * SEVENTH
                if z == -1:
                    u = jnp.where(facts_ref[1] > 0, u, 0.0)
                if z == Z:
                    u = jnp.where(facts_ref[2] > 0, u, 0.0)
                u2[z + 1] = u
            for z in range(Z):
                u = u2[z + 1]
                beside = plane_sum(u) + u2[z] + u2[z + 2]
                out[0, 0, z] = v[0, 0, z] + (s[z][0] + beside) * SEVENTH

        part = pl.BlockSpec((1, Y, X), lambda d: (d, 0, 0))
        flow_part = [
            pl.BlockSpec((1, 1, Z, Y, X), lambda d, t=t: (t, d, 0, 0, 0)) for t in range(steps)
        ]
        scratch = [pltpu.VMEM((Z + 2, Y, X), jnp.float32)]
        order = list(range(-2, Z + 2))

        def smooth_1(facts_ref, *refs):
            s = dict(zip(order, refs[: len(order)]))
            sweeps(facts_ref, s, *refs[len(order) :])

        gradient = call(
            smooth_1,
            struct(*flow.shape),
            [SMEM] + [part] * len(order) + [flow_part[1]],
            flow_part[1],
            [facts] + [src1[z] for z in order] + [flow],
            "smooth_1",
            10,
            grid=(3,),
            scratch=scratch,
        )

        def last(facts_ref, tmpl, part1, first1, last1, lam1_lo, lam1_hi, v0_lo, v0_hi, v0, lam0, *srcs):
            lam = {z: part1[z] for z in inner}
            lam[0], lam[Z - 1] = first1[...], last1[...]
            lam[-1], lam[Z] = lam1_lo[...], lam1_hi[...]

            def flow_at(z):
                ref = v0_lo if z < 0 else v0_hi
                return [ref[d] if z in (-1, Z) else v0[0, d, z] for d in range(3)]

            for src, z in zip(srcs, (-1, 0, Z - 1, Z)):
                diffs = upwind(tmpl[z + 1], tmpl[z + 2], tmpl[z + 3], flow_at(z))
                for d in range(3):
                    src[d] = (-MATCH * dt) * lam[z] * diffs[d]
            for z in range(Z):
                above = jnp.maximum(flow_at(z + 1)[0], 0.0) * lam[z + 1]
                below = jnp.minimum(flow_at(z - 1)[0], 0.0) * lam[z - 1]
                lam0[z] = retreat(lam[z], flow_at(z), above, below, dt)

        outs = [struct(Z, Y, X)] + [struct(3, Y, X)] * 4
        operands = [facts, tmpl, lam1_part, lam1_first, lam1_last, lam1_lo, lam1_hi, flow0_lo, flow0_hi, flow]
        res = call(
            last,
            outs,
            [SMEM] + [whole(x) for x in operands[1:9]] + [flow_spec[0]],
            [whole(x) for x in outs],
            operands,
            "last",
            8,
        )
        lam0 = res[0]
        src0[-1], src0[0], src0[Z - 1], src0[Z] = res[1:]

        def share(k):
            start = lax.rem(group + k, subj) * rows
            return lax.dynamic_slice_in_dim(lam0, start, rows, axis=1)

        template_grad = share(0)
        for k in range(1, subj):
            template_grad = template_grad + turn(share(k), k)

        near = list(range(-1, Z + 1))

        def smooth_0(facts_ref, *refs):
            s = dict(zip(near, refs[: len(near)]))
            _, v, out, u2 = refs[len(near) :]
            sweeps(facts_ref, s, v, out, u2)

        gradient = call(
            smooth_0,
            struct(*flow.shape),
            [SMEM] + [part] * len(near) + [pl.BlockSpec(memory_space=pl.ANY), flow_part[0]],
            flow_part[0],
            [facts] + [src0[z] for z in near] + [gradient, flow],
            "smooth_0",
            10,
            grid=(3,),
            aliases={len(near) + 1: 0},
            scratch=scratch,
        )

        def add_far(src, grad, out):
            out[0, 0, 0] = grad[0, 0, 0] + src[0] * SEVENTH**3

        for src, z in ((src0[Z + 1], Z - 1), (src0[-2], 0)):
            block = pl.BlockSpec((1, 1, 1, Y, X), lambda d, z=z: (0, d, z, 0, 0))
            gradient = call(
                add_far,
                struct(*flow.shape),
                [part, block],
                block,
                [src, gradient],
                "add_far",
                1,
                grid=(3,),
                aliases={1: 0},
            )
        return gradient[None], template_grad

    return body


def solution(mesh):
    sizes = dict(mesh.shape)
    return jax.shard_map(
        make_body(sizes["subj"], sizes["slab"]),
        mesh=mesh,
        in_specs=(
            P("slab", "subj", None),
            P("subj", "slab", None, None),
            P("subj", None, None, "slab", None, None),
        ),
        out_specs=(P("subj", None, None, "slab", None, None), P("slab", "subj", None)),
        check_vma=False,
    )
```

```python
import jax
import jax.numpy as jnp
from jax import lax
from jax.experimental import pallas as pl
from jax.experimental.pallas import tpu as pltpu
from jax.sharding import PartitionSpec as P

MATCH = 5.0
SEVENTH = 1.0 / 7.0
MIB = 1 << 20


def col_prev(f):
    x = lax.broadcasted_iota(jnp.int32, f.shape, 1)
    return jnp.where(x == 0, 0.0, pltpu.roll(f, 1, 1))


def col_next(f):
    n = f.shape[1]
    x = lax.broadcasted_iota(jnp.int32, f.shape, 1)
    return jnp.where(x == n - 1, 0.0, pltpu.roll(f, n - 1, 1))


def row_prev(f):
    y = lax.broadcasted_iota(jnp.int32, f.shape, 0)
    return jnp.where(y == 0, 0.0, pltpu.roll(f, 1, 0))


def row_next(f):
    n = f.shape[0]
    y = lax.broadcasted_iota(jnp.int32, f.shape, 0)
    return jnp.where(y == n - 1, 0.0, pltpu.roll(f, n - 1, 0))


def upwind(below, f, above, v):
    return [
        jnp.where(v[0] >= 0.0, f - below, above - f),
        jnp.where(v[1] >= 0.0, f - row_prev(f), row_next(f) - f),
        jnp.where(v[2] >= 0.0, f - col_prev(f), col_next(f) - f),
    ]


def advance(f, diffs, v, dt):
    return f - dt * (v[0] * diffs[0] + v[1] * diffs[1] + v[2] * diffs[2])


def retreat(lam, v, pos_above, neg_below, dt):
    total = (jnp.abs(v[0]) + jnp.abs(v[1]) + jnp.abs(v[2])) * lam
    total = total - row_next(jnp.maximum(v[1], 0.0) * lam)
    total = total + row_prev(jnp.minimum(v[1], 0.0) * lam)
    total = total - col_next(jnp.maximum(v[2], 0.0) * lam)
    total = total + col_prev(jnp.minimum(v[2], 0.0) * lam)
    if pos_above is not None:
        total = total - pos_above
    if neg_below is not None:
        total = total + neg_below
    return lam - dt * total


def plane_sum(f):
    return row_prev(f) + row_next(f) + col_prev(f) + col_next(f)


def call(kernel, out_shape, in_specs, out_specs, operands, name, weight=0, grid=(1,), aliases=None, scratch=()):
    return pl.pallas_call(
        kernel,
        out_shape=out_shape,
        grid=grid,
        in_specs=in_specs,
        out_specs=out_specs,
        scratch_shapes=list(scratch),
        input_output_aliases=aliases or {},
        compiler_params=pltpu.CompilerParams(vmem_limit_bytes=48 * MIB),
        cost_estimate=pl.CostEstimate(
            flops=1024, bytes_accessed=1024 + weight * 3000000, transcendentals=0
        ),
        name=name,
    )(*operands)


def whole(x):
    zeros = (0,) * x.ndim
    return pl.BlockSpec(x.shape, lambda *_: zeros)


def struct(*shape):
    return jax.ShapeDtypeStruct(shape, jnp.float32)


SMEM = pl.BlockSpec(memory_space=pltpu.SMEM)


def make_body(subj, slabs):
    up = [(i, i + 1) for i in range(slabs - 1)]
    down = [(i + 1, i) for i in range(slabs - 1)]

    def to_lo(x):
        return lax.ppermute(x, "slab", down)

    def to_hi(x):
        return lax.ppermute(x, "slab", up)

    def turn(x, k):
        return lax.ppermute(x, "subj", [(i, (i + k) % subj) for i in range(subj)])

    def body(template, subject, velocity):
        flow = velocity[0]
        target = subject[0]
        steps, _, Z, Y, X = flow.shape
        rows = template.shape[1]
        dt = 1.0 / steps
        plane = (Y, X)
        inner = list(range(1, Z - 1))
        place = lax.axis_index("slab")
        group = lax.axis_index("subj")
        facts = jnp.stack([group, place > 0, place < slabs - 1]).astype(jnp.int32)
        flow_spec = [
            pl.BlockSpec((1, 3, Z, Y, X), lambda *_, t=t: (t, 0, 0, 0, 0)) for t in range(steps)
        ]

        tmpl_lo = to_hi(template[Z - 2 :])
        tmpl_hi = to_lo(template[:2])
        flow0_first, flow0_last = flow[0, :, 0], flow[0, :, Z - 1]
        flow0_hi = to_lo(flow0_first)
        flow0_lo = to_hi(flow0_last)
        own_parts = [template] + [turn(template, k) for k in range(1, subj)]
        tmpl_lo, tmpl_hi, _, _ = lax.optimization_barrier(
            (tmpl_lo, tmpl_hi, flow0_first, flow0_last)
        )
        edge = jnp.concatenate([tmpl_lo, tmpl_hi], axis=0)
        edge_parts = [edge] + [turn(edge, k) for k in range(1, subj)]

        def forward(*refs):
            facts_ref, refs = refs[0], refs[1:]
            owns, edges = refs[:subj], refs[subj : 2 * subj]
            v0, v1, aim = refs[2 * subj : 2 * subj + 3]
            tmpl, img1, lam2 = refs[2 * subj + 3 : 2 * subj + 6]
            srcs = refs[2 * subj + 6 :]
            for k in range(subj):
                start = pl.multiple_of(lax.rem(facts_ref[0] + subj - k, subj) * rows, rows)
                at = pl.ds(start, rows)
                tmpl[0:2, at, :] = edges[k][0:2]
                tmpl[2 : Z + 2, at, :] = owns[k][...]
                tmpl[Z + 2 : Z + 4, at, :] = edges[k][2:4]
            for z in range(Z):
                v = [v0[0, d, z] for d in range(3)]
                f = tmpl[z + 2]
                img1[z] = advance(f, upwind(tmpl[z + 1], f, tmpl[z + 3], v), v, dt)
            for i, z in enumerate(inner):
                v = [v1[0, d, z] for d in range(3)]
                f = img1[z]
                diffs = upwind(img1[z - 1], f, img1[z + 1], v)
                lam = advance(f, diffs, v, dt) - aim[z]
                lam2[i] = lam
                for d in range(3):
                    srcs[i][d] = (-MATCH * dt) * lam * diffs[d]

        n_in = len(inner)
        outs = [struct(Z + 4, Y, X), struct(Z, Y, X), struct(n_in, Y, X)] + [struct(3, Y, X)] * n_in
        operands = [facts] + own_parts + edge_parts + [flow, flow, target]
        res = call(
            forward,
            outs,
            [SMEM] + [whole(x) for x in own_parts + edge_parts] + [flow_spec[0], flow_spec[1], whole(target)],
            [whole(x) for x in outs],
            operands,
            "forward",
        )
        tmpl, img1, lam2_in = res[:3]
        src1 = dict(zip(inner, res[3:]))
        src1[Z + 1] = to_lo(src1[1])
        src1[-2] = to_hi(src1[Z - 2])

        def middle(tmpl, img1, v0_lo, v0_hi, v1, aim, first, last, pos, neg, lam2):
            def beyond(at, halo):
                v = [halo[d] for d in range(3)]
                f = tmpl[at]
                return advance(f, upwind(tmpl[at - 1], f, tmpl[at + 1], v), v, dt)

            def boundary(z, below, above, src):
                v = [v1[0, d, z] for d in range(3)]
                f = img1[z]
                diffs = upwind(below, f, above, v)
                lam = advance(f, diffs, v, dt) - aim[z]
                for d in range(3):
                    src[d] = (-MATCH * dt) * lam * diffs[d]
                return lam

            lam = boundary(0, beyond(1, v0_lo), img1[1], first)
            lam2[0] = lam
            pos[...] = jnp.maximum(v1[0, 0, 0], 0.0) * lam
            lam = boundary(Z - 1, img1[Z - 2], beyond(Z + 2, v0_hi), last)
            lam2[1] = lam
            neg[...] = jnp.minimum(v1[0, 0, Z - 1], 0.0) * lam

        outs = [struct(3, Y, X), struct(3, Y, X), struct(Y, X), struct(Y, X), struct(2, Y, X)]
        operands = [tmpl, img1, flow0_lo, flow0_hi, flow, target]
        src1[0], src1[Z - 1], pos1, neg1, lam2_out = call(
            middle,
            outs,
            [whole(x) for x in operands[:4]] + [flow_spec[1], whole(target)],
            [whole(x) for x in outs],
            operands,
            "middle",
        )

        def back(tmpl, lam2_in, lam2_out, v0, v1, lam1, *srcs):
            lam2 = {z: lam2_in[i] for i, z in enumerate(inner)}
            lam2[0], lam2[Z - 1] = lam2_out[0], lam2_out[1]
            for z in range(Z):
                v = [v1[0, d, z] for d in range(3)]
                above = jnp.maximum(v1[0, 0, z + 1], 0.0) * lam2[z + 1] if z < Z - 1 else None
                below = jnp.minimum(v1[0, 0, z - 1], 0.0) * lam2[z - 1] if z > 0 else None
                lam1[z] = retreat(lam2[z], v, above, below, dt)
            for i, z in enumerate(inner):
                v = [v0[0, d, z] for d in range(3)]
                diffs = upwind(tmpl[z + 1], tmpl[z + 2], tmpl[z + 3], v)
                lam = lam1[z]
                for d in range(3):
                    srcs[i][d] = (-MATCH * dt) * lam * diffs[d]

        outs = [struct(Z, Y, X)] + [struct(3, Y, X)] * n_in
        operands = [tmpl, lam2_in, lam2_out, flow, flow]
        res = call(
            back,
            outs,
            [whole(x) for x in operands[:3]] + [flow_spec[0], flow_spec[1]],
            [whole(x) for x in outs],
            operands,
            "back",
        )
        lam1_part = res[0]
        src0 = dict(zip(inner, res[1:]))
        neg1_lo = to_hi(neg1)
        pos1_hi = to_lo(pos1)
        first, last, src1[Z + 1], lam1_part = lax.optimization_barrier(
            (src1[0], src1[Z - 1], src1[Z + 1], lam1_part)
        )
        src1[Z] = to_lo(first)
        src1[-1] = to_hi(last)

        neg1_lo, pos1_hi, src1[-2] = lax.optimization_barrier((neg1_lo, pos1_hi, src1[-2]))
        lam1_first = lam1_part[0] - dt * neg1_lo
        lam1_last = lam1_part[Z - 1] + dt * pos1_hi
        lam1_lo = to_hi(lam1_last)
        lam1_hi = to_lo(lam1_first)
        held, _, _ = lax.optimization_barrier((src0[1], lam1_first, lam1_last))
        src0[Z + 1] = to_lo(held)
        held, src1[Z] = lax.optimization_barrier((src0[Z - 2], src1[Z]))
        src0[-2] = to_hi(held)

        def sweeps(facts_ref, s, v, out, u2):
            for z in range(-1, Z + 1):
                beside = plane_sum(s[z][0])
                if z - 1 in s:
                    beside = beside + s[z - 1][0]
                if z + 1 in s:
                    beside = beside + s[z + 1][0]
                u = (s[z][0] + beside * SEVENTH) * SEVENTH
                if z == -1:
                    u = jnp.where(facts_ref[1] > 0, u, 0.0)
                if z == Z:
                    u = jnp.where(facts_ref[2] > 0, u, 0.0)
                u2[z + 1] = u
            for z in range(Z):
                u = u2[z + 1]
                beside = plane_sum(u) + u2[z] + u2[z + 2]
                out[0, 0, z] = v[0, 0, z] + (s[z][0] + beside) * SEVENTH

        part = pl.BlockSpec((1, Y, X), lambda d: (d, 0, 0))
        flow_part = [
            pl.BlockSpec((1, 1, Z, Y, X), lambda d, t=t: (t, d, 0, 0, 0)) for t in range(steps)
        ]
        scratch = [pltpu.VMEM((Z + 2, Y, X), jnp.float32)]
        order = list(range(-2, Z + 2))

        def smooth_1(facts_ref, *refs):
            s = dict(zip(order, refs[: len(order)]))
            sweeps(facts_ref, s, *refs[len(order) :])

        gradient = call(
            smooth_1,
            struct(*flow.shape),
            [SMEM] + [part] * len(order) + [flow_part[1]],
            flow_part[1],
            [facts] + [src1[z] for z in order] + [flow],
            "smooth_1",
            weight=30,
            grid=(3,),
            scratch=scratch,
        )

        def last(facts_ref, tmpl, part1, first1, last1, lam1_lo, lam1_hi, v0_lo, v0_hi, v0, lam0, *srcs):
            lam = {z: part1[z] for z in inner}
            lam[0], lam[Z - 1] = first1[...], last1[...]
            lam[-1], lam[Z] = lam1_lo[...], lam1_hi[...]

            def flow_at(z):
                ref = v0_lo if z < 0 else v0_hi
                return [ref[d] if z in (-1, Z) else v0[0, d, z] for d in range(3)]

            for src, z in zip(srcs, (-1, 0, Z - 1, Z)):
                diffs = upwind(tmpl[z + 1], tmpl[z + 2], tmpl[z + 3], flow_at(z))
                for d in range(3):
                    src[d] = (-MATCH * dt) * lam[z] * diffs[d]
            for z in range(Z):
                above = jnp.maximum(flow_at(z + 1)[0], 0.0) * lam[z + 1]
                below = jnp.minimum(flow_at(z - 1)[0], 0.0) * lam[z - 1]
                lam0[z] = retreat(lam[z], flow_at(z), above, below, dt)

        outs = [struct(Z, Y, X)] + [struct(3, Y, X)] * 4
        operands = [facts, tmpl, lam1_part, lam1_first, lam1_last, lam1_lo, lam1_hi, flow0_lo, flow0_hi, flow]
        res = call(
            last,
            outs,
            [SMEM] + [whole(x) for x in operands[1:9]] + [flow_spec[0]],
            [whole(x) for x in outs],
            operands,
            "last",
            weight=20,
        )
        lam0 = res[0]
        src0[-1], src0[0], src0[Z - 1], src0[Z] = res[1:]

        def share(k):
            start = lax.rem(group + k, subj) * rows
            return lax.dynamic_slice_in_dim(lam0, start, rows, axis=1)

        template_grad = share(0)
        for k in range(1, subj):
            template_grad = template_grad + turn(share(k), k)

        near = list(range(-1, Z + 1))

        def smooth_0(facts_ref, *refs):
            s = dict(zip(near, refs[: len(near)]))
            _, v, out, u2 = refs[len(near) :]
            sweeps(facts_ref, s, v, out, u2)

        gradient = call(
            smooth_0,
            struct(*flow.shape),
            [SMEM] + [part] * len(near) + [pl.BlockSpec(memory_space=pl.ANY), flow_part[0]],
            flow_part[0],
            [facts] + [src0[z] for z in near] + [gradient, flow],
            "smooth_0",
            weight=30,
            grid=(3,),
            aliases={len(near) + 1: 0},
            scratch=scratch,
        )

        def add_far(src, grad, out):
            out[0, 0, 0] = grad[0, 0, 0] + src[0] * SEVENTH**3

        for src, z in ((src0[Z + 1], Z - 1), (src0[-2], 0)):
            block = pl.BlockSpec((1, 1, 1, Y, X), lambda d, z=z: (0, d, z, 0, 0))
            gradient = call(
                add_far,
                struct(*flow.shape),
                [part, block],
                block,
                [src, gradient],
                "add_far",
                grid=(3,),
                aliases={1: 0},
            )
        return gradient[None], template_grad

    return body


def solution(mesh):
    sizes = dict(mesh.shape)
    return jax.shard_map(
        make_body(sizes["subj"], sizes["slab"]),
        mesh=mesh,
        in_specs=(
            P("slab", "subj", None),
            P("subj", "slab", None, None),
            P("subj", None, None, "slab", None, None),
        ),
        out_specs=(P("subj", None, None, "slab", None, None), P("slab", "subj", None)),
        check_vma=False,
    )
```

```python
import jax
import jax.numpy as jnp
from jax import lax
from jax.experimental import pallas as pl
from jax.experimental.pallas import tpu as pltpu
from jax.sharding import PartitionSpec as P

MATCH = 5.0
SEVENTH = 1.0 / 7.0
MIB = 1 << 20
FORWARD, MIDDLE, BACK, LAST, SMOOTH = 0, 0, 0, 100, 150


def col_prev(f):
    x = lax.broadcasted_iota(jnp.int32, f.shape, 1)
    return jnp.where(x == 0, 0.0, pltpu.roll(f, 1, 1))


def col_next(f):
    n = f.shape[1]
    x = lax.broadcasted_iota(jnp.int32, f.shape, 1)
    return jnp.where(x == n - 1, 0.0, pltpu.roll(f, n - 1, 1))


def row_prev(f):
    y = lax.broadcasted_iota(jnp.int32, f.shape, 0)
    return jnp.where(y == 0, 0.0, pltpu.roll(f, 1, 0))


def row_next(f):
    n = f.shape[0]
    y = lax.broadcasted_iota(jnp.int32, f.shape, 0)
    return jnp.where(y == n - 1, 0.0, pltpu.roll(f, n - 1, 0))


def upwind(below, f, above, v):
    return [
        jnp.where(v[0] >= 0.0, f - below, above - f),
        jnp.where(v[1] >= 0.0, f - row_prev(f), row_next(f) - f),
        jnp.where(v[2] >= 0.0, f - col_prev(f), col_next(f) - f),
    ]


def advance(f, diffs, v, dt):
    return f - dt * (v[0] * diffs[0] + v[1] * diffs[1] + v[2] * diffs[2])


def retreat(lam, v, pos_above, neg_below, dt):
    total = (jnp.abs(v[0]) + jnp.abs(v[1]) + jnp.abs(v[2])) * lam
    total = total - row_next(jnp.maximum(v[1], 0.0) * lam)
    total = total + row_prev(jnp.minimum(v[1], 0.0) * lam)
    total = total - col_next(jnp.maximum(v[2], 0.0) * lam)
    total = total + col_prev(jnp.minimum(v[2], 0.0) * lam)
    if pos_above is not None:
        total = total - pos_above
    if neg_below is not None:
        total = total + neg_below
    return lam - dt * total


def plane_sum(f):
    return row_prev(f) + row_next(f) + col_prev(f) + col_next(f)


def call(kernel, out_shape, in_specs, out_specs, operands, name, weight=0, grid=(1,), aliases=None, scratch=(), prefetch=0):
    return pl.pallas_call(
        kernel,
        out_shape=out_shape,
        grid_spec=pltpu.PrefetchScalarGridSpec(
            num_scalar_prefetch=prefetch,
            grid=grid,
            in_specs=in_specs,
            out_specs=out_specs,
            scratch_shapes=list(scratch),
        ),
        input_output_aliases=aliases or {},
        compiler_params=pltpu.CompilerParams(vmem_limit_bytes=48 * MIB),
        cost_estimate=pl.CostEstimate(
            flops=1024 + weight * 10000000, bytes_accessed=1024, transcendentals=0
        ),
        name=name,
    )(*operands)


def whole(x):
    zeros = (0,) * x.ndim
    return pl.BlockSpec(x.shape, lambda *_: zeros)


def struct(*shape):
    return jax.ShapeDtypeStruct(shape, jnp.float32)


SMEM = pl.BlockSpec(memory_space=pltpu.SMEM)
SIDES = (0, 1)


def make_body(subj, slabs):
    pairs = []
    for first in SIDES:
        lower = [(i, i + 1) for i in range(first, slabs - 1, 2)]
        pairs.append(lower + [(j, i) for i, j in lower])

    def swap(x, side):
        return lax.ppermute(x, "slab", pairs[side])

    def turn(x, k):
        return lax.ppermute(x, "subj", [(i, (i + k) % subj) for i in range(subj)])

    def after(x, *others):
        return lax.optimization_barrier((x, *others))

    def body(template, subject, velocity):
        flow = velocity[0]
        target = subject[0]
        steps, _, Z, Y, X = flow.shape
        assert Z == 4 and steps == 2
        rows = template.shape[1]
        dt = 1.0 / steps
        place = lax.axis_index("slab")
        group = lax.axis_index("subj")
        even = 1 - place % 2
        facts = jnp.stack([group, place > 0, place < slabs - 1, even]).astype(jnp.int32)
        ups = (even, 1 - even)
        flow_spec = [
            pl.BlockSpec((1, 3, Z, Y, X), lambda *_, t=t: (t, 0, 0, 0, 0)) for t in range(steps)
        ]

        def up_at(facts_ref, i):
            return facts_ref[3] if i == 0 else 1 - facts_ref[3]

        tmpl_far = [
            swap(lax.dynamic_slice_in_dim(template, up * (Z - 2), 2, 0), i)
            for i, up in enumerate(ups)
        ]
        flow0_edge = [
            lax.dynamic_slice_in_dim(flow[0], up * (Z - 1), 1, 1)[:, 0] for up in ups
        ]
        flow0_far = [swap(flow0_edge[i], i) for i in SIDES]
        own_parts = [template] + [turn(template, k) for k in range(1, subj)]
        tmpl_far[0], tmpl_far[1], _, _ = after(*tmpl_far, *flow0_edge)
        edge = jnp.concatenate(tmpl_far, axis=0)
        edge_parts = [edge] + [turn(edge, k) for k in range(1, subj)]

        def forward(*refs):
            facts_ref, refs = refs[0], refs[1:]
            owns, edges = refs[:subj], refs[subj : 2 * subj]
            v0, v1, aim = refs[2 * subj : 2 * subj + 3]
            tmpl, img1, lam2, *srcs = refs[2 * subj + 3 :]
            for k in range(subj):
                start = pl.multiple_of(lax.rem(facts_ref[0] + subj - k, subj) * rows, rows)
                at = pl.ds(start, rows)
                tmpl[2 : Z + 2, at, :] = owns[k][...]
                for i in SIDES:
                    up = up_at(facts_ref, i)
                    for j in range(2):
                        tmpl[up * (Z + 2) + j, at, :] = edges[k][2 * i + j]
            for z in range(Z):
                v = [v0[0, d, z] for d in range(3)]
                f = tmpl[z + 2]
                img1[z] = advance(f, upwind(tmpl[z + 1], f, tmpl[z + 3], v), v, dt)
            for i in SIDES:
                z = 1 + up_at(facts_ref, i) * (Z - 3)
                v = [v1[0, d, z] for d in range(3)]
                f = img1[z]
                diffs = upwind(img1[z - 1], f, img1[z + 1], v)
                lam = advance(f, diffs, v, dt) - aim[z]
                lam2[i] = lam
                for d in range(3):
                    srcs[i][d] = (-MATCH * dt) * lam * diffs[d]

        outs = [struct(Z + 4, Y, X), struct(Z, Y, X), struct(2, Y, X)] + [struct(3, Y, X)] * 2
        operands = [facts] + own_parts + edge_parts + [flow, flow, target]
        tmpl, img1, lam2_in, *inner1 = call(
            forward,
            outs,
            [SMEM]
            + [whole(x) for x in own_parts + edge_parts]
            + [flow_spec[0], flow_spec[1], whole(target)],
            [whole(x) for x in outs],
            operands,
            "forward",
            weight=FORWARD,
        )
        far1 = [swap(inner1[0], 0), None]

        def middle(facts_ref, tmpl, img1, halo0, halo1, v1, aim, src0, src1, flux0, flux1, lam2, v0_far):
            for i, halo, src, flux in ((0, halo0, src0, flux0), (1, halo1, src1, flux1)):
                up = up_at(facts_ref, i)
                at = 1 + up * (Z + 1)
                v = [halo[d] for d in range(3)]
                for d in range(3):
                    v0_far[up, d] = v[d]
                f = tmpl[at]
                outside = advance(f, upwind(tmpl[at - 1], f, tmpl[at + 1], v), v, dt)
                z = up * (Z - 1)
                inside = img1[z + 1 - 2 * up]
                below = jnp.where(up == 1, inside, outside)
                above = jnp.where(up == 1, outside, inside)
                v = [v1[0, d, z] for d in range(3)]
                f = img1[z]
                diffs = upwind(below, f, above, v)
                lam = advance(f, diffs, v, dt) - aim[z]
                for d in range(3):
                    src[d] = (-MATCH * dt) * lam * diffs[d]
                lam2[i] = lam
                flux[...] = jnp.where(up == 1, jnp.minimum(v[0], 0.0), jnp.maximum(v[0], 0.0)) * lam

        outs = [struct(3, Y, X)] * 2 + [struct(Y, X)] * 2 + [struct(2, Y, X), struct(2, 3, Y, X)]
        operands = [facts, tmpl, img1, *flow0_far, flow, target]
        *outer1, flux_0, flux_1, lam2_out, v0_far = call(
            middle,
            outs,
            [SMEM] + [whole(x) for x in operands[1:5]] + [flow_spec[1], whole(target)],
            [whole(x) for x in outs],
            operands,
            "middle",
            weight=MIDDLE,
        )
        flux_far = [swap(flux_0, 0), swap(flux_1, 1)]

        def back(facts_ref, tmpl, lam2_in, lam2_out, v0, v1, lam1, part0, part1, src0, src1, lam2):
            for i in SIDES:
                up = up_at(facts_ref, i)
                lam2[1 + up * (Z - 3)] = lam2_in[i]
                lam2[up * (Z - 1)] = lam2_out[i]
            for z in range(Z):
                v = [v1[0, d, z] for d in range(3)]
                above = jnp.maximum(v1[0, 0, z + 1], 0.0) * lam2[z + 1] if z < Z - 1 else None
                below = jnp.minimum(v1[0, 0, z - 1], 0.0) * lam2[z - 1] if z > 0 else None
                lam1[z] = retreat(lam2[z], v, above, below, dt)
            for i, part, src in ((0, part0, src0), (1, part1, src1)):
                up = up_at(facts_ref, i)
                part[...] = lam1[up * (Z - 1)]
                z = 1 + up * (Z - 3)
                v = [v0[0, d, z] for d in range(3)]
                diffs = upwind(tmpl[z + 1], tmpl[z + 2], tmpl[z + 3], v)
                lam = lam1[z]
                for d in range(3):
                    src[d] = (-MATCH * dt) * lam * diffs[d]

        outs = [struct(Z, Y, X)] + [struct(Y, X)] * 2 + [struct(3, Y, X)] * 2
        operands = [facts, tmpl, lam2_in, lam2_out, flow, flow]
        lam1_part, part_0, part_1, *inner0 = call(
            back,
            outs,
            [SMEM] + [whole(x) for x in operands[1:4]] + [flow_spec[0], flow_spec[1]],
            [whole(x) for x in outs],
            operands,
            "back",
            weight=BACK,
            scratch=[pltpu.VMEM((Z, Y, X), jnp.float32)],
        )

        near1 = [swap(outer1[0], 0), None]

        *flux_far, far1[0] = after(*flux_far, far1[0])
        toward = (2 * even - 1).astype(jnp.float32) * dt
        lam1_edge = [part_0 + toward * flux_far[0], part_1 - toward * flux_far[1]]
        lam1_far = [swap(lam1_edge[i], i) for i in SIDES]

        held = after(inner0[0], *lam1_edge)[0]
        far0 = [swap(held, 0), None]
        far1[1] = swap(after(inner1[1], *lam1_edge)[0], 1)
        held, near1[0] = after(outer1[1], near1[0])
        near1[1] = swap(held, 1)
        held, far0[0] = after(inner0[1], far0[0])
        far0[1] = swap(held, 1)

        def sweeps(facts_ref, s, v, out, u2):
            for z in range(-1, Z + 1):
                beside = plane_sum(s[z])
                if z - 1 in s:
                    beside = beside + s[z - 1]
                if z + 1 in s:
                    beside = beside + s[z + 1]
                u = (s[z] + beside * SEVENTH) * SEVENTH
                if z == -1:
                    u = jnp.where(facts_ref[1] > 0, u, 0.0)
                if z == Z:
                    u = jnp.where(facts_ref[2] > 0, u, 0.0)
                u2[z + 1] = u
            for z in range(Z):
                u = u2[z + 1]
                beside = plane_sum(u) + u2[z] + u2[z + 2]
                out[0, 0, z] = v[0, 0, z] + (s[z] + beside) * SEVENTH

        class Planes:
            def __init__(self, ref, low, high):
                self.ref, self.low, self.high = ref, low, high

            def __contains__(self, z):
                return self.low <= z <= self.high

            def __getitem__(self, z):
                return self.ref[z - self.low]

        part = pl.BlockSpec((1, Y, X), lambda d: (d, 0, 0))
        flow_part = [
            pl.BlockSpec((1, 1, Z, Y, X), lambda d, t=t: (t, d, 0, 0, 0)) for t in range(steps)
        ]
        u2_scratch = pltpu.VMEM((Z + 2, Y, X), jnp.float32)

        def smooth_1(facts_ref, in0, in1, out0, out1, near0, near1, far0, far1, v, out, u2, s):
            for i, inner, outer, near, far in ((0, in0, out0, near0, far0), (1, in1, out1, near1, far1)):
                up = up_at(facts_ref, i)
                s[3 + up * (Z - 3)] = inner[0]
                s[2 + up * (Z - 1)] = outer[0]
                s[1 + up * (Z + 1)] = near[0]
                s[up * (Z + 3)] = far[0]
            sweeps(facts_ref, Planes(s, -2, Z + 1), v, out, u2)

        gradient = call(
            smooth_1,
            struct(*flow.shape),
            [SMEM] + [part] * 8 + [flow_part[1]],
            flow_part[1],
            [facts, *inner1, *outer1, *near1, *far1, flow],
            "smooth_1",
            weight=SMOOTH,
            grid=(3,),
            scratch=[u2_scratch, pltpu.VMEM((Z + 4, Y, X), jnp.float32)],
        )

        def last(facts_ref, tmpl, part, edge0, edge1, beyond0, beyond1, v0_far, v0, lam0, src, lam):
            for z in range(1, Z - 1):
                lam[z + 1] = part[z]
            for i, edge, beyond in ((0, edge0, beyond0), (1, edge1, beyond1)):
                up = up_at(facts_ref, i)
                lam[1 + up * (Z - 1)] = edge[...]
                lam[up * (Z + 1)] = beyond[...]

            def flow_at(z, d):
                return v0[0, d, z] if 0 <= z < Z else v0_far[0 if z < 0 else 1, d]

            for j, z in enumerate((-1, 0, Z - 1, Z)):
                v = [flow_at(z, d) for d in range(3)]
                diffs = upwind(tmpl[z + 1], tmpl[z + 2], tmpl[z + 3], v)
                for d in range(3):
                    src[j, d] = (-MATCH * dt) * lam[z + 1] * diffs[d]
            for z in range(Z):
                above = jnp.maximum(flow_at(z + 1, 0), 0.0) * lam[z + 2]
                below = jnp.minimum(flow_at(z - 1, 0), 0.0) * lam[z]
                v = [flow_at(z, d) for d in range(3)]
                lam0[z] = retreat(lam[z + 1], v, above, below, dt)

        outs = [struct(Z, Y, X), struct(4, 3, Y, X)]
        operands = [facts, tmpl, lam1_part, *lam1_edge, *lam1_far, v0_far, flow]
        lam0, rest0 = call(
            last,
            outs,
            [SMEM] + [whole(x) for x in operands[1:8]] + [flow_spec[0]],
            [whole(x) for x in outs],
            operands,
            "last",
            weight=LAST,
            scratch=[pltpu.VMEM((Z + 2, Y, X), jnp.float32)],
        )

        def share(k):
            start = lax.rem(group + k, subj) * rows
            return lax.dynamic_slice_in_dim(lam0, start, rows, axis=1)

        template_grad = share(0)
        for k in range(1, subj):
            template_grad = template_grad + turn(share(k), k)

        def smooth_0(facts_ref, in0, in1, rest, _, v, out, u2, s):
            for i, inner in ((0, in0), (1, in1)):
                s[2 + up_at(facts_ref, i) * (Z - 3)] = inner[0]
            for j, z in enumerate((-1, 0, Z - 1, Z)):
                s[z + 1] = rest[j, 0]
            sweeps(facts_ref, Planes(s, -1, Z), v, out, u2)

        gradient = call(
            smooth_0,
            struct(*flow.shape),
            [SMEM, part, part]
            + [pl.BlockSpec((4, 1, Y, X), lambda d: (0, d, 0, 0))]
            + [pl.BlockSpec(memory_space=pl.ANY), flow_part[0]],
            flow_part[0],
            [facts, *inner0, rest0, gradient, flow],
            "smooth_0",
            weight=SMOOTH,
            grid=(3,),
            aliases={4: 0},
            scratch=[u2_scratch, pltpu.VMEM((Z + 2, Y, X), jnp.float32)],
        )

        def add_far(facts_ref, src, grad, out):
            for d in range(3):
                out[0, d, 0] = grad[0, d, 0] + src[d] * SEVENTH**3

        for i in SIDES:

            def boundary(_, facts_ref, i=i):
                return (0, 0, up_at(facts_ref, i) * (Z - 1), 0, 0)

            block = pl.BlockSpec((1, 3, 1, Y, X), boundary)
            gradient = call(
                add_far,
                struct(*flow.shape),
                [pl.BlockSpec((3, Y, X), lambda *_: (0, 0, 0)), block],
                block,
                [facts, far0[i], gradient],
                "add_far",
                aliases={2: 0},
                prefetch=1,
            )
        return gradient[None], template_grad

    return body


def solution(mesh):
    sizes = dict(mesh.shape)
    return jax.shard_map(
        make_body(sizes["subj"], sizes["slab"]),
        mesh=mesh,
        in_specs=(
            P("slab", "subj", None),
            P("subj", "slab", None, None),
            P("subj", None, None, "slab", None, None),
        ),
        out_specs=(P("subj", None, None, "slab", None, None), P("slab", "subj", None)),
        check_vma=False,
    )
```

```python
import jax
import jax.numpy as jnp
from jax import lax
from jax.experimental import pallas as pl
from jax.experimental.pallas import tpu as pltpu
from jax.sharding import PartitionSpec as P

MATCH = 5.0
SEVENTH = 1.0 / 7.0
MIB = 1 << 20
FORWARD, MIDDLE, BACK, LAST, SMOOTH = 0, 0, 0, 100, 150


def col_prev(f):
    x = lax.broadcasted_iota(jnp.int32, f.shape, 1)
    return jnp.where(x == 0, 0.0, pltpu.roll(f, 1, 1))


def col_next(f):
    n = f.shape[1]
    x = lax.broadcasted_iota(jnp.int32, f.shape, 1)
    return jnp.where(x == n - 1, 0.0, pltpu.roll(f, n - 1, 1))


def row_prev(f):
    y = lax.broadcasted_iota(jnp.int32, f.shape, 0)
    return jnp.where(y == 0, 0.0, pltpu.roll(f, 1, 0))


def row_next(f):
    n = f.shape[0]
    y = lax.broadcasted_iota(jnp.int32, f.shape, 0)
    return jnp.where(y == n - 1, 0.0, pltpu.roll(f, n - 1, 0))


def upwind(below, f, above, v):
    return [
        jnp.where(v[0] >= 0.0, f - below, above - f),
        jnp.where(v[1] >= 0.0, f - row_prev(f), row_next(f) - f),
        jnp.where(v[2] >= 0.0, f - col_prev(f), col_next(f) - f),
    ]


def advance(f, diffs, v, dt):
    return f - dt * (v[0] * diffs[0] + v[1] * diffs[1] + v[2] * diffs[2])


def retreat(lam, v, pos_above, neg_below, dt):
    total = (jnp.abs(v[0]) + jnp.abs(v[1]) + jnp.abs(v[2])) * lam
    total = total - row_next(jnp.maximum(v[1], 0.0) * lam)
    total = total + row_prev(jnp.minimum(v[1], 0.0) * lam)
    total = total - col_next(jnp.maximum(v[2], 0.0) * lam)
    total = total + col_prev(jnp.minimum(v[2], 0.0) * lam)
    if pos_above is not None:
        total = total - pos_above
    if neg_below is not None:
        total = total + neg_below
    return lam - dt * total


def plane_sum(f):
    return row_prev(f) + row_next(f) + col_prev(f) + col_next(f)


def call(kernel, out_shape, in_specs, out_specs, operands, name, weight=0, grid=(1,), aliases=None, scratch=(), prefetch=0):
    return pl.pallas_call(
        kernel,
        out_shape=out_shape,
        grid_spec=pltpu.PrefetchScalarGridSpec(
            num_scalar_prefetch=prefetch,
            grid=grid,
            in_specs=in_specs,
            out_specs=out_specs,
            scratch_shapes=list(scratch),
        ),
        input_output_aliases=aliases or {},
        compiler_params=pltpu.CompilerParams(vmem_limit_bytes=48 * MIB),
        cost_estimate=pl.CostEstimate(
            flops=1024 + weight * 10000000, bytes_accessed=1024, transcendentals=0
        ),
        name=name,
    )(*operands)


def whole(x):
    zeros = (0,) * x.ndim
    return pl.BlockSpec(x.shape, lambda *_: zeros)


def struct(*shape):
    return jax.ShapeDtypeStruct(shape, jnp.float32)


SMEM = pl.BlockSpec(memory_space=pltpu.SMEM)
SIDES = (0, 1)


def make_body(subj, slabs):
    pairs = []
    for first in SIDES:
        lower = [(i, i + 1) for i in range(first, slabs - 1, 2)]
        pairs.append(lower + [(j, i) for i, j in lower])

    def swap(x, side):
        return lax.ppermute(x, "slab", pairs[side])

    def turn(x, k):
        return lax.ppermute(x, "subj", [(i, (i + k) % subj) for i in range(subj)])

    def after(x, *others):
        return lax.optimization_barrier((x, *others))

    def body(template, subject, velocity):
        flow = velocity[0]
        target = subject[0]
        steps, _, Z, Y, X = flow.shape
        assert Z == 4 and steps == 2
        rows = template.shape[1]
        dt = 1.0 / steps
        place = lax.axis_index("slab")
        group = lax.axis_index("subj")
        even = 1 - place % 2
        facts = jnp.stack([group, place > 0, place < slabs - 1, even]).astype(jnp.int32)
        ups = (even, 1 - even)
        flow_spec = [
            pl.BlockSpec((1, 3, Z, Y, X), lambda *_, t=t: (t, 0, 0, 0, 0)) for t in range(steps)
        ]

        def up_at(facts_ref, i):
            return facts_ref[3] if i == 0 else 1 - facts_ref[3]

        tmpl_far = [
            swap(lax.dynamic_slice_in_dim(template, up * (Z - 2), 2, 0), i)
            for i, up in enumerate(ups)
        ]
        flow0_edge = [
            lax.dynamic_slice_in_dim(flow[0], up * (Z - 1), 1, 1)[:, 0] for up in ups
        ]
        flow0_far = [swap(flow0_edge[i], i) for i in SIDES]
        own_parts = [template] + [turn(template, k) for k in range(1, subj)]
        tmpl_far[0], tmpl_far[1], _, _ = after(*tmpl_far, *flow0_edge)
        edge = jnp.concatenate(tmpl_far, axis=0)
        edge_parts = [edge] + [turn(edge, k) for k in range(1, subj)]

        def forward(*refs):
            facts_ref, refs = refs[0], refs[1:]
            owns, edges = refs[:subj], refs[subj : 2 * subj]
            v0, v1, aim = refs[2 * subj : 2 * subj + 3]
            tmpl, img1, lam2, *srcs = refs[2 * subj + 3 :]
            for k in range(subj):
                start = pl.multiple_of(lax.rem(facts_ref[0] + subj - k, subj) * rows, rows)
                at = pl.ds(start, rows)
                tmpl[2 : Z + 2, at, :] = owns[k][...]
                for i in SIDES:
                    up = up_at(facts_ref, i)
                    for j in range(2):
                        tmpl[up * (Z + 2) + j, at, :] = edges[k][2 * i + j]
            for z in range(Z):
                v = [v0[0, d, z] for d in range(3)]
                f = tmpl[z + 2]
                img1[z] = advance(f, upwind(tmpl[z + 1], f, tmpl[z + 3], v), v, dt)
            for i in SIDES:
                z = 1 + up_at(facts_ref, i) * (Z - 3)
                v = [v1[0, d, z] for d in range(3)]
                f = img1[z]
                diffs = upwind(img1[z - 1], f, img1[z + 1], v)
                lam = advance(f, diffs, v, dt) - aim[z]
                lam2[i] = lam
                for d in range(3):
                    srcs[i][d] = (-MATCH * dt) * lam * diffs[d]

        outs = [struct(Z + 4, Y, X), struct(Z, Y, X), struct(2, Y, X)] + [struct(3, Y, X)] * 2
        operands = [facts] + own_parts + edge_parts + [flow, flow, target]
        tmpl, img1, lam2_in, *inner1 = call(
            forward,
            outs,
            [SMEM]
            + [whole(x) for x in own_parts + edge_parts]
            + [flow_spec[0], flow_spec[1], whole(target)],
            [whole(x) for x in outs],
            operands,
            "forward",
            weight=FORWARD,
        )
        far1 = [swap(inner1[0], 0), None]

        def middle(facts_ref, tmpl, img1, halo0, halo1, v1, aim, src0, src1, flux0, flux1, lam2, v0_far):
            for i, halo, src, flux in ((0, halo0, src0, flux0), (1, halo1, src1, flux1)):
                up = up_at(facts_ref, i)
                at = 1 + up * (Z + 1)
                v = [halo[d] for d in range(3)]
                for d in range(3):
                    v0_far[up, d] = v[d]
                f = tmpl[at]
                outside = advance(f, upwind(tmpl[at - 1], f, tmpl[at + 1], v), v, dt)
                z = up * (Z - 1)
                inside = img1[z + 1 - 2 * up]
                below = jnp.where(up == 1, inside, outside)
                above = jnp.where(up == 1, outside, inside)
                v = [v1[0, d, z] for d in range(3)]
                f = img1[z]
                diffs = upwind(below, f, above, v)
                lam = advance(f, diffs, v, dt) - aim[z]
                for d in range(3):
                    src[d] = (-MATCH * dt) * lam * diffs[d]
                lam2[i] = lam
                flux[...] = jnp.where(up == 1, jnp.minimum(v[0], 0.0), jnp.maximum(v[0], 0.0)) * lam

        outs = [struct(3, Y, X)] * 2 + [struct(Y, X)] * 2 + [struct(2, Y, X), struct(2, 3, Y, X)]
        operands = [facts, tmpl, img1, *flow0_far, flow, target]
        *outer1, flux_0, flux_1, lam2_out, v0_far = call(
            middle,
            outs,
            [SMEM] + [whole(x) for x in operands[1:5]] + [flow_spec[1], whole(target)],
            [whole(x) for x in outs],
            operands,
            "middle",
            weight=MIDDLE,
        )
        flux_far = [swap(flux_0, 0), swap(flux_1, 1)]

        def back(facts_ref, tmpl, lam2_in, lam2_out, v0, v1, lam1, part0, part1, src0, src1, lam2):
            for i in SIDES:
                up = up_at(facts_ref, i)
                lam2[1 + up * (Z - 3)] = lam2_in[i]
                lam2[up * (Z - 1)] = lam2_out[i]
            for z in range(Z):
                v = [v1[0, d, z] for d in range(3)]
                above = jnp.maximum(v1[0, 0, z + 1], 0.0) * lam2[z + 1] if z < Z - 1 else None
                below = jnp.minimum(v1[0, 0, z - 1], 0.0) * lam2[z - 1] if z > 0 else None
                lam1[z] = retreat(lam2[z], v, above, below, dt)
            for i, part, src in ((0, part0, src0), (1, part1, src1)):
                up = up_at(facts_ref, i)
                part[...] = lam1[up * (Z - 1)]
                z = 1 + up * (Z - 3)
                v = [v0[0, d, z] for d in range(3)]
                diffs = upwind(tmpl[z + 1], tmpl[z + 2], tmpl[z + 3], v)
                lam = lam1[z]
                for d in range(3):
                    src[d] = (-MATCH * dt) * lam * diffs[d]

        outs = [struct(Z, Y, X)] + [struct(Y, X)] * 2 + [struct(3, Y, X)] * 2
        operands = [facts, tmpl, lam2_in, lam2_out, flow, flow]
        lam1_part, part_0, part_1, *inner0 = call(
            back,
            outs,
            [SMEM] + [whole(x) for x in operands[1:4]] + [flow_spec[0], flow_spec[1]],
            [whole(x) for x in outs],
            operands,
            "back",
            weight=BACK,
            scratch=[pltpu.VMEM((Z, Y, X), jnp.float32)],
        )

        near1 = [swap(outer1[0], 0), None]

        *flux_far, far1[0] = after(*flux_far, far1[0])
        toward = (2 * even - 1).astype(jnp.float32) * dt
        lam1_edge = [part_0 + toward * flux_far[0], part_1 - toward * flux_far[1]]
        lam1_far = [swap(lam1_edge[i], i) for i in SIDES]

        far0 = [swap(after(inner0[0], *lam1_edge)[0], 0), None]
        held1, held2, near1[0], *lam1_far = after(inner1[1], outer1[1], near1[0], *lam1_far)
        far1[1] = swap(held1, 1)
        near1[1] = swap(held2, 1)
        held, far0[0] = after(inner0[1], far0[0], *lam1_far)[:2]
        far0[1] = swap(held, 1)

        def sweeps(facts_ref, s, v, out, u2):
            for z in range(-1, Z + 1):
                beside = plane_sum(s[z])
                if z - 1 in s:
                    beside = beside + s[z - 1]
                if z + 1 in s:
                    beside = beside + s[z + 1]
                u = (s[z] + beside * SEVENTH) * SEVENTH
                if z == -1:
                    u = jnp.where(facts_ref[1] > 0, u, 0.0)
                if z == Z:
                    u = jnp.where(facts_ref[2] > 0, u, 0.0)
                u2[z + 1] = u
            for z in range(Z):
                u = u2[z + 1]
                beside = plane_sum(u) + u2[z] + u2[z + 2]
                out[0, 0, z] = v[0, 0, z] + (s[z] + beside) * SEVENTH

        class Planes:
            def __init__(self, ref, low, high):
                self.ref, self.low, self.high = ref, low, high

            def __contains__(self, z):
                return self.low <= z <= self.high

            def __getitem__(self, z):
                return self.ref[z - self.low]

        part = pl.BlockSpec((1, Y, X), lambda d: (d, 0, 0))
        flow_part = [
            pl.BlockSpec((1, 1, Z, Y, X), lambda d, t=t: (t, d, 0, 0, 0)) for t in range(steps)
        ]
        u2_scratch = pltpu.VMEM((Z + 2, Y, X), jnp.float32)

        def last(facts_ref, tmpl, part, edge0, edge1, beyond0, beyond1, v0_far, v0, lam0, src, lam):
            for z in range(1, Z - 1):
                lam[z + 1] = part[z]
            for i, edge, beyond in ((0, edge0, beyond0), (1, edge1, beyond1)):
                up = up_at(facts_ref, i)
                lam[1 + up * (Z - 1)] = edge[...]
                lam[up * (Z + 1)] = beyond[...]

            def flow_at(z, d):
                return v0[0, d, z] if 0 <= z < Z else v0_far[0 if z < 0 else 1, d]

            for j, z in enumerate((-1, 0, Z - 1, Z)):
                v = [flow_at(z, d) for d in range(3)]
                diffs = upwind(tmpl[z + 1], tmpl[z + 2], tmpl[z + 3], v)
                for d in range(3):
                    src[j, d] = (-MATCH * dt) * lam[z + 1] * diffs[d]
            for z in range(Z):
                above = jnp.maximum(flow_at(z + 1, 0), 0.0) * lam[z + 2]
                below = jnp.minimum(flow_at(z - 1, 0), 0.0) * lam[z]
                v = [flow_at(z, d) for d in range(3)]
                lam0[z] = retreat(lam[z + 1], v, above, below, dt)

        outs = [struct(Z, Y, X), struct(4, 3, Y, X)]
        operands = [facts, tmpl, lam1_part, *lam1_edge, *lam1_far, v0_far, flow]
        lam0, rest0 = call(
            last,
            outs,
            [SMEM] + [whole(x) for x in operands[1:8]] + [flow_spec[0]],
            [whole(x) for x in outs],
            operands,
            "last",
            weight=LAST,
            scratch=[pltpu.VMEM((Z + 2, Y, X), jnp.float32)],
        )

        def share(k):
            start = lax.rem(group + k, subj) * rows
            return lax.dynamic_slice_in_dim(lam0, start, rows, axis=1)

        template_grad = share(0)
        for k in range(1, subj):
            template_grad = template_grad + turn(share(k), k)

        def smooth_0(facts_ref, in0, in1, rest, v, out, u2, s):
            for i, inner in ((0, in0), (1, in1)):
                s[2 + up_at(facts_ref, i) * (Z - 3)] = inner[0]
            for j, z in enumerate((-1, 0, Z - 1, Z)):
                s[z + 1] = rest[j, 0]
            sweeps(facts_ref, Planes(s, -1, Z), v, out, u2)

        gradient = call(
            smooth_0,
            struct(*flow.shape),
            [SMEM, part, part]
            + [pl.BlockSpec((4, 1, Y, X), lambda d: (0, d, 0, 0))]
            + [flow_part[0]],
            flow_part[0],
            [facts, *inner0, rest0, flow],
            "smooth_0",
            weight=SMOOTH,
            grid=(3,),
            scratch=[u2_scratch, pltpu.VMEM((Z + 2, Y, X), jnp.float32)],
        )

        def smooth_1(facts_ref, in0, in1, out0, out1, near0, near1, far0, far1, _, v, out, u2, s):
            for i, inner, outer, near, far in ((0, in0, out0, near0, far0), (1, in1, out1, near1, far1)):
                up = up_at(facts_ref, i)
                s[3 + up * (Z - 3)] = inner[0]
                s[2 + up * (Z - 1)] = outer[0]
                s[1 + up * (Z + 1)] = near[0]
                s[up * (Z + 3)] = far[0]
            sweeps(facts_ref, Planes(s, -2, Z + 1), v, out, u2)

        gradient = call(
            smooth_1,
            struct(*flow.shape),
            [SMEM] + [part] * 8 + [pl.BlockSpec(memory_space=pl.ANY), flow_part[1]],
            flow_part[1],
            [facts, *inner1, *outer1, *near1, *far1, gradient, flow],
            "smooth_1",
            weight=SMOOTH,
            grid=(3,),
            aliases={9: 0},
            scratch=[u2_scratch, pltpu.VMEM((Z + 4, Y, X), jnp.float32)],
        )

        def add_far(facts_ref, src, grad, out):
            for d in range(3):
                out[0, d, 0] = grad[0, d, 0] + src[d] * SEVENTH**3

        for i in SIDES:

            def boundary(_, facts_ref, i=i):
                return (0, 0, up_at(facts_ref, i) * (Z - 1), 0, 0)

            block = pl.BlockSpec((1, 3, 1, Y, X), boundary)
            gradient = call(
                add_far,
                struct(*flow.shape),
                [pl.BlockSpec((3, Y, X), lambda *_: (0, 0, 0)), block],
                block,
                [facts, far0[i], gradient],
                "add_far",
                aliases={2: 0},
                prefetch=1,
            )
        return gradient[None], template_grad

    return body


def solution(mesh):
    sizes = dict(mesh.shape)
    return jax.shard_map(
        make_body(sizes["subj"], sizes["slab"]),
        mesh=mesh,
        in_specs=(
            P("slab", "subj", None),
            P("subj", "slab", None, None),
            P("subj", None, None, "slab", None, None),
        ),
        out_specs=(P("subj", None, None, "slab", None, None), P("slab", "subj", None)),
        check_vma=False,
    )
```

```python
import jax
import jax.numpy as jnp
from jax import lax
from jax.experimental import pallas as pl
from jax.experimental.pallas import tpu as pltpu
from jax.sharding import PartitionSpec as P

MATCH = 5.0
SEVENTH = 1.0 / 7.0
MIB = 1 << 20
FORWARD, MIDDLE, BACK, SOURCES, LAST, SMOOTH = 0, 0, 1000, 0, 2000, 150


def col_prev(f):
    x = lax.broadcasted_iota(jnp.int32, f.shape, 1)
    return jnp.where(x == 0, 0.0, pltpu.roll(f, 1, 1))


def col_next(f):
    n = f.shape[1]
    x = lax.broadcasted_iota(jnp.int32, f.shape, 1)
    return jnp.where(x == n - 1, 0.0, pltpu.roll(f, n - 1, 1))


def row_prev(f):
    y = lax.broadcasted_iota(jnp.int32, f.shape, 0)
    return jnp.where(y == 0, 0.0, pltpu.roll(f, 1, 0))


def row_next(f):
    n = f.shape[0]
    y = lax.broadcasted_iota(jnp.int32, f.shape, 0)
    return jnp.where(y == n - 1, 0.0, pltpu.roll(f, n - 1, 0))


def upwind(below, f, above, v):
    return [
        jnp.where(v[0] >= 0.0, f - below, above - f),
        jnp.where(v[1] >= 0.0, f - row_prev(f), row_next(f) - f),
        jnp.where(v[2] >= 0.0, f - col_prev(f), col_next(f) - f),
    ]


def advance(f, diffs, v, dt):
    return f - dt * (v[0] * diffs[0] + v[1] * diffs[1] + v[2] * diffs[2])


def retreat(lam, v, pos_above, neg_below, dt):
    total = (jnp.abs(v[0]) + jnp.abs(v[1]) + jnp.abs(v[2])) * lam
    total = total - row_next(jnp.maximum(v[1], 0.0) * lam)
    total = total + row_prev(jnp.minimum(v[1], 0.0) * lam)
    total = total - col_next(jnp.maximum(v[2], 0.0) * lam)
    total = total + col_prev(jnp.minimum(v[2], 0.0) * lam)
    if pos_above is not None:
        total = total - pos_above
    if neg_below is not None:
        total = total + neg_below
    return lam - dt * total


def plane_sum(f):
    return row_prev(f) + row_next(f) + col_prev(f) + col_next(f)


def call(kernel, out_shape, in_specs, out_specs, operands, name, weight=0, grid=(1,), aliases=None, scratch=(), prefetch=0):
    return pl.pallas_call(
        kernel,
        out_shape=out_shape,
        grid_spec=pltpu.PrefetchScalarGridSpec(
            num_scalar_prefetch=prefetch,
            grid=grid,
            in_specs=in_specs,
            out_specs=out_specs,
            scratch_shapes=list(scratch),
        ),
        input_output_aliases=aliases or {},
        compiler_params=pltpu.CompilerParams(vmem_limit_bytes=48 * MIB),
        cost_estimate=pl.CostEstimate(
            flops=1024 + weight * 10000000, bytes_accessed=1024, transcendentals=0
        ),
        name=name,
    )(*operands)


def whole(x):
    zeros = (0,) * x.ndim
    return pl.BlockSpec(x.shape, lambda *_: zeros)


def struct(*shape):
    return jax.ShapeDtypeStruct(shape, jnp.float32)


SMEM = pl.BlockSpec(memory_space=pltpu.SMEM)
SIDES = (0, 1)


def make_body(subj, slabs):
    pairs = []
    for first in SIDES:
        lower = [(i, i + 1) for i in range(first, slabs - 1, 2)]
        pairs.append(lower + [(j, i) for i, j in lower])

    def swap(x, side):
        return lax.ppermute(x, "slab", pairs[side])

    def turn(x, k):
        return lax.ppermute(x, "subj", [(i, (i + k) % subj) for i in range(subj)])

    def after(x, *others):
        return lax.optimization_barrier((x, *others))

    def body(template, subject, velocity):
        flow = velocity[0]
        target = subject[0]
        steps, _, Z, Y, X = flow.shape
        assert Z == 4 and steps == 2
        rows = template.shape[1]
        dt = 1.0 / steps
        place = lax.axis_index("slab")
        group = lax.axis_index("subj")
        even = 1 - place % 2
        facts = jnp.stack([group, place > 0, place < slabs - 1, even]).astype(jnp.int32)
        ups = (even, 1 - even)
        flow_spec = [
            pl.BlockSpec((1, 3, Z, Y, X), lambda *_, t=t: (t, 0, 0, 0, 0)) for t in range(steps)
        ]

        def up_at(facts_ref, i):
            return facts_ref[3] if i == 0 else 1 - facts_ref[3]

        tmpl_far = [
            swap(lax.dynamic_slice_in_dim(template, up * (Z - 2), 2, 0), i)
            for i, up in enumerate(ups)
        ]
        flow0_edge = [
            lax.dynamic_slice_in_dim(flow[0], up * (Z - 1), 1, 1)[:, 0] for up in ups
        ]
        flow0_far = [swap(flow0_edge[i], i) for i in SIDES]
        own_parts = [template] + [turn(template, k) for k in range(1, subj)]
        tmpl_far[0], tmpl_far[1], _, _ = after(*tmpl_far, *flow0_edge)
        edge = jnp.concatenate(tmpl_far, axis=0)
        edge_parts = [edge] + [turn(edge, k) for k in range(1, subj)]

        def forward(*refs):
            facts_ref, refs = refs[0], refs[1:]
            owns, edges = refs[:subj], refs[subj : 2 * subj]
            v0, v1, aim = refs[2 * subj : 2 * subj + 3]
            tmpl, img1, lam2, *srcs = refs[2 * subj + 3 :]
            for k in range(subj):
                start = pl.multiple_of(lax.rem(facts_ref[0] + subj - k, subj) * rows, rows)
                at = pl.ds(start, rows)
                tmpl[2 : Z + 2, at, :] = owns[k][...]
                for i in SIDES:
                    up = up_at(facts_ref, i)
                    for j in range(2):
                        tmpl[up * (Z + 2) + j, at, :] = edges[k][2 * i + j]
            for z in range(Z):
                v = [v0[0, d, z] for d in range(3)]
                f = tmpl[z + 2]
                img1[z] = advance(f, upwind(tmpl[z + 1], f, tmpl[z + 3], v), v, dt)
            for i in SIDES:
                z = 1 + up_at(facts_ref, i) * (Z - 3)
                v = [v1[0, d, z] for d in range(3)]
                f = img1[z]
                diffs = upwind(img1[z - 1], f, img1[z + 1], v)
                lam = advance(f, diffs, v, dt) - aim[z]
                lam2[i] = lam
                for d in range(3):
                    srcs[i][d] = (-MATCH * dt) * lam * diffs[d]

        outs = [struct(Z + 4, Y, X), struct(Z, Y, X), struct(2, Y, X)] + [struct(3, Y, X)] * 2
        operands = [facts] + own_parts + edge_parts + [flow, flow, target]
        tmpl, img1, lam2_in, *inner1 = call(
            forward,
            outs,
            [SMEM]
            + [whole(x) for x in own_parts + edge_parts]
            + [flow_spec[0], flow_spec[1], whole(target)],
            [whole(x) for x in outs],
            operands,
            "forward",
            weight=FORWARD,
        )
        far1 = [swap(inner1[0], 0), None]

        def middle(facts_ref, tmpl, img1, halo0, halo1, v1, aim, src0, src1, flux0, flux1, lam2, v0_far):
            for i, halo, src, flux in ((0, halo0, src0, flux0), (1, halo1, src1, flux1)):
                up = up_at(facts_ref, i)
                at = 1 + up * (Z + 1)
                v = [halo[d] for d in range(3)]
                for d in range(3):
                    v0_far[up, d] = v[d]
                f = tmpl[at]
                outside = advance(f, upwind(tmpl[at - 1], f, tmpl[at + 1], v), v, dt)
                z = up * (Z - 1)
                inside = img1[z + 1 - 2 * up]
                below = jnp.where(up == 1, inside, outside)
                above = jnp.where(up == 1, outside, inside)
                v = [v1[0, d, z] for d in range(3)]
                f = img1[z]
                diffs = upwind(below, f, above, v)
                lam = advance(f, diffs, v, dt) - aim[z]
                for d in range(3):
                    src[d] = (-MATCH * dt) * lam * diffs[d]
                lam2[i] = lam
                flux[...] = jnp.where(up == 1, jnp.minimum(v[0], 0.0), jnp.maximum(v[0], 0.0)) * lam

        outs = [struct(3, Y, X)] * 2 + [struct(Y, X)] * 2 + [struct(2, Y, X), struct(2, 3, Y, X)]
        operands = [facts, tmpl, img1, *flow0_far, flow, target]
        *outer1, flux_0, flux_1, lam2_out, v0_far = call(
            middle,
            outs,
            [SMEM] + [whole(x) for x in operands[1:5]] + [flow_spec[1], whole(target)],
            [whole(x) for x in outs],
            operands,
            "middle",
            weight=MIDDLE,
        )
        flux_far = [swap(flux_0, 0), swap(flux_1, 1)]

        def back(facts_ref, lam2_in, lam2_out, v1, lam1, part0, part1, lam2):
            for i in SIDES:
                up = up_at(facts_ref, i)
                lam2[1 + up * (Z - 3)] = lam2_in[i]
                lam2[up * (Z - 1)] = lam2_out[i]
            for z in range(Z):
                v = [v1[0, d, z] for d in range(3)]
                above = jnp.maximum(v1[0, 0, z + 1], 0.0) * lam2[z + 1] if z < Z - 1 else None
                below = jnp.minimum(v1[0, 0, z - 1], 0.0) * lam2[z - 1] if z > 0 else None
                lam1[z] = retreat(lam2[z], v, above, below, dt)
            for i, part in ((0, part0), (1, part1)):
                part[...] = lam1[up_at(facts_ref, i) * (Z - 1)]

        outs = [struct(Z, Y, X)] + [struct(Y, X)] * 2
        operands = [facts, lam2_in, lam2_out, flow]
        lam1_part, part_0, part_1 = call(
            back,
            outs,
            [SMEM] + [whole(x) for x in operands[1:3]] + [flow_spec[1]],
            [whole(x) for x in outs],
            operands,
            "back",
            weight=BACK,
            scratch=[pltpu.VMEM((Z, Y, X), jnp.float32)],
        )

        near1 = [swap(outer1[0], 0), None]

        *flux_far, far1[0] = after(*flux_far, far1[0])
        toward = (2 * even - 1).astype(jnp.float32) * dt
        lam1_edge = [part_0 + toward * flux_far[0], part_1 - toward * flux_far[1]]
        lam1_far = [swap(lam1_edge[i], i) for i in SIDES]

        def sources(facts_ref, tmpl, part, edge0, edge1, v0, lam1, src0, src1, out0, out1):
            for i, edge, inner, outer in ((0, edge0, src0, out0), (1, edge1, src1, out1)):
                up = up_at(facts_ref, i)
                for z, src in ((1 + up * (Z - 3), inner), (up * (Z - 1), outer)):
                    lam = part[z] if src is inner else edge[...]
                    lam1[z] = lam
                    v = [v0[0, d, z] for d in range(3)]
                    diffs = upwind(tmpl[z + 1], tmpl[z + 2], tmpl[z + 3], v)
                    for d in range(3):
                        src[d] = (-MATCH * dt) * lam * diffs[d]

        outs = [struct(Z, Y, X)] + [struct(3, Y, X)] * 4
        operands = [facts, tmpl, lam1_part, *lam1_edge, flow]
        lam1, *inner_outer = call(
            sources,
            outs,
            [SMEM] + [whole(x) for x in operands[1:5]] + [flow_spec[0]],
            [whole(x) for x in outs],
            operands,
            "sources",
            weight=SOURCES,
        )
        inner0, outer0 = inner_outer[:2], inner_outer[2:]

        far0 = [swap(inner0[0], 0), None]
        held1, held2, near1[0], *lam1_far = after(inner1[1], outer1[1], near1[0], *lam1_far)
        far1[1] = swap(held1, 1)
        near1[1] = swap(held2, 1)
        held, far0[0] = after(inner0[1], far0[0], *lam1_far)[:2]
        far0[1] = swap(held, 1)

        def sweeps(facts_ref, s, v, out, u2):
            for z in range(-1, Z + 1):
                beside = plane_sum(s[z])
                if z - 1 in s:
                    beside = beside + s[z - 1]
                if z + 1 in s:
                    beside = beside + s[z + 1]
                u = (s[z] + beside * SEVENTH) * SEVENTH
                if z == -1:
                    u = jnp.where(facts_ref[1] > 0, u, 0.0)
                if z == Z:
                    u = jnp.where(facts_ref[2] > 0, u, 0.0)
                u2[z + 1] = u
            for z in range(Z):
                u = u2[z + 1]
                beside = plane_sum(u) + u2[z] + u2[z + 2]
                out[0, 0, z] = v[0, 0, z] + (s[z] + beside) * SEVENTH

        class Planes:
            def __init__(self, ref, low, high):
                self.ref, self.low, self.high = ref, low, high

            def __contains__(self, z):
                return self.low <= z <= self.high

            def __getitem__(self, z):
                return self.ref[z - self.low]

        part = pl.BlockSpec((1, Y, X), lambda d: (d, 0, 0))
        flow_part = [
            pl.BlockSpec((1, 1, Z, Y, X), lambda d, t=t: (t, d, 0, 0, 0)) for t in range(steps)
        ]
        u2_scratch = pltpu.VMEM((Z + 2, Y, X), jnp.float32)

        def last(facts_ref, tmpl, lam1, beyond0, beyond1, v0_far, v0, lam0, src, lam):
            for z in range(Z):
                lam[z + 1] = lam1[z]
            for i, beyond in ((0, beyond0), (1, beyond1)):
                lam[up_at(facts_ref, i) * (Z + 1)] = beyond[...]

            def flow_at(z, d):
                return v0[0, d, z] if 0 <= z < Z else v0_far[0 if z < 0 else 1, d]

            for j, z in enumerate((-1, Z)):
                v = [flow_at(z, d) for d in range(3)]
                diffs = upwind(tmpl[z + 1], tmpl[z + 2], tmpl[z + 3], v)
                for d in range(3):
                    src[j, d] = (-MATCH * dt) * lam[z + 1] * diffs[d]
            for z in range(Z):
                above = jnp.maximum(flow_at(z + 1, 0), 0.0) * lam[z + 2]
                below = jnp.minimum(flow_at(z - 1, 0), 0.0) * lam[z]
                v = [flow_at(z, d) for d in range(3)]
                lam0[z] = retreat(lam[z + 1], v, above, below, dt)

        outs = [struct(Z, Y, X), struct(2, 3, Y, X)]
        operands = [facts, tmpl, lam1, *lam1_far, v0_far, flow]
        lam0, near0 = call(
            last,
            outs,
            [SMEM] + [whole(x) for x in operands[1:6]] + [flow_spec[0]],
            [whole(x) for x in outs],
            operands,
            "last",
            weight=LAST,
            scratch=[pltpu.VMEM((Z + 2, Y, X), jnp.float32)],
        )

        def share(k):
            start = lax.rem(group + k, subj) * rows
            return lax.dynamic_slice_in_dim(lam0, start, rows, axis=1)

        template_grad = share(0)
        for k in range(1, subj):
            template_grad = template_grad + turn(share(k), k)

        def smooth_0(facts_ref, in0, in1, out0, out1, near, v, out, u2, s):
            for i, inner, outer in ((0, in0, out0), (1, in1, out1)):
                up = up_at(facts_ref, i)
                s[2 + up * (Z - 3)] = inner[0]
                s[1 + up * (Z - 1)] = outer[0]
            s[0] = near[0, 0]
            s[Z + 1] = near[1, 0]
            sweeps(facts_ref, Planes(s, -1, Z), v, out, u2)

        gradient = call(
            smooth_0,
            struct(*flow.shape),
            [SMEM] + [part] * 4
            + [pl.BlockSpec((2, 1, Y, X), lambda d: (0, d, 0, 0)), flow_part[0]],
            flow_part[0],
            [facts, *inner0, *outer0, near0, flow],
            "smooth_0",
            weight=SMOOTH,
            grid=(3,),
            scratch=[u2_scratch, pltpu.VMEM((Z + 2, Y, X), jnp.float32)],
        )

        def smooth_1(facts_ref, in0, in1, out0, out1, near0, near1, far0, far1, _, v, out, u2, s):
            for i, inner, outer, near, far in ((0, in0, out0, near0, far0), (1, in1, out1, near1, far1)):
                up = up_at(facts_ref, i)
                s[3 + up * (Z - 3)] = inner[0]
                s[2 + up * (Z - 1)] = outer[0]
                s[1 + up * (Z + 1)] = near[0]
                s[up * (Z + 3)] = far[0]
            sweeps(facts_ref, Planes(s, -2, Z + 1), v, out, u2)

        gradient = call(
            smooth_1,
            struct(*flow.shape),
            [SMEM] + [part] * 8 + [pl.BlockSpec(memory_space=pl.ANY), flow_part[1]],
            flow_part[1],
            [facts, *inner1, *outer1, *near1, *far1, gradient, flow],
            "smooth_1",
            weight=SMOOTH,
            grid=(3,),
            aliases={9: 0},
            scratch=[u2_scratch, pltpu.VMEM((Z + 4, Y, X), jnp.float32)],
        )

        def add_far(facts_ref, src, grad, out):
            for d in range(3):
                out[0, d, 0] = grad[0, d, 0] + src[d] * SEVENTH**3

        for i in SIDES:

            def boundary(_, facts_ref, i=i):
                return (0, 0, up_at(facts_ref, i) * (Z - 1), 0, 0)

            block = pl.BlockSpec((1, 3, 1, Y, X), boundary)
            gradient = call(
                add_far,
                struct(*flow.shape),
                [pl.BlockSpec((3, Y, X), lambda *_: (0, 0, 0)), block],
                block,
                [facts, far0[i], gradient],
                "add_far",
                aliases={2: 0},
                prefetch=1,
            )
        return gradient[None], template_grad

    return body


def solution(mesh):
    sizes = dict(mesh.shape)
    return jax.shard_map(
        make_body(sizes["subj"], sizes["slab"]),
        mesh=mesh,
        in_specs=(
            P("slab", "subj", None),
            P("subj", "slab", None, None),
            P("subj", None, None, "slab", None, None),
        ),
        out_specs=(P("subj", None, None, "slab", None, None), P("slab", "subj", None)),
        check_vma=False,
    )
```

```python
import jax
import jax.numpy as jnp
from jax import lax
from jax.experimental import pallas as pl
from jax.experimental.pallas import tpu as pltpu
from jax.sharding import PartitionSpec as P

MATCH = 5.0
SEVENTH = 1.0 / 7.0
MIB = 1 << 20
FORWARD, MIDDLE, BACK, SOURCES, LAST, SMOOTH = 0, 0, 1000, 0, 2000, 1000


def col_prev(f):
    x = lax.broadcasted_iota(jnp.int32, f.shape, 1)
    return jnp.where(x == 0, 0.0, pltpu.roll(f, 1, 1))


def col_next(f):
    n = f.shape[1]
    x = lax.broadcasted_iota(jnp.int32, f.shape, 1)
    return jnp.where(x == n - 1, 0.0, pltpu.roll(f, n - 1, 1))


def row_prev(f):
    y = lax.broadcasted_iota(jnp.int32, f.shape, 0)
    return jnp.where(y == 0, 0.0, pltpu.roll(f, 1, 0))


def row_next(f):
    n = f.shape[0]
    y = lax.broadcasted_iota(jnp.int32, f.shape, 0)
    return jnp.where(y == n - 1, 0.0, pltpu.roll(f, n - 1, 0))


def upwind(below, f, above, v):
    return [
        jnp.where(v[0] >= 0.0, f - below, above - f),
        jnp.where(v[1] >= 0.0, f - row_prev(f), row_next(f) - f),
        jnp.where(v[2] >= 0.0, f - col_prev(f), col_next(f) - f),
    ]


def advance(f, diffs, v, dt):
    return f - dt * (v[0] * diffs[0] + v[1] * diffs[1] + v[2] * diffs[2])


def retreat(lam, v, pos_above, neg_below, dt):
    total = (jnp.abs(v[0]) + jnp.abs(v[1]) + jnp.abs(v[2])) * lam
    total = total - row_next(jnp.maximum(v[1], 0.0) * lam)
    total = total + row_prev(jnp.minimum(v[1], 0.0) * lam)
    total = total - col_next(jnp.maximum(v[2], 0.0) * lam)
    total = total + col_prev(jnp.minimum(v[2], 0.0) * lam)
    if pos_above is not None:
        total = total - pos_above
    if neg_below is not None:
        total = total + neg_below
    return lam - dt * total


def plane_sum(f):
    return row_prev(f) + row_next(f) + col_prev(f) + col_next(f)


def call(kernel, out_shape, in_specs, out_specs, operands, name, weight=0, grid=(1,), aliases=None, scratch=(), prefetch=0):
    return pl.pallas_call(
        kernel,
        out_shape=out_shape,
        grid_spec=pltpu.PrefetchScalarGridSpec(
            num_scalar_prefetch=prefetch,
            grid=grid,
            in_specs=in_specs,
            out_specs=out_specs,
            scratch_shapes=list(scratch),
        ),
        input_output_aliases=aliases or {},
        compiler_params=pltpu.CompilerParams(vmem_limit_bytes=48 * MIB),
        cost_estimate=pl.CostEstimate(
            flops=1024 + weight * 10000000, bytes_accessed=1024, transcendentals=0
        ),
        name=name,
    )(*operands)


def whole(x):
    zeros = (0,) * x.ndim
    return pl.BlockSpec(x.shape, lambda *_: zeros)


def struct(*shape):
    return jax.ShapeDtypeStruct(shape, jnp.float32)


SMEM = pl.BlockSpec(memory_space=pltpu.SMEM)
SIDES = (0, 1)


def make_body(subj, slabs):
    pairs = []
    for first in SIDES:
        lower = [(i, i + 1) for i in range(first, slabs - 1, 2)]
        pairs.append(lower + [(j, i) for i, j in lower])

    def swap(x, side):
        return lax.ppermute(x, "slab", pairs[side])

    def turn(x, k):
        return lax.ppermute(x, "subj", [(i, (i + k) % subj) for i in range(subj)])

    def after(x, *others):
        return lax.optimization_barrier((x, *others))

    def body(template, subject, velocity):
        flow = velocity[0]
        target = subject[0]
        steps, _, Z, Y, X = flow.shape
        assert Z == 4 and steps == 2
        rows = template.shape[1]
        dt = 1.0 / steps
        place = lax.axis_index("slab")
        group = lax.axis_index("subj")
        even = 1 - place % 2
        facts = jnp.stack([group, place > 0, place < slabs - 1, even]).astype(jnp.int32)
        ups = (even, 1 - even)
        flow_spec = [
            pl.BlockSpec((1, 3, Z, Y, X), lambda *_, t=t: (t, 0, 0, 0, 0)) for t in range(steps)
        ]

        def up_at(facts_ref, i):
            return facts_ref[3] if i == 0 else 1 - facts_ref[3]

        tmpl_far = [
            swap(lax.dynamic_slice_in_dim(template, up * (Z - 2), 2, 0), i)
            for i, up in enumerate(ups)
        ]
        flow0_edge = [
            lax.dynamic_slice_in_dim(flow[0], up * (Z - 1), 1, 1)[:, 0] for up in ups
        ]
        flow0_far = [swap(flow0_edge[i], i) for i in SIDES]
        own_parts = [template] + [turn(template, k) for k in range(1, subj)]
        tmpl_far[0], tmpl_far[1], _, _ = after(*tmpl_far, *flow0_edge)
        edge = jnp.concatenate(tmpl_far, axis=0)
        edge_parts = [edge] + [turn(edge, k) for k in range(1, subj)]

        def forward(*refs):
            facts_ref, refs = refs[0], refs[1:]
            owns, edges = refs[:subj], refs[subj : 2 * subj]
            v0, v1, aim = refs[2 * subj : 2 * subj + 3]
            tmpl, img1, lam2, *srcs = refs[2 * subj + 3 :]
            for k in range(subj):
                start = pl.multiple_of(lax.rem(facts_ref[0] + subj - k, subj) * rows, rows)
                at = pl.ds(start, rows)
                tmpl[2 : Z + 2, at, :] = owns[k][...]
                for i in SIDES:
                    up = up_at(facts_ref, i)
                    for j in range(2):
                        tmpl[up * (Z + 2) + j, at, :] = edges[k][2 * i + j]
            for z in range(Z):
                v = [v0[0, d, z] for d in range(3)]
                f = tmpl[z + 2]
                img1[z] = advance(f, upwind(tmpl[z + 1], f, tmpl[z + 3], v), v, dt)
            for i in SIDES:
                z = 1 + up_at(facts_ref, i) * (Z - 3)
                v = [v1[0, d, z] for d in range(3)]
                f = img1[z]
                diffs = upwind(img1[z - 1], f, img1[z + 1], v)
                lam = advance(f, diffs, v, dt) - aim[z]
                lam2[i] = lam
                for d in range(3):
                    srcs[i][d] = (-MATCH * dt) * lam * diffs[d]

        outs = [struct(Z + 4, Y, X), struct(Z, Y, X), struct(2, Y, X)] + [struct(3, Y, X)] * 2
        operands = [facts] + own_parts + edge_parts + [flow, flow, target]
        tmpl, img1, lam2_in, *inner1 = call(
            forward,
            outs,
            [SMEM]
            + [whole(x) for x in own_parts + edge_parts]
            + [flow_spec[0], flow_spec[1], whole(target)],
            [whole(x) for x in outs],
            operands,
            "forward",
            weight=FORWARD,
        )
        far1 = [swap(inner1[0], 0), None]

        def middle(facts_ref, tmpl, img1, halo0, halo1, v1, aim, src0, src1, flux0, flux1, lam2, v0_far):
            for i, halo, src, flux in ((0, halo0, src0, flux0), (1, halo1, src1, flux1)):
                up = up_at(facts_ref, i)
                at = 1 + up * (Z + 1)
                v = [halo[d] for d in range(3)]
                for d in range(3):
                    v0_far[up, d] = v[d]
                f = tmpl[at]
                outside = advance(f, upwind(tmpl[at - 1], f, tmpl[at + 1], v), v, dt)
                z = up * (Z - 1)
                inside = img1[z + 1 - 2 * up]
                below = jnp.where(up == 1, inside, outside)
                above = jnp.where(up == 1, outside, inside)
                v = [v1[0, d, z] for d in range(3)]
                f = img1[z]
                diffs = upwind(below, f, above, v)
                lam = advance(f, diffs, v, dt) - aim[z]
                for d in range(3):
                    src[d] = (-MATCH * dt) * lam * diffs[d]
                lam2[i] = lam
                flux[...] = jnp.where(up == 1, jnp.minimum(v[0], 0.0), jnp.maximum(v[0], 0.0)) * lam

        outs = [struct(3, Y, X)] * 2 + [struct(Y, X)] * 2 + [struct(2, Y, X), struct(2, 3, Y, X)]
        operands = [facts, tmpl, img1, *flow0_far, flow, target]
        *outer1, flux_0, flux_1, lam2_out, v0_far = call(
            middle,
            outs,
            [SMEM] + [whole(x) for x in operands[1:5]] + [flow_spec[1], whole(target)],
            [whole(x) for x in outs],
            operands,
            "middle",
            weight=MIDDLE,
        )
        flux_far = [swap(flux_0, 0), swap(flux_1, 1)]

        def back(facts_ref, lam2_in, lam2_out, v1, lam1, part0, part1, lam2):
            for i in SIDES:
                up = up_at(facts_ref, i)
                lam2[1 + up * (Z - 3)] = lam2_in[i]
                lam2[up * (Z - 1)] = lam2_out[i]
            for z in range(Z):
                v = [v1[0, d, z] for d in range(3)]
                above = jnp.maximum(v1[0, 0, z + 1], 0.0) * lam2[z + 1] if z < Z - 1 else None
                below = jnp.minimum(v1[0, 0, z - 1], 0.0) * lam2[z - 1] if z > 0 else None
                lam1[z] = retreat(lam2[z], v, above, below, dt)
            for i, part in ((0, part0), (1, part1)):
                part[...] = lam1[up_at(facts_ref, i) * (Z - 1)]

        outs = [struct(Z, Y, X)] + [struct(Y, X)] * 2
        operands = [facts, lam2_in, lam2_out, flow]
        lam1_part, part_0, part_1 = call(
            back,
            outs,
            [SMEM] + [whole(x) for x in operands[1:3]] + [flow_spec[1]],
            [whole(x) for x in outs],
            operands,
            "back",
            weight=BACK,
            scratch=[pltpu.VMEM((Z, Y, X), jnp.float32)],
        )

        near1 = [swap(outer1[0], 0), None]

        *flux_far, far1[0] = after(*flux_far, far1[0])
        toward = (2 * even - 1).astype(jnp.float32) * dt
        lam1_edge = [part_0 + toward * flux_far[0], part_1 - toward * flux_far[1]]
        lam1_far = [swap(lam1_edge[i], i) for i in SIDES]

        def sources(facts_ref, tmpl, part, edge0, edge1, v0, lam1, src0, src1, out0, out1):
            for i, edge, inner, outer in ((0, edge0, src0, out0), (1, edge1, src1, out1)):
                up = up_at(facts_ref, i)
                for z, src in ((1 + up * (Z - 3), inner), (up * (Z - 1), outer)):
                    lam = part[z] if src is inner else edge[...]
                    lam1[z] = lam
                    v = [v0[0, d, z] for d in range(3)]
                    diffs = upwind(tmpl[z + 1], tmpl[z + 2], tmpl[z + 3], v)
                    for d in range(3):
                        src[d] = (-MATCH * dt) * lam * diffs[d]

        outs = [struct(Z, Y, X)] + [struct(3, Y, X)] * 4
        operands = [facts, tmpl, lam1_part, *lam1_edge, flow]
        lam1, *inner_outer = call(
            sources,
            outs,
            [SMEM] + [whole(x) for x in operands[1:5]] + [flow_spec[0]],
            [whole(x) for x in outs],
            operands,
            "sources",
            weight=SOURCES,
        )
        inner0, outer0 = inner_outer[:2], inner_outer[2:]

        far0 = [swap(inner0[0], 0), None]
        held, near1[0], *lam1_far = after((inner1[1], outer1[1]), near1[0], *lam1_far)
        far1[1], near1[1] = [swap(x, 1) for x in held]

        def sweeps(facts_ref, s, v, out, u2):
            for z in range(-1, Z + 1):
                beside = plane_sum(s[z])
                if z - 1 in s:
                    beside = beside + s[z - 1]
                if z + 1 in s:
                    beside = beside + s[z + 1]
                u = (s[z] + beside * SEVENTH) * SEVENTH
                if z == -1:
                    u = jnp.where(facts_ref[1] > 0, u, 0.0)
                if z == Z:
                    u = jnp.where(facts_ref[2] > 0, u, 0.0)
                u2[z + 1] = u
            for z in range(Z):
                u = u2[z + 1]
                beside = plane_sum(u) + u2[z] + u2[z + 2]
                out[0, 0, z] = v[0, 0, z] + (s[z] + beside) * SEVENTH

        class Planes:
            def __init__(self, ref, low, high):
                self.ref, self.low, self.high = ref, low, high

            def __contains__(self, z):
                return self.low <= z <= self.high

            def __getitem__(self, z):
                return self.ref[z - self.low]

        part = pl.BlockSpec((1, Y, X), lambda d: (d, 0, 0))
        flow_part = [
            pl.BlockSpec((1, 1, Z, Y, X), lambda d, t=t: (t, d, 0, 0, 0)) for t in range(steps)
        ]
        u2_scratch = pltpu.VMEM((Z + 2, Y, X), jnp.float32)

        def last(facts_ref, tmpl, lam1, beyond0, beyond1, v0_far, v0, lam0, src, lam):
            for z in range(Z):
                lam[z + 1] = lam1[z]
            for i, beyond in ((0, beyond0), (1, beyond1)):
                lam[up_at(facts_ref, i) * (Z + 1)] = beyond[...]

            def flow_at(z, d):
                return v0[0, d, z] if 0 <= z < Z else v0_far[0 if z < 0 else 1, d]

            for j, z in enumerate((-1, Z)):
                v = [flow_at(z, d) for d in range(3)]
                diffs = upwind(tmpl[z + 1], tmpl[z + 2], tmpl[z + 3], v)
                for d in range(3):
                    src[j, d] = (-MATCH * dt) * lam[z + 1] * diffs[d]
            for z in range(Z):
                above = jnp.maximum(flow_at(z + 1, 0), 0.0) * lam[z + 2]
                below = jnp.minimum(flow_at(z - 1, 0), 0.0) * lam[z]
                v = [flow_at(z, d) for d in range(3)]
                lam0[z] = retreat(lam[z + 1], v, above, below, dt)

        outs = [struct(Z, Y, X), struct(2, 3, Y, X)]
        operands = [facts, tmpl, lam1, *lam1_far, v0_far, flow]
        lam0, near0 = call(
            last,
            outs,
            [SMEM] + [whole(x) for x in operands[1:6]] + [flow_spec[0]],
            [whole(x) for x in outs],
            operands,
            "last",
            weight=LAST,
            scratch=[pltpu.VMEM((Z + 2, Y, X), jnp.float32)],
        )

        held, lam0 = after(inner0[1], lam0)
        far0[1] = swap(held, 1)

        def share(k):
            start = lax.rem(group + k, subj) * rows
            return lax.dynamic_slice_in_dim(lam0, start, rows, axis=1)

        template_grad = share(0)
        for k in range(1, subj):
            template_grad = template_grad + turn(share(k), k)

        def smooth_0(facts_ref, in0, in1, out0, out1, near, v, out, u2, s):
            for i, inner, outer in ((0, in0, out0), (1, in1, out1)):
                up = up_at(facts_ref, i)
                s[2 + up * (Z - 3)] = inner[0]
                s[1 + up * (Z - 1)] = outer[0]
            s[0] = near[0, 0]
            s[Z + 1] = near[1, 0]
            sweeps(facts_ref, Planes(s, -1, Z), v, out, u2)

        gradient = call(
            smooth_0,
            struct(*flow.shape),
            [SMEM] + [part] * 4
            + [pl.BlockSpec((2, 1, Y, X), lambda d: (0, d, 0, 0)), flow_part[0]],
            flow_part[0],
            [facts, *inner0, *outer0, near0, flow],
            "smooth_0",
            weight=SMOOTH,
            grid=(3,),
            scratch=[u2_scratch, pltpu.VMEM((Z + 2, Y, X), jnp.float32)],
        )

        def smooth_1(facts_ref, in0, in1, out0, out1, near0, near1, far0, far1, _, v, out, u2, s):
            for i, inner, outer, near, far in ((0, in0, out0, near0, far0), (1, in1, out1, near1, far1)):
                up = up_at(facts_ref, i)
                s[3 + up * (Z - 3)] = inner[0]
                s[2 + up * (Z - 1)] = outer[0]
                s[1 + up * (Z + 1)] = near[0]
                s[up * (Z + 3)] = far[0]
            sweeps(facts_ref, Planes(s, -2, Z + 1), v, out, u2)

        gradient = call(
            smooth_1,
            struct(*flow.shape),
            [SMEM] + [part] * 8 + [pl.BlockSpec(memory_space=pl.ANY), flow_part[1]],
            flow_part[1],
            [facts, *inner1, *outer1, *near1, *far1, gradient, flow],
            "smooth_1",
            weight=SMOOTH,
            grid=(3,),
            aliases={9: 0},
            scratch=[u2_scratch, pltpu.VMEM((Z + 4, Y, X), jnp.float32)],
        )

        def add_far(facts_ref, far_0, far_1, grad, out):
            def add(far):
                for d in range(3):
                    out[0, d, 0] = grad[0, d, 0] + far[d] * SEVENTH**3

            pl.when(pl.program_id(0) == 0)(lambda: add(far_0))
            pl.when(pl.program_id(0) == 1)(lambda: add(far_1))

        def boundary(i, facts_ref):
            up = jnp.where(i == 0, facts_ref[3], 1 - facts_ref[3])
            return (0, 0, up * (Z - 1), 0, 0)

        block = pl.BlockSpec((1, 3, 1, Y, X), boundary)
        gradient = call(
            add_far,
            struct(*flow.shape),
            [whole(x) for x in far0] + [block],
            block,
            [facts, *far0, gradient],
            "add_far",
            grid=(2,),
            aliases={3: 0},
            prefetch=1,
        )
        return gradient[None], template_grad

    return body


def solution(mesh):
    sizes = dict(mesh.shape)
    return jax.shard_map(
        make_body(sizes["subj"], sizes["slab"]),
        mesh=mesh,
        in_specs=(
            P("slab", "subj", None),
            P("subj", "slab", None, None),
            P("subj", None, None, "slab", None, None),
        ),
        out_specs=(P("subj", None, None, "slab", None, None), P("slab", "subj", None)),
        check_vma=False,
    )
```

```python
import jax
import jax.numpy as jnp
from jax import lax
from jax.experimental import pallas as pl
from jax.experimental.pallas import tpu as pltpu
from jax.sharding import PartitionSpec as P

MATCH = 5.0
SEVENTH = 1.0 / 7.0
MIB = 1 << 20
FORWARD, MIDDLE, BACK, SOURCES, LAST, SMOOTH = 0, 0, 1000, 0, 2000, 1000


def col_prev(f):
    x = lax.broadcasted_iota(jnp.int32, f.shape, 1)
    return jnp.where(x == 0, 0.0, pltpu.roll(f, 1, 1))


def col_next(f):
    n = f.shape[1]
    x = lax.broadcasted_iota(jnp.int32, f.shape, 1)
    return jnp.where(x == n - 1, 0.0, pltpu.roll(f, n - 1, 1))


def row_prev(f):
    y = lax.broadcasted_iota(jnp.int32, f.shape, 0)
    return jnp.where(y == 0, 0.0, pltpu.roll(f, 1, 0))


def row_next(f):
    n = f.shape[0]
    y = lax.broadcasted_iota(jnp.int32, f.shape, 0)
    return jnp.where(y == n - 1, 0.0, pltpu.roll(f, n - 1, 0))


def upwind(below, f, above, v):
    return [
        jnp.where(v[0] >= 0.0, f - below, above - f),
        jnp.where(v[1] >= 0.0, f - row_prev(f), row_next(f) - f),
        jnp.where(v[2] >= 0.0, f - col_prev(f), col_next(f) - f),
    ]


def advance(f, diffs, v, dt):
    return f - dt * (v[0] * diffs[0] + v[1] * diffs[1] + v[2] * diffs[2])


def retreat(lam, v, pos_above, neg_below, dt):
    total = (jnp.abs(v[0]) + jnp.abs(v[1]) + jnp.abs(v[2])) * lam
    total = total - row_next(jnp.maximum(v[1], 0.0) * lam)
    total = total + row_prev(jnp.minimum(v[1], 0.0) * lam)
    total = total - col_next(jnp.maximum(v[2], 0.0) * lam)
    total = total + col_prev(jnp.minimum(v[2], 0.0) * lam)
    if pos_above is not None:
        total = total - pos_above
    if neg_below is not None:
        total = total + neg_below
    return lam - dt * total


def plane_sum(f):
    return row_prev(f) + row_next(f) + col_prev(f) + col_next(f)


def call(kernel, out_shape, in_specs, out_specs, operands, name, weight=0, grid=(1,), aliases=None, scratch=(), prefetch=0):
    return pl.pallas_call(
        kernel,
        out_shape=out_shape,
        grid_spec=pltpu.PrefetchScalarGridSpec(
            num_scalar_prefetch=prefetch,
            grid=grid,
            in_specs=in_specs,
            out_specs=out_specs,
            scratch_shapes=list(scratch),
        ),
        input_output_aliases=aliases or {},
        compiler_params=pltpu.CompilerParams(vmem_limit_bytes=48 * MIB),
        cost_estimate=pl.CostEstimate(
            flops=1024 + weight * 10000000, bytes_accessed=1024, transcendentals=0
        ),
        name=name,
    )(*operands)


def whole(x):
    zeros = (0,) * x.ndim
    return pl.BlockSpec(x.shape, lambda *_: zeros)


def struct(*shape):
    return jax.ShapeDtypeStruct(shape, jnp.float32)


SMEM = pl.BlockSpec(memory_space=pltpu.SMEM)
SIDES = (0, 1)


def make_body(subj, slabs):
    pairs = []
    for first in SIDES:
        lower = [(i, i + 1) for i in range(first, slabs - 1, 2)]
        pairs.append(lower + [(j, i) for i, j in lower])

    def swap(x, side):
        return lax.ppermute(x, "slab", pairs[side])

    def turn(x, k):
        return lax.ppermute(x, "subj", [(i, (i + k) % subj) for i in range(subj)])

    def after(x, *others):
        return lax.optimization_barrier((x, *others))

    def body(template, subject, velocity):
        flow = velocity[0]
        target = subject[0]
        steps, _, Z, Y, X = flow.shape
        assert Z == 4 and steps == 2
        rows = template.shape[1]
        dt = 1.0 / steps
        place = lax.axis_index("slab")
        group = lax.axis_index("subj")
        even = 1 - place % 2
        facts = jnp.stack([group, place > 0, place < slabs - 1, even]).astype(jnp.int32)
        ups = (even, 1 - even)
        flow_spec = [
            pl.BlockSpec((1, 3, Z, Y, X), lambda *_, t=t: (t, 0, 0, 0, 0)) for t in range(steps)
        ]

        def up_at(facts_ref, i):
            return facts_ref[3] if i == 0 else 1 - facts_ref[3]

        tmpl_far = [
            swap(lax.dynamic_slice_in_dim(template, up * (Z - 2), 2, 0), i)
            for i, up in enumerate(ups)
        ]
        flow0_edge = [
            lax.dynamic_slice(velocity, (0, 0, 0, up * (Z - 1), 0, 0), (1, 1, 3, 1, Y, X))[0, 0, :, 0]
            for up in ups
        ]
        flow0_far = [swap(flow0_edge[i], i) for i in SIDES]
        own_parts = [template] + [turn(template, k) for k in range(1, subj)]
        tmpl_far[0], tmpl_far[1], _, _ = after(*tmpl_far, *flow0_edge)
        edge = jnp.concatenate(tmpl_far, axis=0)
        edge_parts = [edge] + [turn(edge, k) for k in range(1, subj)]

        def forward(*refs):
            facts_ref, refs = refs[0], refs[1:]
            owns, edges = refs[:subj], refs[subj : 2 * subj]
            v0, v1, aim = refs[2 * subj : 2 * subj + 3]
            tmpl, img1, lam2, *srcs = refs[2 * subj + 3 :]
            for k in range(subj):
                start = pl.multiple_of(lax.rem(facts_ref[0] + subj - k, subj) * rows, rows)
                at = pl.ds(start, rows)
                tmpl[2 : Z + 2, at, :] = owns[k][...]
                for i in SIDES:
                    up = up_at(facts_ref, i)
                    for j in range(2):
                        tmpl[up * (Z + 2) + j, at, :] = edges[k][2 * i + j]
            for z in range(Z):
                v = [v0[0, d, z] for d in range(3)]
                f = tmpl[z + 2]
                img1[z] = advance(f, upwind(tmpl[z + 1], f, tmpl[z + 3], v), v, dt)
            for i in SIDES:
                z = 1 + up_at(facts_ref, i) * (Z - 3)
                v = [v1[0, d, z] for d in range(3)]
                f = img1[z]
                diffs = upwind(img1[z - 1], f, img1[z + 1], v)
                lam = advance(f, diffs, v, dt) - aim[z]
                lam2[i] = lam
                for d in range(3):
                    srcs[i][d] = (-MATCH * dt) * lam * diffs[d]

        outs = [struct(Z + 4, Y, X), struct(Z, Y, X), struct(2, Y, X)] + [struct(3, Y, X)] * 2
        operands = [facts] + own_parts + edge_parts + [flow, flow, target]
        tmpl, img1, lam2_in, *inner1 = call(
            forward,
            outs,
            [SMEM]
            + [whole(x) for x in own_parts + edge_parts]
            + [flow_spec[0], flow_spec[1], whole(target)],
            [whole(x) for x in outs],
            operands,
            "forward",
            weight=FORWARD,
        )
        far1 = [swap(inner1[0], 0), None]

        def middle(facts_ref, tmpl, img1, halo0, halo1, v1, aim, src0, src1, flux0, flux1, lam2, v0_far):
            for i, halo, src, flux in ((0, halo0, src0, flux0), (1, halo1, src1, flux1)):
                up = up_at(facts_ref, i)
                at = 1 + up * (Z + 1)
                v = [halo[d] for d in range(3)]
                for d in range(3):
                    v0_far[up, d] = v[d]
                f = tmpl[at]
                outside = advance(f, upwind(tmpl[at - 1], f, tmpl[at + 1], v), v, dt)
                z = up * (Z - 1)
                inside = img1[z + 1 - 2 * up]
                below = jnp.where(up == 1, inside, outside)
                above = jnp.where(up == 1, outside, inside)
                v = [v1[0, d, z] for d in range(3)]
                f = img1[z]
                diffs = upwind(below, f, above, v)
                lam = advance(f, diffs, v, dt) - aim[z]
                for d in range(3):
                    src[d] = (-MATCH * dt) * lam * diffs[d]
                lam2[i] = lam
                flux[...] = jnp.where(up == 1, jnp.minimum(v[0], 0.0), jnp.maximum(v[0], 0.0)) * lam

        outs = [struct(3, Y, X)] * 2 + [struct(Y, X)] * 2 + [struct(2, Y, X), struct(2, 3, Y, X)]
        operands = [facts, tmpl, img1, *flow0_far, flow, target]
        *outer1, flux_0, flux_1, lam2_out, v0_far = call(
            middle,
            outs,
            [SMEM] + [whole(x) for x in operands[1:5]] + [flow_spec[1], whole(target)],
            [whole(x) for x in outs],
            operands,
            "middle",
            weight=MIDDLE,
        )
        flux_far = [swap(flux_0, 0), swap(flux_1, 1)]

        def back(facts_ref, lam2_in, lam2_out, v1, lam1, part0, part1, lam2):
            for i in SIDES:
                up = up_at(facts_ref, i)
                lam2[1 + up * (Z - 3)] = lam2_in[i]
                lam2[up * (Z - 1)] = lam2_out[i]
            for z in range(Z):
                v = [v1[0, d, z] for d in range(3)]
                above = jnp.maximum(v1[0, 0, z + 1], 0.0) * lam2[z + 1] if z < Z - 1 else None
                below = jnp.minimum(v1[0, 0, z - 1], 0.0) * lam2[z - 1] if z > 0 else None
                lam1[z] = retreat(lam2[z], v, above, below, dt)
            for i, part in ((0, part0), (1, part1)):
                part[...] = lam1[up_at(facts_ref, i) * (Z - 1)]

        outs = [struct(Z, Y, X)] + [struct(Y, X)] * 2
        operands = [facts, lam2_in, lam2_out, flow]
        lam1_part, part_0, part_1 = call(
            back,
            outs,
            [SMEM] + [whole(x) for x in operands[1:3]] + [flow_spec[1]],
            [whole(x) for x in outs],
            operands,
            "back",
            weight=BACK,
            scratch=[pltpu.VMEM((Z, Y, X), jnp.float32)],
        )

        near1 = [swap(outer1[0], 0), None]

        *flux_far, far1[0] = after(*flux_far, far1[0])
        toward = (2 * even - 1).astype(jnp.float32) * dt
        lam1_edge = [part_0 + toward * flux_far[0], part_1 - toward * flux_far[1]]
        lam1_far = [swap(lam1_edge[i], i) for i in SIDES]

        def sources(facts_ref, tmpl, part, edge0, edge1, v0, lam1, src0, src1, out0, out1):
            for i, edge, inner, outer in ((0, edge0, src0, out0), (1, edge1, src1, out1)):
                up = up_at(facts_ref, i)
                for z, src in ((1 + up * (Z - 3), inner), (up * (Z - 1), outer)):
                    lam = part[z] if src is inner else edge[...]
                    lam1[z] = lam
                    v = [v0[0, d, z] for d in range(3)]
                    diffs = upwind(tmpl[z + 1], tmpl[z + 2], tmpl[z + 3], v)
                    for d in range(3):
                        src[d] = (-MATCH * dt) * lam * diffs[d]

        outs = [struct(Z, Y, X)] + [struct(3, Y, X)] * 4
        operands = [facts, tmpl, lam1_part, *lam1_edge, flow]
        lam1, *inner_outer = call(
            sources,
            outs,
            [SMEM] + [whole(x) for x in operands[1:5]] + [flow_spec[0]],
            [whole(x) for x in outs],
            operands,
            "sources",
            weight=SOURCES,
        )
        inner0, outer0 = inner_outer[:2], inner_outer[2:]

        far0 = [swap(inner0[0], 0), None]
        held, near1[0], *lam1_far = after((inner1[1], outer1[1]), near1[0], *lam1_far)
        far1[1], near1[1] = [swap(x, 1) for x in held]

        def sweeps(facts_ref, s, v, out, u2):
            for z in range(-1, Z + 1):
                beside = plane_sum(s[z])
                if z - 1 in s:
                    beside = beside + s[z - 1]
                if z + 1 in s:
                    beside = beside + s[z + 1]
                u = (s[z] + beside * SEVENTH) * SEVENTH
                if z == -1:
                    u = jnp.where(facts_ref[1] > 0, u, 0.0)
                if z == Z:
                    u = jnp.where(facts_ref[2] > 0, u, 0.0)
                u2[z + 1] = u
            for z in range(Z):
                u = u2[z + 1]
                beside = plane_sum(u) + u2[z] + u2[z + 2]
                out[0, 0, z] = v[0, 0, z] + (s[z] + beside) * SEVENTH

        class Planes:
            def __init__(self, ref, low, high):
                self.ref, self.low, self.high = ref, low, high

            def __contains__(self, z):
                return self.low <= z <= self.high

            def __getitem__(self, z):
                return self.ref[z - self.low]

        part = pl.BlockSpec((1, Y, X), lambda d: (d, 0, 0))
        flow_part = [
            pl.BlockSpec((1, 1, Z, Y, X), lambda d, t=t: (t, d, 0, 0, 0)) for t in range(steps)
        ]
        u2_scratch = pltpu.VMEM((Z + 2, Y, X), jnp.float32)

        def last(facts_ref, tmpl, lam1, beyond0, beyond1, v0_far, v0, lam0, src, lam):
            for z in range(Z):
                lam[z + 1] = lam1[z]
            for i, beyond in ((0, beyond0), (1, beyond1)):
                lam[up_at(facts_ref, i) * (Z + 1)] = beyond[...]

            def flow_at(z, d):
                return v0[0, d, z] if 0 <= z < Z else v0_far[0 if z < 0 else 1, d]

            for j, z in enumerate((-1, Z)):
                v = [flow_at(z, d) for d in range(3)]
                diffs = upwind(tmpl[z + 1], tmpl[z + 2], tmpl[z + 3], v)
                for d in range(3):
                    src[j, d] = (-MATCH * dt) * lam[z + 1] * diffs[d]
            for z in range(Z):
                above = jnp.maximum(flow_at(z + 1, 0), 0.0) * lam[z + 2]
                below = jnp.minimum(flow_at(z - 1, 0), 0.0) * lam[z]
                v = [flow_at(z, d) for d in range(3)]
                lam0[z] = retreat(lam[z + 1], v, above, below, dt)

        outs = [struct(Z, Y, X), struct(2, 3, Y, X)]
        operands = [facts, tmpl, lam1, *lam1_far, v0_far, flow]
        lam0, near0 = call(
            last,
            outs,
            [SMEM] + [whole(x) for x in operands[1:6]] + [flow_spec[0]],
            [whole(x) for x in outs],
            operands,
            "last",
            weight=LAST,
            scratch=[pltpu.VMEM((Z + 2, Y, X), jnp.float32)],
        )

        held, lam0 = after(inner0[1], lam0)
        far0[1] = swap(held, 1)

        def share(k):
            start = lax.rem(group + k, subj) * rows
            return lax.dynamic_slice_in_dim(lam0, start, rows, axis=1)

        template_grad = share(0)
        for k in range(1, subj):
            template_grad = template_grad + turn(share(k), k)

        def smooth_0(facts_ref, in0, in1, out0, out1, near, v, out, rim, u2, s):
            for i, inner, outer in ((0, in0, out0), (1, in1, out1)):
                up = up_at(facts_ref, i)
                s[2 + up * (Z - 3)] = inner[0]
                s[1 + up * (Z - 1)] = outer[0]
            s[0] = near[0, 0]
            s[Z + 1] = near[1, 0]
            sweeps(facts_ref, Planes(s, -1, Z), v, out, u2)
            for i in SIDES:
                rim[i, 0] = out[0, 0, up_at(facts_ref, i) * (Z - 1)]

        both = pl.BlockSpec((2, 1, Y, X), lambda d: (0, d, 0, 0))
        gradient, rim = call(
            smooth_0,
            [struct(*flow.shape), struct(2, 3, Y, X)],
            [SMEM] + [part] * 4 + [both, flow_part[0]],
            [flow_part[0], both],
            [facts, *inner0, *outer0, near0, flow],
            "smooth_0",
            weight=SMOOTH,
            grid=(3,),
            scratch=[u2_scratch, pltpu.VMEM((Z + 2, Y, X), jnp.float32)],
        )

        def smooth_1(facts_ref, in0, in1, out0, out1, near0, near1, far0, far1, _, v, out, u2, s):
            for i, inner, outer, near, far in ((0, in0, out0, near0, far0), (1, in1, out1, near1, far1)):
                up = up_at(facts_ref, i)
                s[3 + up * (Z - 3)] = inner[0]
                s[2 + up * (Z - 1)] = outer[0]
                s[1 + up * (Z + 1)] = near[0]
                s[up * (Z + 3)] = far[0]
            sweeps(facts_ref, Planes(s, -2, Z + 1), v, out, u2)

        gradient = call(
            smooth_1,
            struct(*flow.shape),
            [SMEM] + [part] * 8 + [pl.BlockSpec(memory_space=pl.ANY), flow_part[1]],
            flow_part[1],
            [facts, *inner1, *outer1, *near1, *far1, gradient, flow],
            "smooth_1",
            weight=SMOOTH,
            grid=(3,),
            aliases={9: 0},
            scratch=[u2_scratch, pltpu.VMEM((Z + 4, Y, X), jnp.float32)],
        )

        def add_far(facts_ref, far_0, far_1, rim, _, out):
            def add(i, far):
                for d in range(3):
                    out[0, d, 0] = rim[i, d] + far[d] * SEVENTH**3

            pl.when(pl.program_id(0) == 0)(lambda: add(0, far_0))
            pl.when(pl.program_id(0) == 1)(lambda: add(1, far_1))

        def boundary(i, facts_ref):
            up = jnp.where(i == 0, facts_ref[3], 1 - facts_ref[3])
            return (0, 0, up * (Z - 1), 0, 0)

        gradient = call(
            add_far,
            struct(*flow.shape),
            [whole(x) for x in (*far0, rim)] + [pl.BlockSpec(memory_space=pl.ANY)],
            pl.BlockSpec((1, 3, 1, Y, X), boundary),
            [facts, *far0, rim, gradient],
            "add_far",
            grid=(2,),
            aliases={4: 0},
            prefetch=1,
        )
        return gradient[None], template_grad

    return body


def solution(mesh):
    sizes = dict(mesh.shape)
    return jax.shard_map(
        make_body(sizes["subj"], sizes["slab"]),
        mesh=mesh,
        in_specs=(
            P("slab", "subj", None),
            P("subj", "slab", None, None),
            P("subj", None, None, "slab", None, None),
        ),
        out_specs=(P("subj", None, None, "slab", None, None), P("slab", "subj", None)),
        check_vma=False,
    )
```

```python
import jax
import jax.numpy as jnp
from jax import lax
from jax.experimental import pallas as pl
from jax.experimental.pallas import tpu as pltpu
from jax.sharding import PartitionSpec as P

MATCH = 5.0
SEVENTH = 1.0 / 7.0
MIB = 1 << 20
FORWARD, MIDDLE, BACK, SOURCES, LAST, SMOOTH = 0, 0, 1000, 0, 2000, 1000


def col_prev(f):
    x = lax.broadcasted_iota(jnp.int32, f.shape, 1)
    return jnp.where(x == 0, 0.0, pltpu.roll(f, 1, 1))


def col_next(f):
    n = f.shape[1]
    x = lax.broadcasted_iota(jnp.int32, f.shape, 1)
    return jnp.where(x == n - 1, 0.0, pltpu.roll(f, n - 1, 1))


def row_prev(f):
    y = lax.broadcasted_iota(jnp.int32, f.shape, 0)
    return jnp.where(y == 0, 0.0, pltpu.roll(f, 1, 0))


def row_next(f):
    n = f.shape[0]
    y = lax.broadcasted_iota(jnp.int32, f.shape, 0)
    return jnp.where(y == n - 1, 0.0, pltpu.roll(f, n - 1, 0))


def upwind(below, f, above, v):
    return [
        jnp.where(v[0] >= 0.0, f - below, above - f),
        jnp.where(v[1] >= 0.0, f - row_prev(f), row_next(f) - f),
        jnp.where(v[2] >= 0.0, f - col_prev(f), col_next(f) - f),
    ]


def advance(f, diffs, v, dt):
    return f - dt * (v[0] * diffs[0] + v[1] * diffs[1] + v[2] * diffs[2])


def retreat(lam, v, pos_above, neg_below, dt):
    total = (jnp.abs(v[0]) + jnp.abs(v[1]) + jnp.abs(v[2])) * lam
    total = total - row_next(jnp.maximum(v[1], 0.0) * lam)
    total = total + row_prev(jnp.minimum(v[1], 0.0) * lam)
    total = total - col_next(jnp.maximum(v[2], 0.0) * lam)
    total = total + col_prev(jnp.minimum(v[2], 0.0) * lam)
    if pos_above is not None:
        total = total - pos_above
    if neg_below is not None:
        total = total + neg_below
    return lam - dt * total


def plane_sum(f):
    return row_prev(f) + row_next(f) + col_prev(f) + col_next(f)


def call(kernel, out_shape, in_specs, out_specs, operands, name, weight=0, grid=(1,), aliases=None, scratch=(), prefetch=0):
    return pl.pallas_call(
        kernel,
        out_shape=out_shape,
        grid_spec=pltpu.PrefetchScalarGridSpec(
            num_scalar_prefetch=prefetch,
            grid=grid,
            in_specs=in_specs,
            out_specs=out_specs,
            scratch_shapes=list(scratch),
        ),
        input_output_aliases=aliases or {},
        compiler_params=pltpu.CompilerParams(vmem_limit_bytes=48 * MIB),
        cost_estimate=pl.CostEstimate(
            flops=1024 + weight * 10000000, bytes_accessed=1024, transcendentals=0
        ),
        name=name,
    )(*operands)


def whole(x):
    zeros = (0,) * x.ndim
    return pl.BlockSpec(x.shape, lambda *_: zeros)


def struct(*shape):
    return jax.ShapeDtypeStruct(shape, jnp.float32)


SMEM = pl.BlockSpec(memory_space=pltpu.SMEM)
SIDES = (0, 1)


def make_body(subj, slabs):
    pairs = []
    for first in SIDES:
        lower = [(i, i + 1) for i in range(first, slabs - 1, 2)]
        pairs.append(lower + [(j, i) for i, j in lower])

    def swap(x, side):
        return lax.ppermute(x, "slab", pairs[side])

    def turn(x, k):
        return lax.ppermute(x, "subj", [(i, (i + k) % subj) for i in range(subj)])

    def after(x, *others):
        return lax.optimization_barrier((x, *others))

    def body(template, subject, velocity):
        flow = velocity[0]
        target = subject[0]
        steps, _, Z, Y, X = flow.shape
        assert Z == 4 and steps == 2
        rows = template.shape[1]
        dt = 1.0 / steps
        place = lax.axis_index("slab")
        group = lax.axis_index("subj")
        even = 1 - place % 2
        facts = jnp.stack([group, place > 0, place < slabs - 1, even]).astype(jnp.int32)
        ups = (even, 1 - even)
        flow_spec = [
            pl.BlockSpec((1, 3, Z, Y, X), lambda *_, t=t: (t, 0, 0, 0, 0)) for t in range(steps)
        ]

        def up_at(facts_ref, i):
            return facts_ref[3] if i == 0 else 1 - facts_ref[3]

        tmpl_far = [
            swap(lax.dynamic_slice_in_dim(template, up * (Z - 2), 2, 0), i)
            for i, up in enumerate(ups)
        ]
        flow0_edge = [
            lax.dynamic_slice(velocity, (0, 0, 0, up * (Z - 1), 0, 0), (1, 1, 3, 1, Y, X))[0, 0, :, 0]
            for up in ups
        ]
        flow0_far = [swap(flow0_edge[i], i) for i in SIDES]
        own_parts = [template] + [turn(template, k) for k in range(1, subj)]
        tmpl_far[1], tmpl_far[0], _, _ = after(*tmpl_far[::-1], *flow0_edge)
        edge = jnp.concatenate(tmpl_far[::-1], axis=0)
        edge_parts = [edge] + [turn(edge, k) for k in range(1, subj)]

        def forward(*refs):
            facts_ref, refs = refs[0], refs[1:]
            owns, edges = refs[:subj], refs[subj : 2 * subj]
            v0, v1, aim = refs[2 * subj : 2 * subj + 3]
            tmpl, img1, lam2, *srcs = refs[2 * subj + 3 :]
            for k in range(subj):
                start = pl.multiple_of(lax.rem(facts_ref[0] + subj - k, subj) * rows, rows)
                at = pl.ds(start, rows)
                tmpl[2 : Z + 2, at, :] = owns[k][...]
                for i in SIDES:
                    up = up_at(facts_ref, i)
                    for j in range(2):
                        tmpl[up * (Z + 2) + j, at, :] = edges[k][2 * (1 - i) + j]
            for z in range(Z):
                v = [v0[0, d, z] for d in range(3)]
                f = tmpl[z + 2]
                img1[z] = advance(f, upwind(tmpl[z + 1], f, tmpl[z + 3], v), v, dt)
            for i in SIDES:
                z = 1 + up_at(facts_ref, i) * (Z - 3)
                v = [v1[0, d, z] for d in range(3)]
                f = img1[z]
                diffs = upwind(img1[z - 1], f, img1[z + 1], v)
                lam = advance(f, diffs, v, dt) - aim[z]
                lam2[i] = lam
                for d in range(3):
                    srcs[i][d] = (-MATCH * dt) * lam * diffs[d]

        outs = [struct(Z + 4, Y, X), struct(Z, Y, X), struct(2, Y, X)] + [struct(3, Y, X)] * 2
        operands = [facts] + own_parts + edge_parts + [flow, flow, target]
        tmpl, img1, lam2_in, *inner1 = call(
            forward,
            outs,
            [SMEM]
            + [whole(x) for x in own_parts + edge_parts]
            + [flow_spec[0], flow_spec[1], whole(target)],
            [whole(x) for x in outs],
            operands,
            "forward",
            weight=FORWARD,
        )
        far1 = [swap(inner1[0], 0), None]

        def middle(facts_ref, tmpl, img1, halo0, halo1, v1, aim, src0, src1, flux0, flux1, lam2, v0_far):
            for i, halo, src, flux in ((0, halo0, src0, flux0), (1, halo1, src1, flux1)):
                up = up_at(facts_ref, i)
                at = 1 + up * (Z + 1)
                v = [halo[d] for d in range(3)]
                for d in range(3):
                    v0_far[up, d] = v[d]
                f = tmpl[at]
                outside = advance(f, upwind(tmpl[at - 1], f, tmpl[at + 1], v), v, dt)
                z = up * (Z - 1)
                inside = img1[z + 1 - 2 * up]
                below = jnp.where(up == 1, inside, outside)
                above = jnp.where(up == 1, outside, inside)
                v = [v1[0, d, z] for d in range(3)]
                f = img1[z]
                diffs = upwind(below, f, above, v)
                lam = advance(f, diffs, v, dt) - aim[z]
                for d in range(3):
                    src[d] = (-MATCH * dt) * lam * diffs[d]
                lam2[i] = lam
                flux[...] = jnp.where(up == 1, jnp.minimum(v[0], 0.0), jnp.maximum(v[0], 0.0)) * lam

        outs = [struct(3, Y, X)] * 2 + [struct(Y, X)] * 2 + [struct(2, Y, X), struct(2, 3, Y, X)]
        operands = [facts, tmpl, img1, *flow0_far, flow, target]
        *outer1, flux_0, flux_1, lam2_out, v0_far = call(
            middle,
            outs,
            [SMEM] + [whole(x) for x in operands[1:5]] + [flow_spec[1], whole(target)],
            [whole(x) for x in outs],
            operands,
            "middle",
            weight=MIDDLE,
        )
        flux_far = [swap(flux_0, 0), swap(flux_1, 1)]

        def back(facts_ref, lam2_in, lam2_out, v1, lam1, part0, part1, lam2):
            for i in SIDES:
                up = up_at(facts_ref, i)
                lam2[1 + up * (Z - 3)] = lam2_in[i]
                lam2[up * (Z - 1)] = lam2_out[i]
            for z in range(Z):
                v = [v1[0, d, z] for d in range(3)]
                above = jnp.maximum(v1[0, 0, z + 1], 0.0) * lam2[z + 1] if z < Z - 1 else None
                below = jnp.minimum(v1[0, 0, z - 1], 0.0) * lam2[z - 1] if z > 0 else None
                lam1[z] = retreat(lam2[z], v, above, below, dt)
            for i, part in ((0, part0), (1, part1)):
                part[...] = lam1[up_at(facts_ref, i) * (Z - 1)]

        outs = [struct(Z, Y, X)] + [struct(Y, X)] * 2
        operands = [facts, lam2_in, lam2_out, flow]
        lam1_part, part_0, part_1 = call(
            back,
            outs,
            [SMEM] + [whole(x) for x in operands[1:3]] + [flow_spec[1]],
            [whole(x) for x in outs],
            operands,
            "back",
            weight=BACK,
            scratch=[pltpu.VMEM((Z, Y, X), jnp.float32)],
        )

        near1 = [swap(outer1[0], 0), None]

        *flux_far, far1[0] = after(*flux_far, far1[0])
        toward = (2 * even - 1).astype(jnp.float32) * dt
        lam1_edge = [part_0 + toward * flux_far[0], part_1 - toward * flux_far[1]]
        lam1_far = [swap(lam1_edge[i], i) for i in SIDES]

        def sources(facts_ref, tmpl, part, edge0, edge1, v0, lam1, src0, src1, out0, out1):
            for i, edge, inner, outer in ((0, edge0, src0, out0), (1, edge1, src1, out1)):
                up = up_at(facts_ref, i)
                for z, src in ((1 + up * (Z - 3), inner), (up * (Z - 1), outer)):
                    lam = part[z] if src is inner else edge[...]
                    lam1[z] = lam
                    v = [v0[0, d, z] for d in range(3)]
                    diffs = upwind(tmpl[z + 1], tmpl[z + 2], tmpl[z + 3], v)
                    for d in range(3):
                        src[d] = (-MATCH * dt) * lam * diffs[d]

        outs = [struct(Z, Y, X)] + [struct(3, Y, X)] * 4
        operands = [facts, tmpl, lam1_part, *lam1_edge, flow]
        lam1, *inner_outer = call(
            sources,
            outs,
            [SMEM] + [whole(x) for x in operands[1:5]] + [flow_spec[0]],
            [whole(x) for x in outs],
            operands,
            "sources",
            weight=SOURCES,
        )
        inner0, outer0 = inner_outer[:2], inner_outer[2:]

        far0 = [swap(inner0[0], 0), None]
        held, near1[0], *lam1_far = after((inner1[1], outer1[1]), near1[0], *lam1_far)
        far1[1], near1[1] = [swap(x, 1) for x in held]

        def sweeps(facts_ref, s, v, out, u2):
            for z in range(-1, Z + 1):
                beside = plane_sum(s[z])
                if z - 1 in s:
                    beside = beside + s[z - 1]
                if z + 1 in s:
                    beside = beside + s[z + 1]
                u = (s[z] + beside * SEVENTH) * SEVENTH
                if z == -1:
                    u = jnp.where(facts_ref[1] > 0, u, 0.0)
                if z == Z:
                    u = jnp.where(facts_ref[2] > 0, u, 0.0)
                u2[z + 1] = u
            for z in range(Z):
                u = u2[z + 1]
                beside = plane_sum(u) + u2[z] + u2[z + 2]
                out[0, 0, z] = v[0, 0, z] + (s[z] + beside) * SEVENTH

        class Planes:
            def __init__(self, ref, low, high):
                self.ref, self.low, self.high = ref, low, high

            def __contains__(self, z):
                return self.low <= z <= self.high

            def __getitem__(self, z):
                return self.ref[z - self.low]

        part = pl.BlockSpec((1, Y, X), lambda d: (d, 0, 0))
        flow_part = [
            pl.BlockSpec((1, 1, Z, Y, X), lambda d, t=t: (t, d, 0, 0, 0)) for t in range(steps)
        ]
        u2_scratch = pltpu.VMEM((Z + 2, Y, X), jnp.float32)

        def last(facts_ref, tmpl, lam1, beyond0, beyond1, v0_far, v0, lam0, src, lam):
            for z in range(Z):
                lam[z + 1] = lam1[z]
            for i, beyond in ((0, beyond0), (1, beyond1)):
                lam[up_at(facts_ref, i) * (Z + 1)] = beyond[...]

            def flow_at(z, d):
                return v0[0, d, z] if 0 <= z < Z else v0_far[0 if z < 0 else 1, d]

            for j, z in enumerate((-1, Z)):
                v = [flow_at(z, d) for d in range(3)]
                diffs = upwind(tmpl[z + 1], tmpl[z + 2], tmpl[z + 3], v)
                for d in range(3):
                    src[j, d] = (-MATCH * dt) * lam[z + 1] * diffs[d]
            for z in range(Z):
                above = jnp.maximum(flow_at(z + 1, 0), 0.0) * lam[z + 2]
                below = jnp.minimum(flow_at(z - 1, 0), 0.0) * lam[z]
                v = [flow_at(z, d) for d in range(3)]
                lam0[z] = retreat(lam[z + 1], v, above, below, dt)

        outs = [struct(Z, Y, X), struct(2, 3, Y, X)]
        operands = [facts, tmpl, lam1, *lam1_far, v0_far, flow]
        lam0, near0 = call(
            last,
            outs,
            [SMEM] + [whole(x) for x in operands[1:6]] + [flow_spec[0]],
            [whole(x) for x in outs],
            operands,
            "last",
            weight=LAST,
            scratch=[pltpu.VMEM((Z + 2, Y, X), jnp.float32)],
        )

        held, lam0 = after(inner0[1], lam0)
        far0[1] = swap(held, 1)

        def share(k):
            start = lax.rem(group + k, subj) * rows
            return lax.dynamic_slice_in_dim(lam0, start, rows, axis=1)

        template_grad = share(0)
        for k in range(1, subj):
            template_grad = template_grad + turn(share(k), k)

        def smooth_0(facts_ref, in0, in1, out0, out1, near, v, out, rim, u2, s):
            for i, inner, outer in ((0, in0, out0), (1, in1, out1)):
                up = up_at(facts_ref, i)
                s[2 + up * (Z - 3)] = inner[0]
                s[1 + up * (Z - 1)] = outer[0]
            s[0] = near[0, 0]
            s[Z + 1] = near[1, 0]
            sweeps(facts_ref, Planes(s, -1, Z), v, out, u2)
            for i in SIDES:
                rim[i, 0] = out[0, 0, up_at(facts_ref, i) * (Z - 1)]

        both = pl.BlockSpec((2, 1, Y, X), lambda d: (0, d, 0, 0))
        gradient, rim = call(
            smooth_0,
            [struct(*flow.shape), struct(2, 3, Y, X)],
            [SMEM] + [part] * 4 + [both, flow_part[0]],
            [flow_part[0], both],
            [facts, *inner0, *outer0, near0, flow],
            "smooth_0",
            weight=SMOOTH,
            grid=(3,),
            scratch=[u2_scratch, pltpu.VMEM((Z + 2, Y, X), jnp.float32)],
        )

        def smooth_1(facts_ref, in0, in1, out0, out1, near0, near1, far0, far1, _, v, out, u2, s):
            for i, inner, outer, near, far in ((0, in0, out0, near0, far0), (1, in1, out1, near1, far1)):
                up = up_at(facts_ref, i)
                s[3 + up * (Z - 3)] = inner[0]
                s[2 + up * (Z - 1)] = outer[0]
                s[1 + up * (Z + 1)] = near[0]
                s[up * (Z + 3)] = far[0]
            sweeps(facts_ref, Planes(s, -2, Z + 1), v, out, u2)

        gradient = call(
            smooth_1,
            struct(*flow.shape),
            [SMEM] + [part] * 8 + [pl.BlockSpec(memory_space=pl.ANY), flow_part[1]],
            flow_part[1],
            [facts, *inner1, *outer1, *near1, *far1, gradient, flow],
            "smooth_1",
            weight=SMOOTH,
            grid=(3,),
            aliases={9: 0},
            scratch=[u2_scratch, pltpu.VMEM((Z + 4, Y, X), jnp.float32)],
        )

        def add_far(facts_ref, far_0, far_1, rim, _, out):
            def add(i, far):
                for d in range(3):
                    out[0, d, 0] = rim[i, d] + far[d] * SEVENTH**3

            pl.when(pl.program_id(0) == 0)(lambda: add(0, far_0))
            pl.when(pl.program_id(0) == 1)(lambda: add(1, far_1))

        def boundary(i, facts_ref):
            up = jnp.where(i == 0, facts_ref[3], 1 - facts_ref[3])
            return (0, 0, up * (Z - 1), 0, 0)

        gradient = call(
            add_far,
            struct(*flow.shape),
            [whole(x) for x in (*far0, rim)] + [pl.BlockSpec(memory_space=pl.ANY)],
            pl.BlockSpec((1, 3, 1, Y, X), boundary),
            [facts, *far0, rim, gradient],
            "add_far",
            grid=(2,),
            aliases={4: 0},
            prefetch=1,
        )
        return gradient[None], template_grad

    return body


def solution(mesh):
    sizes = dict(mesh.shape)
    return jax.shard_map(
        make_body(sizes["subj"], sizes["slab"]),
        mesh=mesh,
        in_specs=(
            P("slab", "subj", None),
            P("subj", "slab", None, None),
            P("subj", None, None, "slab", None, None),
        ),
        out_specs=(P("subj", None, None, "slab", None, None), P("slab", "subj", None)),
        check_vma=False,
    )
```

```python
import jax
import jax.numpy as jnp
from jax import lax
from jax.experimental import pallas as pl
from jax.experimental.pallas import tpu as pltpu
from jax.sharding import PartitionSpec as P

MATCH = 5.0
SEVENTH = 1.0 / 7.0
MIB = 1 << 20
FORWARD, MIDDLE, BACK, LAST, SMOOTH = 0, 0, 1000, 2000, 1000


def col_prev(f):
    x = lax.broadcasted_iota(jnp.int32, f.shape, 1)
    return jnp.where(x == 0, 0.0, pltpu.roll(f, 1, 1))


def col_next(f):
    n = f.shape[1]
    x = lax.broadcasted_iota(jnp.int32, f.shape, 1)
    return jnp.where(x == n - 1, 0.0, pltpu.roll(f, n - 1, 1))


def row_prev(f):
    y = lax.broadcasted_iota(jnp.int32, f.shape, 0)
    return jnp.where(y == 0, 0.0, pltpu.roll(f, 1, 0))


def row_next(f):
    n = f.shape[0]
    y = lax.broadcasted_iota(jnp.int32, f.shape, 0)
    return jnp.where(y == n - 1, 0.0, pltpu.roll(f, n - 1, 0))


def upwind(below, f, above, v):
    return [
        jnp.where(v[0] >= 0.0, f - below, above - f),
        jnp.where(v[1] >= 0.0, f - row_prev(f), row_next(f) - f),
        jnp.where(v[2] >= 0.0, f - col_prev(f), col_next(f) - f),
    ]


def advance(f, diffs, v, dt):
    return f - dt * (v[0] * diffs[0] + v[1] * diffs[1] + v[2] * diffs[2])


def retreat(lam, v, pos_above, neg_below, dt):
    total = (jnp.abs(v[0]) + jnp.abs(v[1]) + jnp.abs(v[2])) * lam
    total = total - row_next(jnp.maximum(v[1], 0.0) * lam)
    total = total + row_prev(jnp.minimum(v[1], 0.0) * lam)
    total = total - col_next(jnp.maximum(v[2], 0.0) * lam)
    total = total + col_prev(jnp.minimum(v[2], 0.0) * lam)
    if pos_above is not None:
        total = total - pos_above
    if neg_below is not None:
        total = total + neg_below
    return lam - dt * total


def plane_sum(f):
    return row_prev(f) + row_next(f) + col_prev(f) + col_next(f)


def call(kernel, out_shape, in_specs, out_specs, operands, name, weight=0, grid=(1,), aliases=None, scratch=(), prefetch=0):
    return pl.pallas_call(
        kernel,
        out_shape=out_shape,
        grid_spec=pltpu.PrefetchScalarGridSpec(
            num_scalar_prefetch=prefetch,
            grid=grid,
            in_specs=in_specs,
            out_specs=out_specs,
            scratch_shapes=list(scratch),
        ),
        input_output_aliases=aliases or {},
        compiler_params=pltpu.CompilerParams(vmem_limit_bytes=48 * MIB),
        cost_estimate=pl.CostEstimate(
            flops=1024 + weight * 10000000, bytes_accessed=1024, transcendentals=0
        ),
        name=name,
    )(*operands)


def whole(x):
    zeros = (0,) * x.ndim
    return pl.BlockSpec(x.shape, lambda *_: zeros)


def struct(*shape):
    return jax.ShapeDtypeStruct(shape, jnp.float32)


SMEM = pl.BlockSpec(memory_space=pltpu.SMEM)
SIDES = (0, 1)


def make_body(subj, slabs):
    pairs = []
    for first in SIDES:
        lower = [(i, i + 1) for i in range(first, slabs - 1, 2)]
        pairs.append(lower + [(j, i) for i, j in lower])

    def swap(x, side):
        return lax.ppermute(x, "slab", pairs[side])

    def turn(x, k):
        return lax.ppermute(x, "subj", [(i, (i + k) % subj) for i in range(subj)])

    def after(x, *others):
        return lax.optimization_barrier((x, *others))

    def body(template, subject, velocity):
        flow = velocity[0]
        target = subject[0]
        steps, _, Z, Y, X = flow.shape
        assert Z == 4 and steps == 2
        rows = template.shape[1]
        dt = 1.0 / steps
        place = lax.axis_index("slab")
        group = lax.axis_index("subj")
        even = 1 - place % 2
        facts = jnp.stack([group, place > 0, place < slabs - 1, even]).astype(jnp.int32)
        ups = (even, 1 - even)
        flow_spec = [
            pl.BlockSpec((1, 3, Z, Y, X), lambda *_, t=t: (t, 0, 0, 0, 0)) for t in range(steps)
        ]

        def up_at(facts_ref, i):
            return facts_ref[3] if i == 0 else 1 - facts_ref[3]

        tmpl_far = [
            swap(lax.dynamic_slice_in_dim(template, up * (Z - 2), 2, 0), i)
            for i, up in enumerate(ups)
        ]
        flow0_edge = [
            lax.dynamic_slice(velocity, (0, 0, 0, up * (Z - 1), 0, 0), (1, 1, 3, 1, Y, X))[0, 0, :, 0]
            for up in ups
        ]
        flow0_far = [swap(flow0_edge[i], i) for i in SIDES]
        own_parts = [template] + [turn(template, k) for k in range(1, subj)]
        tmpl_far[1], tmpl_far[0], _, _ = after(*tmpl_far[::-1], *flow0_edge)
        edge = jnp.concatenate(tmpl_far[::-1], axis=0)
        edge_parts = [edge] + [turn(edge, k) for k in range(1, subj)]

        def forward(*refs):
            facts_ref, refs = refs[0], refs[1:]
            owns, edges = refs[:subj], refs[subj : 2 * subj]
            v0, v1, aim = refs[2 * subj : 2 * subj + 3]
            tmpl, img1, lam2, *srcs = refs[2 * subj + 3 :]
            for k in range(subj):
                start = pl.multiple_of(lax.rem(facts_ref[0] + subj - k, subj) * rows, rows)
                at = pl.ds(start, rows)
                tmpl[2 : Z + 2, at, :] = owns[k][...]
                for i in SIDES:
                    up = up_at(facts_ref, i)
                    for j in range(2):
                        tmpl[up * (Z + 2) + j, at, :] = edges[k][2 * (1 - i) + j]
            for z in range(Z):
                v = [v0[0, d, z] for d in range(3)]
                f = tmpl[z + 2]
                img1[z] = advance(f, upwind(tmpl[z + 1], f, tmpl[z + 3], v), v, dt)
            for i in SIDES:
                z = 1 + up_at(facts_ref, i) * (Z - 3)
                v = [v1[0, d, z] for d in range(3)]
                f = img1[z]
                diffs = upwind(img1[z - 1], f, img1[z + 1], v)
                lam = advance(f, diffs, v, dt) - aim[z]
                lam2[i] = lam
                for d in range(3):
                    srcs[i][d] = (-MATCH * dt) * lam * diffs[d]

        outs = [struct(Z + 4, Y, X), struct(Z, Y, X), struct(2, Y, X)] + [struct(3, Y, X)] * 2
        operands = [facts] + own_parts + edge_parts + [flow, flow, target]
        tmpl, img1, lam2_in, *inner1 = call(
            forward,
            outs,
            [SMEM]
            + [whole(x) for x in own_parts + edge_parts]
            + [flow_spec[0], flow_spec[1], whole(target)],
            [whole(x) for x in outs],
            operands,
            "forward",
            weight=FORWARD,
        )
        far1 = [swap(inner1[0], 0), None]

        def middle(facts_ref, tmpl, img1, halo0, halo1, v1, aim, src0, src1, lam2, v0_far):
            for i, halo, src in ((0, halo0, src0), (1, halo1, src1)):
                up = up_at(facts_ref, i)
                at = 1 + up * (Z + 1)
                v = [halo[d] for d in range(3)]
                for d in range(3):
                    v0_far[up, d] = v[d]
                f = tmpl[at]
                outside = advance(f, upwind(tmpl[at - 1], f, tmpl[at + 1], v), v, dt)
                z = up * (Z - 1)
                inside = img1[z + 1 - 2 * up]
                below = jnp.where(up == 1, inside, outside)
                above = jnp.where(up == 1, outside, inside)
                v = [v1[0, d, z] for d in range(3)]
                f = img1[z]
                diffs = upwind(below, f, above, v)
                lam = advance(f, diffs, v, dt) - aim[z]
                for d in range(3):
                    src[d] = (-MATCH * dt) * lam * diffs[d]
                lam2[i] = lam

        outs = [struct(3, Y, X)] * 2 + [struct(2, Y, X), struct(2, 3, Y, X)]
        operands = [facts, tmpl, img1, *flow0_far, flow, target]
        *outer1, lam2_out, v0_far = call(
            middle,
            outs,
            [SMEM] + [whole(x) for x in operands[1:5]] + [flow_spec[1], whole(target)],
            [whole(x) for x in outs],
            operands,
            "middle",
            weight=MIDDLE,
        )
        def back(facts_ref, lam2_in, lam2_out, v1, lam1, word0, word1, lam2):
            for i in SIDES:
                up = up_at(facts_ref, i)
                lam2[1 + up * (Z - 3)] = lam2_in[i]
                lam2[up * (Z - 1)] = lam2_out[i]
            for z in range(Z):
                v = [v1[0, d, z] for d in range(3)]
                above = jnp.maximum(v1[0, 0, z + 1], 0.0) * lam2[z + 1] if z < Z - 1 else None
                below = jnp.minimum(v1[0, 0, z - 1], 0.0) * lam2[z - 1] if z > 0 else None
                lam1[z] = retreat(lam2[z], v, above, below, dt)
            for i, word in ((0, word0), (1, word1)):
                up = up_at(facts_ref, i)
                z = up * (Z - 1)
                v = v1[0, 0, z]
                word[0] = jnp.where(up == 1, jnp.minimum(v, 0.0), jnp.maximum(v, 0.0)) * lam2[z]
                word[1] = lam1[z]

        outs = [struct(Z, Y, X)] + [struct(2, Y, X)] * 2
        operands = [facts, lam2_in, lam2_out, flow]
        lam1_part, *words = call(
            back,
            outs,
            [SMEM] + [whole(x) for x in operands[1:3]] + [flow_spec[1]],
            [whole(x) for x in outs],
            operands,
            "back",
            weight=BACK,
            scratch=[pltpu.VMEM((Z, Y, X), jnp.float32)],
        )
        words_far = [swap(words[i], i) for i in SIDES]
        near1 = [swap(after(outer1[0], *words)[0], 0), None]

        held, far1[0], *words_far = after((inner1[1], outer1[1]), far1[0], *words_far)
        far1[1], near1[1] = [swap(x, 1) for x in held]

        def last(facts_ref, tmpl, part, own0, own1, far0, far1, v0_far, v0, lam0, src0, src1, out0, out1, near, lam):
            for z in range(1, Z - 1):
                lam[z + 1] = part[z]
            for i, own, far in ((0, own0, far0), (1, own1, far1)):
                up = up_at(facts_ref, i)
                toward = dt * (2 * up - 1).astype(jnp.float32)
                inside = jnp.where(up == 1, facts_ref[2], facts_ref[1]) > 0
                lam[1 + up * (Z - 1)] = own[1] + toward * far[0]
                lam[up * (Z + 1)] = jnp.where(inside, far[1] - toward * own[0], 0.0)

            def flow_at(z, d):
                return v0[0, d, z] if 0 <= z < Z else v0_far[0 if z < 0 else 1, d]

            def source(z, v, src, *at):
                diffs = upwind(tmpl[z + 1], tmpl[z + 2], tmpl[z + 3], v)
                for d in range(3):
                    src[(*at, d)] = (-MATCH * dt) * lam[z + 1] * diffs[d]

            for i, inner, outer in ((0, src0, out0), (1, src1, out1)):
                up = up_at(facts_ref, i)
                for z, src in ((1 + up * (Z - 3), inner), (up * (Z - 1), outer)):
                    source(z, [v0[0, d, z] for d in range(3)], src)
            for j, z in enumerate((-1, Z)):
                source(z, [flow_at(z, d) for d in range(3)], near, j)
            for z in range(Z):
                above = jnp.maximum(flow_at(z + 1, 0), 0.0) * lam[z + 2]
                below = jnp.minimum(flow_at(z - 1, 0), 0.0) * lam[z]
                v = [flow_at(z, d) for d in range(3)]
                lam0[z] = retreat(lam[z + 1], v, above, below, dt)

        outs = [struct(Z, Y, X)] + [struct(3, Y, X)] * 4 + [struct(2, 3, Y, X)]
        operands = [facts, tmpl, lam1_part, *words, *words_far, v0_far, flow]
        lam0, *inner_outer, near0 = call(
            last,
            outs,
            [SMEM] + [whole(x) for x in operands[1:8]] + [flow_spec[0]],
            [whole(x) for x in outs],
            operands,
            "last",
            weight=LAST,
            scratch=[pltpu.VMEM((Z + 2, Y, X), jnp.float32)],
        )
        inner0, outer0 = inner_outer[:2], inner_outer[2:]
        far0 = [swap(inner0[i], i) for i in SIDES]

        def sweeps(facts_ref, s, v, out, u2):
            for z in range(-1, Z + 1):
                beside = plane_sum(s[z])
                if z - 1 in s:
                    beside = beside + s[z - 1]
                if z + 1 in s:
                    beside = beside + s[z + 1]
                u = (s[z] + beside * SEVENTH) * SEVENTH
                if z == -1:
                    u = jnp.where(facts_ref[1] > 0, u, 0.0)
                if z == Z:
                    u = jnp.where(facts_ref[2] > 0, u, 0.0)
                u2[z + 1] = u
            for z in range(Z):
                u = u2[z + 1]
                beside = plane_sum(u) + u2[z] + u2[z + 2]
                out[0, 0, z] = v[0, 0, z] + (s[z] + beside) * SEVENTH

        class Planes:
            def __init__(self, ref, low, high):
                self.ref, self.low, self.high = ref, low, high

            def __contains__(self, z):
                return self.low <= z <= self.high

            def __getitem__(self, z):
                return self.ref[z - self.low]

        part = pl.BlockSpec((1, Y, X), lambda d: (d, 0, 0))
        flow_part = [
            pl.BlockSpec((1, 1, Z, Y, X), lambda d, t=t: (t, d, 0, 0, 0)) for t in range(steps)
        ]
        u2_scratch = pltpu.VMEM((Z + 2, Y, X), jnp.float32)

        def share(k):
            start = lax.rem(group + k, subj) * rows
            return lax.dynamic_slice_in_dim(lam0, start, rows, axis=1)

        template_grad = share(0)
        for k in range(1, subj):
            template_grad = template_grad + turn(share(k), k)

        def smooth_0(facts_ref, in0, in1, out0, out1, near, v, out, rim, u2, s):
            for i, inner, outer in ((0, in0, out0), (1, in1, out1)):
                up = up_at(facts_ref, i)
                s[2 + up * (Z - 3)] = inner[0]
                s[1 + up * (Z - 1)] = outer[0]
            s[0] = near[0, 0]
            s[Z + 1] = near[1, 0]
            sweeps(facts_ref, Planes(s, -1, Z), v, out, u2)
            for i in SIDES:
                rim[i, 0] = out[0, 0, up_at(facts_ref, i) * (Z - 1)]

        both = pl.BlockSpec((2, 1, Y, X), lambda d: (0, d, 0, 0))
        gradient, rim = call(
            smooth_0,
            [struct(*flow.shape), struct(2, 3, Y, X)],
            [SMEM] + [part] * 4 + [both, flow_part[0]],
            [flow_part[0], both],
            [facts, *inner0, *outer0, near0, flow],
            "smooth_0",
            weight=SMOOTH,
            grid=(3,),
            scratch=[u2_scratch, pltpu.VMEM((Z + 2, Y, X), jnp.float32)],
        )

        def smooth_1(facts_ref, in0, in1, out0, out1, near0, near1, far0, far1, _, v, out, u2, s):
            for i, inner, outer, near, far in ((0, in0, out0, near0, far0), (1, in1, out1, near1, far1)):
                up = up_at(facts_ref, i)
                s[3 + up * (Z - 3)] = inner[0]
                s[2 + up * (Z - 1)] = outer[0]
                s[1 + up * (Z + 1)] = near[0]
                s[up * (Z + 3)] = far[0]
            sweeps(facts_ref, Planes(s, -2, Z + 1), v, out, u2)

        gradient = call(
            smooth_1,
            struct(*flow.shape),
            [SMEM] + [part] * 8 + [pl.BlockSpec(memory_space=pl.ANY), flow_part[1]],
            flow_part[1],
            [facts, *inner1, *outer1, *near1, *far1, gradient, flow],
            "smooth_1",
            weight=SMOOTH,
            grid=(3,),
            aliases={9: 0},
            scratch=[u2_scratch, pltpu.VMEM((Z + 4, Y, X), jnp.float32)],
        )

        def add_far(facts_ref, far_0, far_1, rim, _, out, held, done):
            copies = []
            for i, far in ((0, far_0), (1, far_1)):
                z = up_at(facts_ref, i) * (Z - 1)
                for d in range(3):
                    held[i, d] = rim[i, d] + far[d] * SEVENTH**3
                    copies.append(pltpu.make_async_copy(held.at[i, d], out.at[0, d, z], done.at[i, d]))
                    copies[-1].start()
            for copy in copies:
                copy.wait()

        gradient = call(
            add_far,
            struct(*flow.shape),
            [SMEM] + [whole(x) for x in (*far0, rim)] + [pl.BlockSpec(memory_space=pl.ANY)],
            pl.BlockSpec(memory_space=pl.ANY),
            [facts, *far0, rim, gradient],
            "add_far",
            aliases={4: 0},
            scratch=[pltpu.VMEM((2, 3, Y, X), jnp.float32), pltpu.SemaphoreType.DMA((2, 3))],
        )
        return gradient[None], template_grad

    return body


def solution(mesh):
    sizes = dict(mesh.shape)
    return jax.shard_map(
        make_body(sizes["subj"], sizes["slab"]),
        mesh=mesh,
        in_specs=(
            P("slab", "subj", None),
            P("subj", "slab", None, None),
            P("subj", None, None, "slab", None, None),
        ),
        out_specs=(P("subj", None, None, "slab", None, None), P("slab", "subj", None)),
        check_vma=False,
    )
```

```python
import jax
import jax.numpy as jnp
from jax import lax
from jax.experimental import pallas as pl
from jax.experimental.pallas import tpu as pltpu
from jax.sharding import PartitionSpec as P

MATCH = 5.0
SEVENTH = 1.0 / 7.0
MIB = 1 << 20
FORWARD, MIDDLE, BACK, LAST, SMOOTH = 0, 0, 1000, 2000, 1000


def col_prev(f):
    x = lax.broadcasted_iota(jnp.int32, f.shape, 1)
    return jnp.where(x == 0, 0.0, pltpu.roll(f, 1, 1))


def col_next(f):
    n = f.shape[1]
    x = lax.broadcasted_iota(jnp.int32, f.shape, 1)
    return jnp.where(x == n - 1, 0.0, pltpu.roll(f, n - 1, 1))


def row_prev(f):
    y = lax.broadcasted_iota(jnp.int32, f.shape, 0)
    return jnp.where(y == 0, 0.0, pltpu.roll(f, 1, 0))


def row_next(f):
    n = f.shape[0]
    y = lax.broadcasted_iota(jnp.int32, f.shape, 0)
    return jnp.where(y == n - 1, 0.0, pltpu.roll(f, n - 1, 0))


def upwind(below, f, above, v):
    return [
        jnp.where(v[0] >= 0.0, f - below, above - f),
        jnp.where(v[1] >= 0.0, f - row_prev(f), row_next(f) - f),
        jnp.where(v[2] >= 0.0, f - col_prev(f), col_next(f) - f),
    ]


def advance(f, diffs, v, dt):
    return f - dt * (v[0] * diffs[0] + v[1] * diffs[1] + v[2] * diffs[2])


def retreat(lam, v, pos_above, neg_below, dt):
    total = (jnp.abs(v[0]) + jnp.abs(v[1]) + jnp.abs(v[2])) * lam
    total = total - row_next(jnp.maximum(v[1], 0.0) * lam)
    total = total + row_prev(jnp.minimum(v[1], 0.0) * lam)
    total = total - col_next(jnp.maximum(v[2], 0.0) * lam)
    total = total + col_prev(jnp.minimum(v[2], 0.0) * lam)
    if pos_above is not None:
        total = total - pos_above
    if neg_below is not None:
        total = total + neg_below
    return lam - dt * total


def plane_sum(f):
    return row_prev(f) + row_next(f) + col_prev(f) + col_next(f)


def call(kernel, out_shape, in_specs, out_specs, operands, name, weight=0, grid=(), aliases=None, scratch=()):
    return pl.pallas_call(
        kernel,
        out_shape=out_shape,
        grid=grid,
        in_specs=in_specs,
        out_specs=out_specs,
        scratch_shapes=list(scratch),
        input_output_aliases=aliases or {},
        compiler_params=pltpu.CompilerParams(vmem_limit_bytes=48 * MIB),
        cost_estimate=pl.CostEstimate(
            flops=1024 + weight * 10000000, bytes_accessed=1024, transcendentals=0
        ),
        name=name,
    )(*operands)


def whole(x):
    zeros = (0,) * x.ndim
    return pl.BlockSpec(x.shape, lambda *_: zeros)


def struct(*shape):
    return jax.ShapeDtypeStruct(shape, jnp.float32)


SMEM = pl.BlockSpec(memory_space=pltpu.SMEM)
VMEM = pl.BlockSpec(memory_space=pltpu.VMEM)
SIDES = (0, 1)


def make_body(subj, slabs):
    pairs = []
    for first in SIDES:
        lower = [(i, i + 1) for i in range(first, slabs - 1, 2)]
        pairs.append(lower + [(j, i) for i, j in lower])

    def swap(x, side):
        return lax.ppermute(x, "slab", pairs[side])

    def turn(x, k):
        return lax.ppermute(x, "subj", [(i, (i + k) % subj) for i in range(subj)])

    def after(x, *others):
        return lax.optimization_barrier((x, *others))

    def body(template, subject, velocity):
        flow = velocity[0]
        target = subject[0]
        steps, _, Z, Y, X = flow.shape
        assert Z == 4 and steps == 2
        rows = template.shape[1]
        dt = 1.0 / steps
        place = lax.axis_index("slab")
        group = lax.axis_index("subj")
        even = 1 - place % 2
        facts = jnp.stack([group, place > 0, place < slabs - 1, even]).astype(jnp.int32)
        ups = (even, 1 - even)
        flow_spec = [
            pl.BlockSpec((1, 3, Z, Y, X), lambda *_, t=t: (t, 0, 0, 0, 0)) for t in range(steps)
        ]

        def up_at(facts_ref, i):
            return facts_ref[3] if i == 0 else 1 - facts_ref[3]

        tmpl_far = [
            swap(lax.dynamic_slice_in_dim(template, up * (Z - 2), 2, 0), i)
            for i, up in enumerate(ups)
        ]
        flow0_edge = [
            lax.dynamic_slice(velocity, (0, 0, 0, up * (Z - 1), 0, 0), (1, 1, 3, 1, Y, X))[0, 0, :, 0]
            for up in ups
        ]
        flow0_far = [swap(flow0_edge[i], i) for i in SIDES]
        own_parts = [template] + [turn(template, k) for k in range(1, subj)]
        tmpl_far[1], tmpl_far[0], _, _ = after(*tmpl_far[::-1], *flow0_edge)
        edge = jnp.concatenate(tmpl_far[::-1], axis=0)
        edge_parts = [edge] + [turn(edge, k) for k in range(1, subj)]

        def forward(*refs):
            facts_ref, refs = refs[0], refs[1:]
            owns, edges = refs[:subj], refs[subj : 2 * subj]
            v0, v1, aim = refs[2 * subj : 2 * subj + 3]
            tmpl, img1, lam2, *srcs = refs[2 * subj + 3 :]
            for k in range(subj):
                start = pl.multiple_of(lax.rem(facts_ref[0] + subj - k, subj) * rows, rows)
                at = pl.ds(start, rows)
                tmpl[2 : Z + 2, at, :] = owns[k][...]
                for i in SIDES:
                    up = up_at(facts_ref, i)
                    for j in range(2):
                        tmpl[up * (Z + 2) + j, at, :] = edges[k][2 * (1 - i) + j]
            for z in range(Z):
                v = [v0[0, d, z] for d in range(3)]
                f = tmpl[z + 2]
                img1[z] = advance(f, upwind(tmpl[z + 1], f, tmpl[z + 3], v), v, dt)
            for i in SIDES:
                z = 1 + up_at(facts_ref, i) * (Z - 3)
                v = [v1[0, d, z] for d in range(3)]
                f = img1[z]
                diffs = upwind(img1[z - 1], f, img1[z + 1], v)
                lam = advance(f, diffs, v, dt) - aim[z]
                lam2[i] = lam
                for d in range(3):
                    srcs[i][d] = (-MATCH * dt) * lam * diffs[d]

        outs = [struct(Z + 4, Y, X), struct(Z, Y, X), struct(2, Y, X)] + [struct(3, Y, X)] * 2
        operands = [facts] + own_parts + edge_parts + [flow, flow, target]
        tmpl, img1, lam2_in, *inner1 = call(
            forward,
            outs,
            [SMEM]
            + [whole(x) for x in own_parts + edge_parts]
            + [flow_spec[0], flow_spec[1], whole(target)],
            [whole(x) for x in outs],
            operands,
            "forward",
            grid=(1,),
            weight=FORWARD,
        )
        far1 = [swap(inner1[0], 0), None]

        def middle(facts_ref, tmpl, img1, halo0, halo1, v1, aim, src0, src1, lam2, v0_far):
            for i, halo, src in ((0, halo0, src0), (1, halo1, src1)):
                up = up_at(facts_ref, i)
                at = 1 + up * (Z + 1)
                v = [halo[d] for d in range(3)]
                for d in range(3):
                    v0_far[up, d] = v[d]
                f = tmpl[at]
                outside = advance(f, upwind(tmpl[at - 1], f, tmpl[at + 1], v), v, dt)
                z = up * (Z - 1)
                inside = img1[z + 1 - 2 * up]
                below = jnp.where(up == 1, inside, outside)
                above = jnp.where(up == 1, outside, inside)
                v = [v1[0, d, z] for d in range(3)]
                f = img1[z]
                diffs = upwind(below, f, above, v)
                lam = advance(f, diffs, v, dt) - aim[z]
                for d in range(3):
                    src[d] = (-MATCH * dt) * lam * diffs[d]
                lam2[i] = lam

        outs = [struct(3, Y, X)] * 2 + [struct(2, Y, X), struct(2, 3, Y, X)]
        operands = [facts, tmpl, img1, *flow0_far, flow, target]
        *outer1, lam2_out, v0_far = call(
            middle,
            outs,
            [SMEM] + [whole(x) for x in operands[1:5]] + [flow_spec[1], whole(target)],
            [whole(x) for x in outs],
            operands,
            "middle",
            grid=(1,),
            weight=MIDDLE,
        )
        def back(facts_ref, lam2_in, lam2_out, v1, lam1, word0, word1, lam2):
            for i in SIDES:
                up = up_at(facts_ref, i)
                lam2[1 + up * (Z - 3)] = lam2_in[i]
                lam2[up * (Z - 1)] = lam2_out[i]
            for z in range(Z):
                v = [v1[0, d, z] for d in range(3)]
                above = jnp.maximum(v1[0, 0, z + 1], 0.0) * lam2[z + 1] if z < Z - 1 else None
                below = jnp.minimum(v1[0, 0, z - 1], 0.0) * lam2[z - 1] if z > 0 else None
                lam1[z] = retreat(lam2[z], v, above, below, dt)
            for i, word in ((0, word0), (1, word1)):
                up = up_at(facts_ref, i)
                z = up * (Z - 1)
                v = v1[0, 0, z]
                word[0] = jnp.where(up == 1, jnp.minimum(v, 0.0), jnp.maximum(v, 0.0)) * lam2[z]
                word[1] = lam1[z]

        outs = [struct(Z, Y, X)] + [struct(2, Y, X)] * 2
        operands = [facts, lam2_in, lam2_out, flow]
        lam1_part, *words = call(
            back,
            outs,
            [SMEM] + [whole(x) for x in operands[1:3]] + [flow_spec[1]],
            [whole(x) for x in outs],
            operands,
            "back",
            grid=(1,),
            weight=BACK,
            scratch=[pltpu.VMEM((Z, Y, X), jnp.float32)],
        )
        words_far = [swap(words[i], i) for i in SIDES]
        near1 = [swap(after(outer1[0], *words)[0], 0), None]

        held, far1[0], *words_far = after((inner1[1], outer1[1]), far1[0], *words_far)
        far1[1], near1[1] = [swap(x, 1) for x in held]

        def last(facts_ref, tmpl, part, own0, own1, far0, far1, v0_far, v0, lam0, src0, src1, out0, out1, near, lam):
            for z in range(1, Z - 1):
                lam[z + 1] = part[z]
            for i, own, far in ((0, own0, far0), (1, own1, far1)):
                up = up_at(facts_ref, i)
                toward = dt * (2 * up - 1).astype(jnp.float32)
                inside = jnp.where(up == 1, facts_ref[2], facts_ref[1]) > 0
                lam[1 + up * (Z - 1)] = own[1] + toward * far[0]
                lam[up * (Z + 1)] = jnp.where(inside, far[1] - toward * own[0], 0.0)

            def flow_at(z, d):
                return v0[0, d, z] if 0 <= z < Z else v0_far[0 if z < 0 else 1, d]

            def source(z, v, src, *at):
                diffs = upwind(tmpl[z + 1], tmpl[z + 2], tmpl[z + 3], v)
                for d in range(3):
                    src[(*at, d)] = (-MATCH * dt) * lam[z + 1] * diffs[d]

            for i, inner, outer in ((0, src0, out0), (1, src1, out1)):
                up = up_at(facts_ref, i)
                for z, src in ((1 + up * (Z - 3), inner), (up * (Z - 1), outer)):
                    source(z, [v0[0, d, z] for d in range(3)], src)
            for j, z in enumerate((-1, Z)):
                source(z, [flow_at(z, d) for d in range(3)], near, j)
            for z in range(Z):
                above = jnp.maximum(flow_at(z + 1, 0), 0.0) * lam[z + 2]
                below = jnp.minimum(flow_at(z - 1, 0), 0.0) * lam[z]
                v = [flow_at(z, d) for d in range(3)]
                lam0[z] = retreat(lam[z + 1], v, above, below, dt)

        outs = [struct(Z, Y, X)] + [struct(3, Y, X)] * 4 + [struct(2, 3, Y, X)]
        operands = [facts, tmpl, lam1_part, *words, *words_far, v0_far, flow]
        lam0, *inner_outer, near0 = call(
            last,
            outs,
            [SMEM] + [whole(x) for x in operands[1:8]] + [flow_spec[0]],
            [whole(x) for x in outs],
            operands,
            "last",
            grid=(1,),
            weight=LAST,
            scratch=[pltpu.VMEM((Z + 2, Y, X), jnp.float32)],
        )
        inner0, outer0 = inner_outer[:2], inner_outer[2:]
        far0 = [swap(inner0[i], i) for i in SIDES]

        def sweeps(facts_ref, s, v, out, u2):
            for z in range(-1, Z + 1):
                beside = plane_sum(s[z])
                if z - 1 in s:
                    beside = beside + s[z - 1]
                if z + 1 in s:
                    beside = beside + s[z + 1]
                u = (s[z] + beside * SEVENTH) * SEVENTH
                if z == -1:
                    u = jnp.where(facts_ref[1] > 0, u, 0.0)
                if z == Z:
                    u = jnp.where(facts_ref[2] > 0, u, 0.0)
                u2[z + 1] = u
            for z in range(Z):
                u = u2[z + 1]
                beside = plane_sum(u) + u2[z] + u2[z + 2]
                out[0, 0, z] = v[0, 0, z] + (s[z] + beside) * SEVENTH

        class Planes:
            def __init__(self, ref, low, high):
                self.ref, self.low, self.high = ref, low, high

            def __contains__(self, z):
                return self.low <= z <= self.high

            def __getitem__(self, z):
                return self.ref[z - self.low]

        part = pl.BlockSpec((1, Y, X), lambda d: (d, 0, 0))
        flow_part = [
            pl.BlockSpec((1, 1, Z, Y, X), lambda d, t=t: (t, d, 0, 0, 0)) for t in range(steps)
        ]
        u2_scratch = pltpu.VMEM((Z + 2, Y, X), jnp.float32)

        def share(k):
            start = lax.rem(group + k, subj) * rows
            return lax.dynamic_slice_in_dim(lam0, start, rows, axis=1)

        template_grad = share(0)
        for k in range(1, subj):
            template_grad = template_grad + turn(share(k), k)

        def smooth_0(facts_ref, in0, in1, out0, out1, near, v, out, rim, u2, s):
            for i, inner, outer in ((0, in0, out0), (1, in1, out1)):
                up = up_at(facts_ref, i)
                s[2 + up * (Z - 3)] = inner[0]
                s[1 + up * (Z - 1)] = outer[0]
            s[0] = near[0, 0]
            s[Z + 1] = near[1, 0]
            sweeps(facts_ref, Planes(s, -1, Z), v, out, u2)
            for i in SIDES:
                rim[i, 0] = out[0, 0, up_at(facts_ref, i) * (Z - 1)]

        both = pl.BlockSpec((2, 1, Y, X), lambda d: (0, d, 0, 0))
        gradient, rim = call(
            smooth_0,
            [struct(*flow.shape), struct(2, 3, Y, X)],
            [SMEM] + [part] * 4 + [both, flow_part[0]],
            [flow_part[0], both],
            [facts, *inner0, *outer0, near0, flow],
            "smooth_0",
            weight=SMOOTH,
            grid=(3,),
            scratch=[u2_scratch, pltpu.VMEM((Z + 2, Y, X), jnp.float32)],
        )

        def smooth_1(facts_ref, in0, in1, out0, out1, near0, near1, far0, far1, _, v, out, u2, s):
            for i, inner, outer, near, far in ((0, in0, out0, near0, far0), (1, in1, out1, near1, far1)):
                up = up_at(facts_ref, i)
                s[3 + up * (Z - 3)] = inner[0]
                s[2 + up * (Z - 1)] = outer[0]
                s[1 + up * (Z + 1)] = near[0]
                s[up * (Z + 3)] = far[0]
            sweeps(facts_ref, Planes(s, -2, Z + 1), v, out, u2)

        gradient = call(
            smooth_1,
            struct(*flow.shape),
            [SMEM] + [part] * 8 + [pl.BlockSpec(memory_space=pl.ANY), flow_part[1]],
            flow_part[1],
            [facts, *inner1, *outer1, *near1, *far1, gradient, flow],
            "smooth_1",
            weight=SMOOTH,
            grid=(3,),
            aliases={9: 0},
            scratch=[u2_scratch, pltpu.VMEM((Z + 4, Y, X), jnp.float32)],
        )

        def add_far(facts_ref, far_0, far_1, rim, _, out, held, done):
            copies = []
            for i, far in ((0, far_0), (1, far_1)):
                z = up_at(facts_ref, i) * (Z - 1)
                for d in range(3):
                    held[i, d] = rim[i, d] + far[d] * SEVENTH**3
                    copies.append(pltpu.make_async_copy(held.at[i, d], out.at[0, d, z], done.at[i, d]))
                    copies[-1].start()
            for copy in copies:
                copy.wait()

        gradient = call(
            add_far,
            struct(*flow.shape),
            [SMEM, VMEM, VMEM, VMEM, pl.BlockSpec(memory_space=pl.ANY)],
            pl.BlockSpec(memory_space=pl.ANY),
            [facts, *far0, rim, gradient],
            "add_far",
            aliases={4: 0},
            scratch=[pltpu.VMEM((2, 3, Y, X), jnp.float32), pltpu.SemaphoreType.DMA((2, 3))],
        )
        return gradient[None], template_grad

    return body


def solution(mesh):
    sizes = dict(mesh.shape)
    return jax.shard_map(
        make_body(sizes["subj"], sizes["slab"]),
        mesh=mesh,
        in_specs=(
            P("slab", "subj", None),
            P("subj", "slab", None, None),
            P("subj", None, None, "slab", None, None),
        ),
        out_specs=(P("subj", None, None, "slab", None, None), P("slab", "subj", None)),
        check_vma=False,
    )
```

```python
import jax
import jax.numpy as jnp
from jax import lax
from jax.experimental import pallas as pl
from jax.experimental.pallas import tpu as pltpu
from jax.sharding import PartitionSpec as P

MATCH = 5.0
SEVENTH = 1.0 / 7.0
MIB = 1 << 20
FORWARD, MIDDLE, BACK, INSIDE, LAST, SMOOTH = 0, 0, 1000, 0, 2000, 1000


def col_prev(f):
    x = lax.broadcasted_iota(jnp.int32, f.shape, 1)
    return jnp.where(x == 0, 0.0, pltpu.roll(f, 1, 1))


def col_next(f):
    n = f.shape[1]
    x = lax.broadcasted_iota(jnp.int32, f.shape, 1)
    return jnp.where(x == n - 1, 0.0, pltpu.roll(f, n - 1, 1))


def row_prev(f):
    y = lax.broadcasted_iota(jnp.int32, f.shape, 0)
    return jnp.where(y == 0, 0.0, pltpu.roll(f, 1, 0))


def row_next(f):
    n = f.shape[0]
    y = lax.broadcasted_iota(jnp.int32, f.shape, 0)
    return jnp.where(y == n - 1, 0.0, pltpu.roll(f, n - 1, 0))


def upwind(below, f, above, v):
    return [
        jnp.where(v[0] >= 0.0, f - below, above - f),
        jnp.where(v[1] >= 0.0, f - row_prev(f), row_next(f) - f),
        jnp.where(v[2] >= 0.0, f - col_prev(f), col_next(f) - f),
    ]


def advance(f, diffs, v, dt):
    return f - dt * (v[0] * diffs[0] + v[1] * diffs[1] + v[2] * diffs[2])


def retreat(lam, v, pos_above, neg_below, dt):
    total = (jnp.abs(v[0]) + jnp.abs(v[1]) + jnp.abs(v[2])) * lam
    total = total - row_next(jnp.maximum(v[1], 0.0) * lam)
    total = total + row_prev(jnp.minimum(v[1], 0.0) * lam)
    total = total - col_next(jnp.maximum(v[2], 0.0) * lam)
    total = total + col_prev(jnp.minimum(v[2], 0.0) * lam)
    if pos_above is not None:
        total = total - pos_above
    if neg_below is not None:
        total = total + neg_below
    return lam - dt * total


def plane_sum(f):
    return row_prev(f) + row_next(f) + col_prev(f) + col_next(f)


def call(kernel, out_shape, in_specs, out_specs, operands, name, weight=0, grid=(1,), aliases=None, scratch=(), prefetch=0):
    return pl.pallas_call(
        kernel,
        out_shape=out_shape,
        grid_spec=pltpu.PrefetchScalarGridSpec(
            num_scalar_prefetch=prefetch,
            grid=grid,
            in_specs=in_specs,
            out_specs=out_specs,
            scratch_shapes=list(scratch),
        ),
        input_output_aliases=aliases or {},
        compiler_params=pltpu.CompilerParams(vmem_limit_bytes=48 * MIB),
        cost_estimate=pl.CostEstimate(
            flops=1024 + weight * 10000000, bytes_accessed=1024, transcendentals=0
        ),
        name=name,
    )(*operands)


def whole(x):
    zeros = (0,) * x.ndim
    return pl.BlockSpec(x.shape, lambda *_: zeros)


def struct(*shape):
    return jax.ShapeDtypeStruct(shape, jnp.float32)


SMEM = pl.BlockSpec(memory_space=pltpu.SMEM)
SIDES = (0, 1)


def make_body(subj, slabs):
    pairs = []
    for first in SIDES:
        lower = [(i, i + 1) for i in range(first, slabs - 1, 2)]
        pairs.append(lower + [(j, i) for i, j in lower])

    def swap(x, side):
        return lax.ppermute(x, "slab", pairs[side])

    def turn(x, k):
        return lax.ppermute(x, "subj", [(i, (i + k) % subj) for i in range(subj)])

    def after(x, *others):
        return lax.optimization_barrier((x, *others))

    def body(template, subject, velocity):
        flow = velocity[0]
        target = subject[0]
        steps, _, Z, Y, X = flow.shape
        assert Z == 4 and steps == 2
        rows = template.shape[1]
        dt = 1.0 / steps
        place = lax.axis_index("slab")
        group = lax.axis_index("subj")
        even = 1 - place % 2
        facts = jnp.stack([group, place > 0, place < slabs - 1, even]).astype(jnp.int32)
        ups = (even, 1 - even)
        flow_spec = [
            pl.BlockSpec((1, 3, Z, Y, X), lambda *_, t=t: (t, 0, 0, 0, 0)) for t in range(steps)
        ]

        def up_at(facts_ref, i):
            return facts_ref[3] if i == 0 else 1 - facts_ref[3]

        tmpl_far = [
            swap(lax.dynamic_slice_in_dim(template, up * (Z - 2), 2, 0), i)
            for i, up in enumerate(ups)
        ]
        flow0_edge = [
            lax.dynamic_slice(velocity, (0, 0, 0, up * (Z - 1), 0, 0), (1, 1, 3, 1, Y, X))[0, 0, :, 0]
            for up in ups
        ]
        flow0_far = [swap(flow0_edge[i], i) for i in SIDES]
        own_parts = [template] + [turn(template, k) for k in range(1, subj)]
        tmpl_far[1], tmpl_far[0], _, _ = after(*tmpl_far[::-1], *flow0_edge)
        edge = jnp.concatenate(tmpl_far[::-1], axis=0)
        edge_parts = [edge] + [turn(edge, k) for k in range(1, subj)]

        def forward(*refs):
            facts_ref, refs = refs[0], refs[1:]
            owns, edges = refs[:subj], refs[subj : 2 * subj]
            v0, v1, aim = refs[2 * subj : 2 * subj + 3]
            tmpl, img1, lam2, *srcs = refs[2 * subj + 3 :]
            for k in range(subj):
                start = pl.multiple_of(lax.rem(facts_ref[0] + subj - k, subj) * rows, rows)
                at = pl.ds(start, rows)
                tmpl[2 : Z + 2, at, :] = owns[k][...]
                for i in SIDES:
                    up = up_at(facts_ref, i)
                    for j in range(2):
                        tmpl[up * (Z + 2) + j, at, :] = edges[k][2 * (1 - i) + j]
            for z in range(Z):
                v = [v0[0, d, z] for d in range(3)]
                f = tmpl[z + 2]
                img1[z] = advance(f, upwind(tmpl[z + 1], f, tmpl[z + 3], v), v, dt)
            for i in SIDES:
                z = 1 + up_at(facts_ref, i) * (Z - 3)
                v = [v1[0, d, z] for d in range(3)]
                f = img1[z]
                diffs = upwind(img1[z - 1], f, img1[z + 1], v)
                lam = advance(f, diffs, v, dt) - aim[z]
                lam2[i] = lam
                for d in range(3):
                    srcs[i][d] = (-MATCH * dt) * lam * diffs[d]

        outs = [struct(Z + 4, Y, X), struct(Z, Y, X), struct(2, Y, X)] + [struct(3, Y, X)] * 2
        operands = [facts] + own_parts + edge_parts + [flow, flow, target]
        tmpl, img1, lam2_in, *inner1 = call(
            forward,
            outs,
            [SMEM]
            + [whole(x) for x in own_parts + edge_parts]
            + [flow_spec[0], flow_spec[1], whole(target)],
            [whole(x) for x in outs],
            operands,
            "forward",
            weight=FORWARD,
        )
        far1 = [swap(inner1[0], 0), None]

        def middle(facts_ref, tmpl, img1, halo0, halo1, v1, aim, src0, src1, lam2, v0_far):
            for i, halo, src in ((0, halo0, src0), (1, halo1, src1)):
                up = up_at(facts_ref, i)
                at = 1 + up * (Z + 1)
                v = [halo[d] for d in range(3)]
                for d in range(3):
                    v0_far[up, d] = v[d]
                f = tmpl[at]
                outside = advance(f, upwind(tmpl[at - 1], f, tmpl[at + 1], v), v, dt)
                z = up * (Z - 1)
                inside = img1[z + 1 - 2 * up]
                below = jnp.where(up == 1, inside, outside)
                above = jnp.where(up == 1, outside, inside)
                v = [v1[0, d, z] for d in range(3)]
                f = img1[z]
                diffs = upwind(below, f, above, v)
                lam = advance(f, diffs, v, dt) - aim[z]
                for d in range(3):
                    src[d] = (-MATCH * dt) * lam * diffs[d]
                lam2[i] = lam

        outs = [struct(3, Y, X)] * 2 + [struct(2, Y, X), struct(2, 3, Y, X)]
        operands = [facts, tmpl, img1, *flow0_far, flow, target]
        *outer1, lam2_out, v0_far = call(
            middle,
            outs,
            [SMEM] + [whole(x) for x in operands[1:5]] + [flow_spec[1], whole(target)],
            [whole(x) for x in outs],
            operands,
            "middle",
            weight=MIDDLE,
        )
        def back(facts_ref, lam2_in, lam2_out, v1, lam1, word0, word1, lam2):
            for i in SIDES:
                up = up_at(facts_ref, i)
                lam2[1 + up * (Z - 3)] = lam2_in[i]
                lam2[up * (Z - 1)] = lam2_out[i]
            for z in range(Z):
                v = [v1[0, d, z] for d in range(3)]
                above = jnp.maximum(v1[0, 0, z + 1], 0.0) * lam2[z + 1] if z < Z - 1 else None
                below = jnp.minimum(v1[0, 0, z - 1], 0.0) * lam2[z - 1] if z > 0 else None
                lam1[z] = retreat(lam2[z], v, above, below, dt)
            for i, word in ((0, word0), (1, word1)):
                up = up_at(facts_ref, i)
                z = up * (Z - 1)
                v = v1[0, 0, z]
                word[0] = jnp.where(up == 1, jnp.minimum(v, 0.0), jnp.maximum(v, 0.0)) * lam2[z]
                word[1] = lam1[z]

        outs = [struct(Z, Y, X)] + [struct(2, Y, X)] * 2
        operands = [facts, lam2_in, lam2_out, flow]
        lam1_part, *words = call(
            back,
            outs,
            [SMEM] + [whole(x) for x in operands[1:3]] + [flow_spec[1]],
            [whole(x) for x in outs],
            operands,
            "back",
            weight=BACK,
            scratch=[pltpu.VMEM((Z, Y, X), jnp.float32)],
        )
        words_far = [swap(words[i], i) for i in SIDES]
        near1 = [swap(outer1[0], 0), None]

        def inside(facts_ref, tmpl, lam1, v0, src0, src1):
            for i, src in ((0, src0), (1, src1)):
                z = 1 + up_at(facts_ref, i) * (Z - 3)
                v = [v0[0, d, z] for d in range(3)]
                diffs = upwind(tmpl[z + 1], tmpl[z + 2], tmpl[z + 3], v)
                for d in range(3):
                    src[d] = (-MATCH * dt) * lam1[z] * diffs[d]

        outs = [struct(3, Y, X)] * 2
        held = after(lam1_part, *words)[0]
        inner0 = call(
            inside,
            outs,
            [SMEM, whole(tmpl), whole(held), flow_spec[0]],
            [whole(x) for x in outs],
            [facts, tmpl, held, flow],
            "inside",
            weight=INSIDE,
        )
        far0 = [swap(inner0[0], 0), None]

        held, far1[0], *words_far = after((inner1[1], outer1[1]), far1[0], *words_far)
        far1[1], near1[1] = [swap(x, 1) for x in held]

        def last(facts_ref, tmpl, part, own0, own1, far0, far1, v0_far, v0, lam0, out0, out1, near, lam):
            for z in range(1, Z - 1):
                lam[z + 1] = part[z]
            for i, own, far in ((0, own0, far0), (1, own1, far1)):
                up = up_at(facts_ref, i)
                toward = dt * (2 * up - 1).astype(jnp.float32)
                inside = jnp.where(up == 1, facts_ref[2], facts_ref[1]) > 0
                lam[1 + up * (Z - 1)] = own[1] + toward * far[0]
                lam[up * (Z + 1)] = jnp.where(inside, far[1] - toward * own[0], 0.0)

            def flow_at(z, d):
                return v0[0, d, z] if 0 <= z < Z else v0_far[0 if z < 0 else 1, d]

            def source(z, v, src, *at):
                diffs = upwind(tmpl[z + 1], tmpl[z + 2], tmpl[z + 3], v)
                for d in range(3):
                    src[(*at, d)] = (-MATCH * dt) * lam[z + 1] * diffs[d]

            for i, outer in ((0, out0), (1, out1)):
                z = up_at(facts_ref, i) * (Z - 1)
                source(z, [v0[0, d, z] for d in range(3)], outer)
            for j, z in enumerate((-1, Z)):
                source(z, [flow_at(z, d) for d in range(3)], near, j)
            for z in range(Z):
                above = jnp.maximum(flow_at(z + 1, 0), 0.0) * lam[z + 2]
                below = jnp.minimum(flow_at(z - 1, 0), 0.0) * lam[z]
                v = [flow_at(z, d) for d in range(3)]
                lam0[z] = retreat(lam[z + 1], v, above, below, dt)

        outs = [struct(Z, Y, X)] + [struct(3, Y, X)] * 2 + [struct(2, 3, Y, X)]
        operands = [facts, tmpl, lam1_part, *words, *words_far, v0_far, flow]
        lam0, *outer0, near0 = call(
            last,
            outs,
            [SMEM] + [whole(x) for x in operands[1:8]] + [flow_spec[0]],
            [whole(x) for x in outs],
            operands,
            "last",
            weight=LAST,
            scratch=[pltpu.VMEM((Z + 2, Y, X), jnp.float32)],
        )
        held, lam0 = after(inner0[1], lam0)
        far0[1] = swap(held, 1)

        def sweeps(facts_ref, s, v, out, u2):
            for z in range(-1, Z + 1):
                beside = plane_sum(s[z])
                if z - 1 in s:
                    beside = beside + s[z - 1]
                if z + 1 in s:
                    beside = beside + s[z + 1]
                u = (s[z] + beside * SEVENTH) * SEVENTH
                if z == -1:
                    u = jnp.where(facts_ref[1] > 0, u, 0.0)
                if z == Z:
                    u = jnp.where(facts_ref[2] > 0, u, 0.0)
                u2[z + 1] = u
            for z in range(Z):
                u = u2[z + 1]
                beside = plane_sum(u) + u2[z] + u2[z + 2]
                out[0, 0, z] = v[0, 0, z] + (s[z] + beside) * SEVENTH

        class Planes:
            def __init__(self, ref, low, high):
                self.ref, self.low, self.high = ref, low, high

            def __contains__(self, z):
                return self.low <= z <= self.high

            def __getitem__(self, z):
                return self.ref[z - self.low]

        part = pl.BlockSpec((1, Y, X), lambda d: (d, 0, 0))
        flow_part = [
            pl.BlockSpec((1, 1, Z, Y, X), lambda d, t=t: (t, d, 0, 0, 0)) for t in range(steps)
        ]
        u2_scratch = pltpu.VMEM((Z + 2, Y, X), jnp.float32)

        def share(k):
            start = lax.rem(group + k, subj) * rows
            return lax.dynamic_slice_in_dim(lam0, start, rows, axis=1)

        template_grad = share(0)
        for k in range(1, subj):
            template_grad = template_grad + turn(share(k), k)

        def smooth_0(facts_ref, in0, in1, out0, out1, near, v, out, rim, u2, s):
            for i, inner, outer in ((0, in0, out0), (1, in1, out1)):
                up = up_at(facts_ref, i)
                s[2 + up * (Z - 3)] = inner[0]
                s[1 + up * (Z - 1)] = outer[0]
            s[0] = near[0, 0]
            s[Z + 1] = near[1, 0]
            sweeps(facts_ref, Planes(s, -1, Z), v, out, u2)
            for i in SIDES:
                rim[i, 0] = out[0, 0, up_at(facts_ref, i) * (Z - 1)]

        both = pl.BlockSpec((2, 1, Y, X), lambda d: (0, d, 0, 0))
        gradient, rim = call(
            smooth_0,
            [struct(*flow.shape), struct(2, 3, Y, X)],
            [SMEM] + [part] * 4 + [both, flow_part[0]],
            [flow_part[0], both],
            [facts, *inner0, *outer0, near0, flow],
            "smooth_0",
            weight=SMOOTH,
            grid=(3,),
            scratch=[u2_scratch, pltpu.VMEM((Z + 2, Y, X), jnp.float32)],
        )

        def smooth_1(facts_ref, in0, in1, out0, out1, near0, near1, far0, far1, _, v, out, u2, s):
            for i, inner, outer, near, far in ((0, in0, out0, near0, far0), (1, in1, out1, near1, far1)):
                up = up_at(facts_ref, i)
                s[3 + up * (Z - 3)] = inner[0]
                s[2 + up * (Z - 1)] = outer[0]
                s[1 + up * (Z + 1)] = near[0]
                s[up * (Z + 3)] = far[0]
            sweeps(facts_ref, Planes(s, -2, Z + 1), v, out, u2)

        gradient = call(
            smooth_1,
            struct(*flow.shape),
            [SMEM] + [part] * 8 + [pl.BlockSpec(memory_space=pl.ANY), flow_part[1]],
            flow_part[1],
            [facts, *inner1, *outer1, *near1, *far1, gradient, flow],
            "smooth_1",
            weight=SMOOTH,
            grid=(3,),
            aliases={9: 0},
            scratch=[u2_scratch, pltpu.VMEM((Z + 4, Y, X), jnp.float32)],
        )

        def add_far(facts_ref, far_0, far_1, rim, _, out, held, done):
            copies = []
            for i, far in ((0, far_0), (1, far_1)):
                z = up_at(facts_ref, i) * (Z - 1)
                for d in range(3):
                    held[i, d] = rim[i, d] + far[d] * SEVENTH**3
                    copies.append(pltpu.make_async_copy(held.at[i, d], out.at[0, d, z], done.at[i, d]))
                    copies[-1].start()
            for copy in copies:
                copy.wait()

        gradient = call(
            add_far,
            struct(*flow.shape),
            [SMEM] + [whole(x) for x in (*far0, rim)] + [pl.BlockSpec(memory_space=pl.ANY)],
            pl.BlockSpec(memory_space=pl.ANY),
            [facts, *far0, rim, gradient],
            "add_far",
            aliases={4: 0},
            scratch=[pltpu.VMEM((2, 3, Y, X), jnp.float32), pltpu.SemaphoreType.DMA((2, 3))],
        )
        return gradient[None], template_grad

    return body


def solution(mesh):
    sizes = dict(mesh.shape)
    return jax.shard_map(
        make_body(sizes["subj"], sizes["slab"]),
        mesh=mesh,
        in_specs=(
            P("slab", "subj", None),
            P("subj", "slab", None, None),
            P("subj", None, None, "slab", None, None),
        ),
        out_specs=(P("subj", None, None, "slab", None, None), P("slab", "subj", None)),
        check_vma=False,
    )
```

```python
import jax
import jax.numpy as jnp
from jax import lax
from jax.experimental import pallas as pl
from jax.experimental.pallas import tpu as pltpu
from jax.sharding import PartitionSpec as P

MATCH = 5.0
SEVENTH = 1.0 / 7.0
MIB = 1 << 20
FORWARD, MIDDLE, BACK, LAST, SMOOTH = 0, 0, 1000, 2000, 1000


def col_prev(f):
    x = lax.broadcasted_iota(jnp.int32, f.shape, 1)
    return jnp.where(x == 0, 0.0, pltpu.roll(f, 1, 1))


def col_next(f):
    n = f.shape[1]
    x = lax.broadcasted_iota(jnp.int32, f.shape, 1)
    return jnp.where(x == n - 1, 0.0, pltpu.roll(f, n - 1, 1))


def row_prev(f):
    y = lax.broadcasted_iota(jnp.int32, f.shape, 0)
    return jnp.where(y == 0, 0.0, pltpu.roll(f, 1, 0))


def row_next(f):
    n = f.shape[0]
    y = lax.broadcasted_iota(jnp.int32, f.shape, 0)
    return jnp.where(y == n - 1, 0.0, pltpu.roll(f, n - 1, 0))


def upwind(below, f, above, v):
    return [
        jnp.where(v[0] >= 0.0, f - below, above - f),
        jnp.where(v[1] >= 0.0, f - row_prev(f), row_next(f) - f),
        jnp.where(v[2] >= 0.0, f - col_prev(f), col_next(f) - f),
    ]


def advance(f, diffs, v, dt):
    return f - dt * (v[0] * diffs[0] + v[1] * diffs[1] + v[2] * diffs[2])


def retreat(lam, v, pos_above, neg_below, dt):
    total = (jnp.abs(v[0]) + jnp.abs(v[1]) + jnp.abs(v[2])) * lam
    total = total - row_next(jnp.maximum(v[1], 0.0) * lam)
    total = total + row_prev(jnp.minimum(v[1], 0.0) * lam)
    total = total - col_next(jnp.maximum(v[2], 0.0) * lam)
    total = total + col_prev(jnp.minimum(v[2], 0.0) * lam)
    if pos_above is not None:
        total = total - pos_above
    if neg_below is not None:
        total = total + neg_below
    return lam - dt * total


def plane_sum(f):
    return row_prev(f) + row_next(f) + col_prev(f) + col_next(f)


def call(kernel, out_shape, in_specs, out_specs, operands, name, weight=0, grid=(1,), aliases=None, scratch=(), prefetch=0):
    return pl.pallas_call(
        kernel,
        out_shape=out_shape,
        grid_spec=pltpu.PrefetchScalarGridSpec(
            num_scalar_prefetch=prefetch,
            grid=grid,
            in_specs=in_specs,
            out_specs=out_specs,
            scratch_shapes=list(scratch),
        ),
        input_output_aliases=aliases or {},
        compiler_params=pltpu.CompilerParams(vmem_limit_bytes=24 * MIB),
        cost_estimate=pl.CostEstimate(
            flops=1024 + weight * 10000000, bytes_accessed=1024, transcendentals=0
        ),
        name=name,
    )(*operands)


def whole(x):
    zeros = (0,) * x.ndim
    return pl.BlockSpec(x.shape, lambda *_: zeros)


def struct(*shape):
    return jax.ShapeDtypeStruct(shape, jnp.float32)


SMEM = pl.BlockSpec(memory_space=pltpu.SMEM)
SIDES = (0, 1)


def make_body(subj, slabs):
    pairs = []
    for first in SIDES:
        lower = [(i, i + 1) for i in range(first, slabs - 1, 2)]
        pairs.append(lower + [(j, i) for i, j in lower])

    def swap(x, side):
        return lax.ppermute(x, "slab", pairs[side])

    def turn(x, k):
        return lax.ppermute(x, "subj", [(i, (i + k) % subj) for i in range(subj)])

    def after(x, *others):
        return lax.optimization_barrier((x, *others))

    def body(template, subject, velocity):
        flow = velocity[0]
        target = subject[0]
        steps, _, Z, Y, X = flow.shape
        assert Z == 4 and steps == 2
        rows = template.shape[1]
        dt = 1.0 / steps
        place = lax.axis_index("slab")
        group = lax.axis_index("subj")
        even = 1 - place % 2
        facts = jnp.stack([group, place > 0, place < slabs - 1, even]).astype(jnp.int32)
        ups = (even, 1 - even)
        flow_spec = [
            pl.BlockSpec((1, 3, Z, Y, X), lambda *_, t=t: (t, 0, 0, 0, 0)) for t in range(steps)
        ]

        def up_at(facts_ref, i):
            return facts_ref[3] if i == 0 else 1 - facts_ref[3]

        tmpl_far = [
            swap(lax.dynamic_slice_in_dim(template, up * (Z - 2), 2, 0), i)
            for i, up in enumerate(ups)
        ]
        flow0_edge = [
            lax.dynamic_slice(velocity, (0, 0, 0, up * (Z - 1), 0, 0), (1, 1, 3, 1, Y, X))[0, 0, :, 0]
            for up in ups
        ]
        flow0_far = [swap(flow0_edge[i], i) for i in SIDES]
        own_parts = [template] + [turn(template, k) for k in range(1, subj)]
        tmpl_far[1], tmpl_far[0], _, _ = after(*tmpl_far[::-1], *flow0_edge)
        edge = jnp.concatenate(tmpl_far[::-1], axis=0)
        edge_parts = [edge] + [turn(edge, k) for k in range(1, subj)]

        def forward(*refs):
            facts_ref, refs = refs[0], refs[1:]
            owns, edges = refs[:subj], refs[subj : 2 * subj]
            v0, v1, aim = refs[2 * subj : 2 * subj + 3]
            tmpl, img1, lam2, *srcs = refs[2 * subj + 3 :]
            for k in range(subj):
                start = pl.multiple_of(lax.rem(facts_ref[0] + subj - k, subj) * rows, rows)
                at = pl.ds(start, rows)
                tmpl[2 : Z + 2, at, :] = owns[k][...]
                for i in SIDES:
                    up = up_at(facts_ref, i)
                    for j in range(2):
                        tmpl[up * (Z + 2) + j, at, :] = edges[k][2 * (1 - i) + j]
            for z in range(Z):
                v = [v0[0, d, z] for d in range(3)]
                f = tmpl[z + 2]
                img1[z] = advance(f, upwind(tmpl[z + 1], f, tmpl[z + 3], v), v, dt)
            for i in SIDES:
                z = 1 + up_at(facts_ref, i) * (Z - 3)
                v = [v1[0, d, z] for d in range(3)]
                f = img1[z]
                diffs = upwind(img1[z - 1], f, img1[z + 1], v)
                lam = advance(f, diffs, v, dt) - aim[z]
                lam2[i] = lam
                for d in range(3):
                    srcs[i][d] = (-MATCH * dt) * lam * diffs[d]

        outs = [struct(Z + 4, Y, X), struct(Z, Y, X), struct(2, Y, X)] + [struct(3, Y, X)] * 2
        operands = [facts] + own_parts + edge_parts + [flow, flow, target]
        tmpl, img1, lam2_in, *inner1 = call(
            forward,
            outs,
            [SMEM]
            + [whole(x) for x in own_parts + edge_parts]
            + [flow_spec[0], flow_spec[1], whole(target)],
            [whole(x) for x in outs],
            operands,
            "forward",
            weight=FORWARD,
        )
        far1 = [swap(inner1[0], 0), None]

        def middle(facts_ref, tmpl, img1, halo0, halo1, v1, aim, src0, src1, lam2, v0_far):
            for i, halo, src in ((0, halo0, src0), (1, halo1, src1)):
                up = up_at(facts_ref, i)
                at = 1 + up * (Z + 1)
                v = [halo[d] for d in range(3)]
                for d in range(3):
                    v0_far[up, d] = v[d]
                f = tmpl[at]
                outside = advance(f, upwind(tmpl[at - 1], f, tmpl[at + 1], v), v, dt)
                z = up * (Z - 1)
                inside = img1[z + 1 - 2 * up]
                below = jnp.where(up == 1, inside, outside)
                above = jnp.where(up == 1, outside, inside)
                v = [v1[0, d, z] for d in range(3)]
                f = img1[z]
                diffs = upwind(below, f, above, v)
                lam = advance(f, diffs, v, dt) - aim[z]
                for d in range(3):
                    src[d] = (-MATCH * dt) * lam * diffs[d]
                lam2[i] = lam

        outs = [struct(3, Y, X)] * 2 + [struct(2, Y, X), struct(2, 3, Y, X)]
        operands = [facts, tmpl, img1, *flow0_far, flow, target]
        *outer1, lam2_out, v0_far = call(
            middle,
            outs,
            [SMEM] + [whole(x) for x in operands[1:5]] + [flow_spec[1], whole(target)],
            [whole(x) for x in outs],
            operands,
            "middle",
            weight=MIDDLE,
        )
        def back(facts_ref, lam2_in, lam2_out, v1, lam1, word0, word1, lam2):
            for i in SIDES:
                up = up_at(facts_ref, i)
                lam2[1 + up * (Z - 3)] = lam2_in[i]
                lam2[up * (Z - 1)] = lam2_out[i]
            for z in range(Z):
                v = [v1[0, d, z] for d in range(3)]
                above = jnp.maximum(v1[0, 0, z + 1], 0.0) * lam2[z + 1] if z < Z - 1 else None
                below = jnp.minimum(v1[0, 0, z - 1], 0.0) * lam2[z - 1] if z > 0 else None
                lam1[z] = retreat(lam2[z], v, above, below, dt)
            for i, word in ((0, word0), (1, word1)):
                up = up_at(facts_ref, i)
                z = up * (Z - 1)
                v = v1[0, 0, z]
                word[0] = jnp.where(up == 1, jnp.minimum(v, 0.0), jnp.maximum(v, 0.0)) * lam2[z]
                word[1] = lam1[z]

        outs = [struct(Z, Y, X)] + [struct(2, Y, X)] * 2
        operands = [facts, lam2_in, lam2_out, flow]
        lam1_part, *words = call(
            back,
            outs,
            [SMEM] + [whole(x) for x in operands[1:3]] + [flow_spec[1]],
            [whole(x) for x in outs],
            operands,
            "back",
            weight=BACK,
            scratch=[pltpu.VMEM((Z, Y, X), jnp.float32)],
        )
        words_far = [swap(words[i], i) for i in SIDES]
        near1 = [swap(after(outer1[0], *words)[0], 0), None]

        held, far1[0], *words_far = after((inner1[1], outer1[1]), far1[0], *words_far)
        far1[1], near1[1] = [swap(x, 1) for x in held]

        def last(facts_ref, tmpl, part, own0, own1, far0, far1, v0_far, v0, lam0, src0, src1, out0, out1, near, lam):
            for z in range(1, Z - 1):
                lam[z + 1] = part[z]
            for i, own, far in ((0, own0, far0), (1, own1, far1)):
                up = up_at(facts_ref, i)
                toward = dt * (2 * up - 1).astype(jnp.float32)
                inside = jnp.where(up == 1, facts_ref[2], facts_ref[1]) > 0
                lam[1 + up * (Z - 1)] = own[1] + toward * far[0]
                lam[up * (Z + 1)] = jnp.where(inside, far[1] - toward * own[0], 0.0)

            def flow_at(z, d):
                return v0[0, d, z] if 0 <= z < Z else v0_far[0 if z < 0 else 1, d]

            def source(z, v, src, *at):
                diffs = upwind(tmpl[z + 1], tmpl[z + 2], tmpl[z + 3], v)
                for d in range(3):
                    src[(*at, d)] = (-MATCH * dt) * lam[z + 1] * diffs[d]

            for i, inner, outer in ((0, src0, out0), (1, src1, out1)):
                up = up_at(facts_ref, i)
                for z, src in ((1 + up * (Z - 3), inner), (up * (Z - 1), outer)):
                    source(z, [v0[0, d, z] for d in range(3)], src)
            for j, z in enumerate((-1, Z)):
                source(z, [flow_at(z, d) for d in range(3)], near, j)
            for z in range(Z):
                above = jnp.maximum(flow_at(z + 1, 0), 0.0) * lam[z + 2]
                below = jnp.minimum(flow_at(z - 1, 0), 0.0) * lam[z]
                v = [flow_at(z, d) for d in range(3)]
                lam0[z] = retreat(lam[z + 1], v, above, below, dt)

        outs = [struct(Z, Y, X)] + [struct(3, Y, X)] * 4 + [struct(2, 3, Y, X)]
        operands = [facts, tmpl, lam1_part, *words, *words_far, v0_far, flow]
        lam0, *inner_outer, near0 = call(
            last,
            outs,
            [SMEM] + [whole(x) for x in operands[1:8]] + [flow_spec[0]],
            [whole(x) for x in outs],
            operands,
            "last",
            weight=LAST,
            scratch=[pltpu.VMEM((Z + 2, Y, X), jnp.float32)],
        )
        inner0, outer0 = inner_outer[:2], inner_outer[2:]
        far0 = [swap(inner0[i], i) for i in SIDES]

        def sweeps(facts_ref, s, v, out, u2):
            for z in range(-1, Z + 1):
                beside = plane_sum(s[z])
                if z - 1 in s:
                    beside = beside + s[z - 1]
                if z + 1 in s:
                    beside = beside + s[z + 1]
                u = (s[z] + beside * SEVENTH) * SEVENTH
                if z == -1:
                    u = jnp.where(facts_ref[1] > 0, u, 0.0)
                if z == Z:
                    u = jnp.where(facts_ref[2] > 0, u, 0.0)
                u2[z + 1] = u
            for z in range(Z):
                u = u2[z + 1]
                beside = plane_sum(u) + u2[z] + u2[z + 2]
                out[0, 0, z] = v[0, 0, z] + (s[z] + beside) * SEVENTH

        class Planes:
            def __init__(self, ref, low, high):
                self.ref, self.low, self.high = ref, low, high

            def __contains__(self, z):
                return self.low <= z <= self.high

            def __getitem__(self, z):
                return self.ref[z - self.low]

        part = pl.BlockSpec((1, Y, X), lambda d: (d, 0, 0))
        flow_part = [
            pl.BlockSpec((1, 1, Z, Y, X), lambda d, t=t: (t, d, 0, 0, 0)) for t in range(steps)
        ]
        u2_scratch = pltpu.VMEM((Z + 2, Y, X), jnp.float32)

        def share(k):
            start = lax.rem(group + k, subj) * rows
            return lax.dynamic_slice_in_dim(lam0, start, rows, axis=1)

        template_grad = share(0)
        for k in range(1, subj):
            template_grad = template_grad + turn(share(k), k)

        def smooth_0(facts_ref, in0, in1, out0, out1, near, v, out, rim, u2, s):
            for i, inner, outer in ((0, in0, out0), (1, in1, out1)):
                up = up_at(facts_ref, i)
                s[2 + up * (Z - 3)] = inner[0]
                s[1 + up * (Z - 1)] = outer[0]
            s[0] = near[0, 0]
            s[Z + 1] = near[1, 0]
            sweeps(facts_ref, Planes(s, -1, Z), v, out, u2)
            for i in SIDES:
                rim[i, 0] = out[0, 0, up_at(facts_ref, i) * (Z - 1)]

        both = pl.BlockSpec((2, 1, Y, X), lambda d: (0, d, 0, 0))
        gradient, rim = call(
            smooth_0,
            [struct(*flow.shape), struct(2, 3, Y, X)],
            [SMEM] + [part] * 4 + [both, flow_part[0]],
            [flow_part[0], both],
            [facts, *inner0, *outer0, near0, flow],
            "smooth_0",
            weight=SMOOTH,
            grid=(3,),
            scratch=[u2_scratch, pltpu.VMEM((Z + 2, Y, X), jnp.float32)],
        )

        def smooth_1(facts_ref, in0, in1, out0, out1, near0, near1, far0, far1, _, v, out, u2, s):
            for i, inner, outer, near, far in ((0, in0, out0, near0, far0), (1, in1, out1, near1, far1)):
                up = up_at(facts_ref, i)
                s[3 + up * (Z - 3)] = inner[0]
                s[2 + up * (Z - 1)] = outer[0]
                s[1 + up * (Z + 1)] = near[0]
                s[up * (Z + 3)] = far[0]
            sweeps(facts_ref, Planes(s, -2, Z + 1), v, out, u2)

        gradient = call(
            smooth_1,
            struct(*flow.shape),
            [SMEM] + [part] * 8 + [pl.BlockSpec(memory_space=pl.ANY), flow_part[1]],
            flow_part[1],
            [facts, *inner1, *outer1, *near1, *far1, gradient, flow],
            "smooth_1",
            weight=SMOOTH,
            grid=(3,),
            aliases={9: 0},
            scratch=[u2_scratch, pltpu.VMEM((Z + 4, Y, X), jnp.float32)],
        )

        def add_far(facts_ref, far_0, far_1, rim, _, out, held, done):
            copies = []
            for i, far in ((0, far_0), (1, far_1)):
                z = up_at(facts_ref, i) * (Z - 1)
                for d in range(3):
                    held[i, d] = rim[i, d] + far[d] * SEVENTH**3
                    copies.append(pltpu.make_async_copy(held.at[i, d], out.at[0, d, z], done.at[i, d]))
                    copies[-1].start()
            for copy in copies:
                copy.wait()

        gradient = call(
            add_far,
            struct(*flow.shape),
            [SMEM] + [whole(x) for x in (*far0, rim)] + [pl.BlockSpec(memory_space=pl.ANY)],
            pl.BlockSpec(memory_space=pl.ANY),
            [facts, *far0, rim, gradient],
            "add_far",
            aliases={4: 0},
            scratch=[pltpu.VMEM((2, 3, Y, X), jnp.float32), pltpu.SemaphoreType.DMA((2, 3))],
        )
        return gradient[None], template_grad

    return body


def solution(mesh):
    sizes = dict(mesh.shape)
    return jax.shard_map(
        make_body(sizes["subj"], sizes["slab"]),
        mesh=mesh,
        in_specs=(
            P("slab", "subj", None),
            P("subj", "slab", None, None),
            P("subj", None, None, "slab", None, None),
        ),
        out_specs=(P("subj", None, None, "slab", None, None), P("slab", "subj", None)),
        check_vma=False,
    )
```

```python
import jax
import jax.numpy as jnp
from jax import lax
from jax.experimental import pallas as pl
from jax.experimental.pallas import tpu as pltpu
from jax.sharding import PartitionSpec as P

MATCH = 5.0
SEVENTH = 1.0 / 7.0
MIB = 1 << 20
FORWARD, MIDDLE, BACK, LAST, SMOOTH = 0, 0, 1000, 2000, 1000


def col_prev(f):
    x = lax.broadcasted_iota(jnp.int32, f.shape, 1)
    return jnp.where(x == 0, 0.0, pltpu.roll(f, 1, 1))


def col_next(f):
    n = f.shape[1]
    x = lax.broadcasted_iota(jnp.int32, f.shape, 1)
    return jnp.where(x == n - 1, 0.0, pltpu.roll(f, n - 1, 1))


def row_prev(f):
    y = lax.broadcasted_iota(jnp.int32, f.shape, 0)
    return jnp.where(y == 0, 0.0, pltpu.roll(f, 1, 0))


def row_next(f):
    n = f.shape[0]
    y = lax.broadcasted_iota(jnp.int32, f.shape, 0)
    return jnp.where(y == n - 1, 0.0, pltpu.roll(f, n - 1, 0))


def upwind(below, f, above, v):
    return [
        jnp.where(v[0] >= 0.0, f - below, above - f),
        jnp.where(v[1] >= 0.0, f - row_prev(f), row_next(f) - f),
        jnp.where(v[2] >= 0.0, f - col_prev(f), col_next(f) - f),
    ]


def advance(f, diffs, v, dt):
    return f - dt * (v[0] * diffs[0] + v[1] * diffs[1] + v[2] * diffs[2])


def retreat(lam, v, pos_above, neg_below, dt):
    total = (jnp.abs(v[0]) + jnp.abs(v[1]) + jnp.abs(v[2])) * lam
    total = total - row_next(jnp.maximum(v[1], 0.0) * lam)
    total = total + row_prev(jnp.minimum(v[1], 0.0) * lam)
    total = total - col_next(jnp.maximum(v[2], 0.0) * lam)
    total = total + col_prev(jnp.minimum(v[2], 0.0) * lam)
    if pos_above is not None:
        total = total - pos_above
    if neg_below is not None:
        total = total + neg_below
    return lam - dt * total


def plane_sum(f):
    return row_prev(f) + row_next(f) + col_prev(f) + col_next(f)


def call(kernel, out_shape, in_specs, out_specs, operands, name, weight=0, grid=(1,), aliases=None, scratch=()):
    return pl.pallas_call(
        kernel,
        out_shape=out_shape,
        grid=grid,
        in_specs=in_specs,
        out_specs=out_specs,
        scratch_shapes=list(scratch),
        input_output_aliases=aliases or {},
        compiler_params=pltpu.CompilerParams(vmem_limit_bytes=48 * MIB),
        cost_estimate=pl.CostEstimate(
            flops=1024 + weight * 10000000, bytes_accessed=1024, transcendentals=0
        ),
        name=name,
    )(*operands)


def whole(x):
    zeros = (0,) * x.ndim
    return pl.BlockSpec(x.shape, lambda *_: zeros)


def struct(*shape):
    return jax.ShapeDtypeStruct(shape, jnp.float32)


SMEM = pl.BlockSpec(memory_space=pltpu.SMEM)
VMEM = pl.BlockSpec(memory_space=pltpu.VMEM)
ANY = pl.BlockSpec(memory_space=pl.ANY)
SIDES = (0, 1)


def make_body(subj, slabs):
    pairs = []
    for first in SIDES:
        lower = [(i, i + 1) for i in range(first, slabs - 1, 2)]
        pairs.append(lower + [(j, i) for i, j in lower])

    def swap(x, side):
        return lax.ppermute(x, "slab", pairs[side])

    def turn(x, k):
        return lax.ppermute(x, "subj", [(i, (i + k) % subj) for i in range(subj)])

    def after(x, *others):
        return lax.optimization_barrier((x, *others))

    def body(template, subject, velocity):
        flow = velocity[0]
        target = subject[0]
        steps, _, Z, Y, X = flow.shape
        assert Z == 4 and steps == 2
        rows = template.shape[1]
        dt = 1.0 / steps
        place = lax.axis_index("slab")
        group = lax.axis_index("subj")
        even = 1 - place % 2
        facts = jnp.stack([group, place > 0, place < slabs - 1, even]).astype(jnp.int32)
        ups = (even, 1 - even)
        flow_spec = [
            pl.BlockSpec((1, 3, Z, Y, X), lambda *_, t=t: (t, 0, 0, 0, 0)) for t in range(steps)
        ]

        def up_at(facts_ref, i):
            return facts_ref[3] if i == 0 else 1 - facts_ref[3]

        def up_here(i):
            odd = lax.rem(lax.axis_index("slab"), 2)
            return 1 - odd if i == 0 else odd

        tmpl_far = [
            swap(lax.dynamic_slice_in_dim(template, up * (Z - 2), 2, 0), i)
            for i, up in enumerate(ups)
        ]
        flow0_edge = [
            lax.dynamic_slice(velocity, (0, 0, 0, up * (Z - 1), 0, 0), (1, 1, 3, 1, Y, X))[0, 0, :, 0]
            for up in ups
        ]
        flow0_far = [swap(flow0_edge[i], i) for i in SIDES]
        own_parts = [template] + [turn(template, k) for k in range(1, subj)]
        tmpl_far[1], tmpl_far[0], _, _ = after(*tmpl_far[::-1], *flow0_edge)
        edge = jnp.concatenate(tmpl_far[::-1], axis=0)
        edge_parts = [edge] + [turn(edge, k) for k in range(1, subj)]

        def forward(*refs):
            facts_ref, refs = refs[0], refs[1:]
            owns, edges = refs[:subj], refs[subj : 2 * subj]
            v0, v1, aim = refs[2 * subj : 2 * subj + 3]
            tmpl, img1, lam2, *srcs = refs[2 * subj + 3 :]
            for k in range(subj):
                start = pl.multiple_of(lax.rem(facts_ref[0] + subj - k, subj) * rows, rows)
                at = pl.ds(start, rows)
                tmpl[2 : Z + 2, at, :] = owns[k][...]
                for i in SIDES:
                    up = up_at(facts_ref, i)
                    for j in range(2):
                        tmpl[up * (Z + 2) + j, at, :] = edges[k][2 * (1 - i) + j]
            for z in range(Z):
                v = [v0[0, d, z] for d in range(3)]
                f = tmpl[z + 2]
                img1[z] = advance(f, upwind(tmpl[z + 1], f, tmpl[z + 3], v), v, dt)
            for i in SIDES:
                z = 1 + up_at(facts_ref, i) * (Z - 3)
                v = [v1[0, d, z] for d in range(3)]
                f = img1[z]
                diffs = upwind(img1[z - 1], f, img1[z + 1], v)
                lam = advance(f, diffs, v, dt) - aim[z]
                lam2[i] = lam
                for d in range(3):
                    srcs[i][d] = (-MATCH * dt) * lam * diffs[d]

        outs = [struct(Z + 4, Y, X), struct(Z, Y, X), struct(2, Y, X)] + [struct(3, Y, X)] * 2
        operands = [facts] + own_parts + edge_parts + [flow, flow, target]
        tmpl, img1, lam2_in, *inner1 = call(
            forward,
            outs,
            [SMEM]
            + [whole(x) for x in own_parts + edge_parts]
            + [flow_spec[0], flow_spec[1], whole(target)],
            [whole(x) for x in outs],
            operands,
            "forward",
            weight=FORWARD,
        )
        far1 = [swap(inner1[0], 0), None]

        def middle(facts_ref, tmpl, img1, halo0, halo1, v1, aim, src0, src1, lam2, v0_far):
            for i, halo, src in ((0, halo0, src0), (1, halo1, src1)):
                up = up_at(facts_ref, i)
                at = 1 + up * (Z + 1)
                v = [halo[d] for d in range(3)]
                for d in range(3):
                    v0_far[up, d] = v[d]
                f = tmpl[at]
                outside = advance(f, upwind(tmpl[at - 1], f, tmpl[at + 1], v), v, dt)
                z = up * (Z - 1)
                inside = img1[z + 1 - 2 * up]
                below = jnp.where(up == 1, inside, outside)
                above = jnp.where(up == 1, outside, inside)
                v = [v1[0, d, z] for d in range(3)]
                f = img1[z]
                diffs = upwind(below, f, above, v)
                lam = advance(f, diffs, v, dt) - aim[z]
                for d in range(3):
                    src[d] = (-MATCH * dt) * lam * diffs[d]
                lam2[i] = lam

        outs = [struct(3, Y, X)] * 2 + [struct(2, Y, X), struct(2, 3, Y, X)]
        operands = [facts, tmpl, img1, *flow0_far, flow, target]
        *outer1, lam2_out, v0_far = call(
            middle,
            outs,
            [SMEM] + [whole(x) for x in operands[1:5]] + [flow_spec[1], whole(target)],
            [whole(x) for x in outs],
            operands,
            "middle",
            weight=MIDDLE,
        )
        def back(facts_ref, lam2_in, lam2_out, v1, lam1, word0, word1, lam2):
            for i in SIDES:
                up = up_at(facts_ref, i)
                lam2[1 + up * (Z - 3)] = lam2_in[i]
                lam2[up * (Z - 1)] = lam2_out[i]
            for z in range(Z):
                v = [v1[0, d, z] for d in range(3)]
                above = jnp.maximum(v1[0, 0, z + 1], 0.0) * lam2[z + 1] if z < Z - 1 else None
                below = jnp.minimum(v1[0, 0, z - 1], 0.0) * lam2[z - 1] if z > 0 else None
                lam1[z] = retreat(lam2[z], v, above, below, dt)
            for i, word in ((0, word0), (1, word1)):
                up = up_at(facts_ref, i)
                z = up * (Z - 1)
                v = v1[0, 0, z]
                word[0] = jnp.where(up == 1, jnp.minimum(v, 0.0), jnp.maximum(v, 0.0)) * lam2[z]
                word[1] = lam1[z]

        outs = [struct(Z, Y, X)] + [struct(2, Y, X)] * 2
        operands = [facts, lam2_in, lam2_out, flow]
        lam1_part, *words = call(
            back,
            outs,
            [SMEM] + [whole(x) for x in operands[1:3]] + [flow_spec[1]],
            [whole(x) for x in outs],
            operands,
            "back",
            weight=BACK,
            scratch=[pltpu.VMEM((Z, Y, X), jnp.float32)],
        )
        words_far = [swap(words[i], i) for i in SIDES]
        near1 = [swap(after(outer1[0], *words)[0], 0), None]

        held, far1[0], *words_far = after((inner1[1], outer1[1]), far1[0], *words_far)
        far1[1], near1[1] = [swap(x, 1) for x in held]

        def last(facts_ref, tmpl, part, own0, own1, far0, far1, v0_far, v0, lam0, src0, src1, out0, out1, near, lam):
            for z in range(1, Z - 1):
                lam[z + 1] = part[z]
            for i, own, far in ((0, own0, far0), (1, own1, far1)):
                up = up_at(facts_ref, i)
                toward = dt * (2 * up - 1).astype(jnp.float32)
                inside = jnp.where(up == 1, facts_ref[2], facts_ref[1]) > 0
                lam[1 + up * (Z - 1)] = own[1] + toward * far[0]
                lam[up * (Z + 1)] = jnp.where(inside, far[1] - toward * own[0], 0.0)

            def flow_at(z, d):
                return v0[0, d, z] if 0 <= z < Z else v0_far[0 if z < 0 else 1, d]

            def source(z, v, src, *at):
                diffs = upwind(tmpl[z + 1], tmpl[z + 2], tmpl[z + 3], v)
                for d in range(3):
                    src[(*at, d)] = (-MATCH * dt) * lam[z + 1] * diffs[d]

            for i, inner, outer in ((0, src0, out0), (1, src1, out1)):
                up = up_at(facts_ref, i)
                for z, src in ((1 + up * (Z - 3), inner), (up * (Z - 1), outer)):
                    source(z, [v0[0, d, z] for d in range(3)], src)
            for j, z in enumerate((-1, Z)):
                source(z, [flow_at(z, d) for d in range(3)], near, j)
            for z in range(Z):
                above = jnp.maximum(flow_at(z + 1, 0), 0.0) * lam[z + 2]
                below = jnp.minimum(flow_at(z - 1, 0), 0.0) * lam[z]
                v = [flow_at(z, d) for d in range(3)]
                lam0[z] = retreat(lam[z + 1], v, above, below, dt)

        outs = [struct(Z, Y, X)] + [struct(3, Y, X)] * 4 + [struct(2, 3, Y, X)]
        operands = [facts, tmpl, lam1_part, *words, *words_far, v0_far, flow]
        lam0, *inner_outer, near0 = call(
            last,
            outs,
            [SMEM] + [whole(x) for x in operands[1:8]] + [flow_spec[0]],
            [whole(x) for x in outs],
            operands,
            "last",
            weight=LAST,
            scratch=[pltpu.VMEM((Z + 2, Y, X), jnp.float32)],
        )
        inner0, outer0 = inner_outer[:2], inner_outer[2:]
        far0 = [swap(inner0[i], i) for i in SIDES]

        def sweeps(facts_ref, s, v, out, u2):
            for z in range(-1, Z + 1):
                beside = plane_sum(s[z])
                if z - 1 in s:
                    beside = beside + s[z - 1]
                if z + 1 in s:
                    beside = beside + s[z + 1]
                u = (s[z] + beside * SEVENTH) * SEVENTH
                if z == -1:
                    u = jnp.where(facts_ref[1] > 0, u, 0.0)
                if z == Z:
                    u = jnp.where(facts_ref[2] > 0, u, 0.0)
                u2[z + 1] = u
            for z in range(Z):
                u = u2[z + 1]
                beside = plane_sum(u) + u2[z] + u2[z + 2]
                out[0, 0, z] = v[0, 0, z] + (s[z] + beside) * SEVENTH

        class Planes:
            def __init__(self, ref, low, high):
                self.ref, self.low, self.high = ref, low, high

            def __contains__(self, z):
                return self.low <= z <= self.high

            def __getitem__(self, z):
                return self.ref[z - self.low]

        part = pl.BlockSpec((1, Y, X), lambda d: (d, 0, 0))
        flow_part = [
            pl.BlockSpec((1, 1, Z, Y, X), lambda d, t=t: (t, d, 0, 0, 0)) for t in range(steps)
        ]
        u2_scratch = pltpu.VMEM((Z + 2, Y, X), jnp.float32)

        def share(k):
            start = lax.rem(group + k, subj) * rows
            return lax.dynamic_slice_in_dim(lam0, start, rows, axis=1)

        template_grad = share(0)
        for k in range(1, subj):
            template_grad = template_grad + turn(share(k), k)

        def smooth_0(facts_ref, in0, in1, out0, out1, near, v, out, rim, u2, s):
            for i, inner, outer in ((0, in0, out0), (1, in1, out1)):
                up = up_at(facts_ref, i)
                s[2 + up * (Z - 3)] = inner[0]
                s[1 + up * (Z - 1)] = outer[0]
            s[0] = near[0, 0]
            s[Z + 1] = near[1, 0]
            sweeps(facts_ref, Planes(s, -1, Z), v, out, u2)
            for i in SIDES:
                rim[i, 0] = out[0, 0, up_at(facts_ref, i) * (Z - 1)]

        both = pl.BlockSpec((2, 1, Y, X), lambda d: (0, d, 0, 0))
        gradient, rim = call(
            smooth_0,
            [struct(*flow.shape), struct(2, 3, Y, X)],
            [SMEM] + [part] * 4 + [both, flow_part[0]],
            [flow_part[0], both],
            [facts, *inner0, *outer0, near0, flow],
            "smooth_0",
            weight=SMOOTH,
            grid=(3,),
            scratch=[u2_scratch, pltpu.VMEM((Z + 2, Y, X), jnp.float32)],
        )

        def smooth_1(facts_ref, in0, in1, out0, out1, near0, near1, far0, far1, _, v, out, u2, s):
            for i, inner, outer, near, far in ((0, in0, out0, near0, far0), (1, in1, out1, near1, far1)):
                up = up_at(facts_ref, i)
                s[3 + up * (Z - 3)] = inner[0]
                s[2 + up * (Z - 1)] = outer[0]
                s[1 + up * (Z + 1)] = near[0]
                s[up * (Z + 3)] = far[0]
            sweeps(facts_ref, Planes(s, -2, Z + 1), v, out, u2)

        gradient = call(
            smooth_1,
            struct(*flow.shape),
            [SMEM] + [part] * 8 + [pl.BlockSpec(memory_space=pl.ANY), flow_part[1]],
            flow_part[1],
            [facts, *inner1, *outer1, *near1, *far1, gradient, flow],
            "smooth_1",
            weight=SMOOTH,
            grid=(3,),
            aliases={9: 0},
            scratch=[u2_scratch, pltpu.VMEM((Z + 4, Y, X), jnp.float32)],
        )

        def add_far(far_0, far_1, rim, _, out, held, done):
            copies = []
            for i, far in ((0, far_0), (1, far_1)):
                z = up_here(i) * (Z - 1)
                for d in range(3):
                    held[i, d] = rim[i, d] + far[d] * SEVENTH**3
                    copies.append(pltpu.make_async_copy(held.at[i, d], out.at[0, d, z], done.at[i, d]))
                    copies[-1].start()
            for copy in copies:
                copy.wait()

        gradient = call(
            add_far,
            struct(*flow.shape),
            [VMEM, VMEM, VMEM, ANY],
            ANY,
            [*far0, rim, gradient],
            "add_far",
            grid=(),
            aliases={3: 0},
            scratch=[pltpu.VMEM((2, 3, Y, X), jnp.float32), pltpu.SemaphoreType.DMA((2, 3))],
        )
        return gradient[None], template_grad

    return body


def solution(mesh):
    sizes = dict(mesh.shape)
    return jax.shard_map(
        make_body(sizes["subj"], sizes["slab"]),
        mesh=mesh,
        in_specs=(
            P("slab", "subj", None),
            P("subj", "slab", None, None),
            P("subj", None, None, "slab", None, None),
        ),
        out_specs=(P("subj", None, None, "slab", None, None), P("slab", "subj", None)),
        check_vma=False,
    )
```

```python
import jax
import jax.numpy as jnp
from jax import lax
from jax.experimental import pallas as pl
from jax.experimental.pallas import tpu as pltpu
from jax.sharding import PartitionSpec as P

MATCH = 5.0
SEVENTH = 1.0 / 7.0
MIB = 1 << 20
FORWARD, MIDDLE, BACK, LAST, SMOOTH = 0, 0, 1000, 2000, 1000


def col_prev(f):
    x = lax.broadcasted_iota(jnp.int32, f.shape, 1)
    return jnp.where(x == 0, 0.0, pltpu.roll(f, 1, 1))


def col_next(f):
    n = f.shape[1]
    x = lax.broadcasted_iota(jnp.int32, f.shape, 1)
    return jnp.where(x == n - 1, 0.0, pltpu.roll(f, n - 1, 1))


def row_prev(f):
    y = lax.broadcasted_iota(jnp.int32, f.shape, 0)
    return jnp.where(y == 0, 0.0, pltpu.roll(f, 1, 0))


def row_next(f):
    n = f.shape[0]
    y = lax.broadcasted_iota(jnp.int32, f.shape, 0)
    return jnp.where(y == n - 1, 0.0, pltpu.roll(f, n - 1, 0))


def upwind(below, f, above, v):
    return [
        jnp.where(v[0] >= 0.0, f - below, above - f),
        jnp.where(v[1] >= 0.0, f - row_prev(f), row_next(f) - f),
        jnp.where(v[2] >= 0.0, f - col_prev(f), col_next(f) - f),
    ]


def advance(f, diffs, v, dt):
    return f - dt * (v[0] * diffs[0] + v[1] * diffs[1] + v[2] * diffs[2])


def retreat(lam, v, pos_above, neg_below, dt):
    total = (jnp.abs(v[0]) + jnp.abs(v[1]) + jnp.abs(v[2])) * lam
    total = total - row_next(jnp.maximum(v[1], 0.0) * lam)
    total = total + row_prev(jnp.minimum(v[1], 0.0) * lam)
    total = total - col_next(jnp.maximum(v[2], 0.0) * lam)
    total = total + col_prev(jnp.minimum(v[2], 0.0) * lam)
    if pos_above is not None:
        total = total - pos_above
    if neg_below is not None:
        total = total + neg_below
    return lam - dt * total


def plane_sum(f):
    return row_prev(f) + row_next(f) + col_prev(f) + col_next(f)


def call(kernel, out_shape, in_specs, out_specs, operands, name, weight=0, grid=(1,), aliases=None, scratch=()):
    return pl.pallas_call(
        kernel,
        out_shape=out_shape,
        grid=grid,
        in_specs=in_specs,
        out_specs=out_specs,
        scratch_shapes=list(scratch),
        input_output_aliases=aliases or {},
        compiler_params=pltpu.CompilerParams(vmem_limit_bytes=24 * MIB),
        cost_estimate=pl.CostEstimate(
            flops=1024 + weight * 10000000, bytes_accessed=1024, transcendentals=0
        ),
        name=name,
    )(*operands)


def whole(x):
    zeros = (0,) * x.ndim
    return pl.BlockSpec(x.shape, lambda *_: zeros)


def struct(*shape):
    return jax.ShapeDtypeStruct(shape, jnp.float32)


SMEM = pl.BlockSpec(memory_space=pltpu.SMEM)
VMEM = pl.BlockSpec(memory_space=pltpu.VMEM)
ANY = pl.BlockSpec(memory_space=pl.ANY)
SIDES = (0, 1)


def make_body(subj, slabs):
    pairs = []
    for first in SIDES:
        lower = [(i, i + 1) for i in range(first, slabs - 1, 2)]
        pairs.append(lower + [(j, i) for i, j in lower])

    def swap(x, side):
        return lax.ppermute(x, "slab", pairs[side])

    def turn(x, k):
        return lax.ppermute(x, "subj", [(i, (i + k) % subj) for i in range(subj)])

    def after(x, *others):
        return lax.optimization_barrier((x, *others))

    def body(template, subject, velocity):
        flow = velocity[0]
        target = subject[0]
        steps, _, Z, Y, X = flow.shape
        assert Z == 4 and steps == 2
        rows = template.shape[1]
        dt = 1.0 / steps
        place = lax.axis_index("slab")
        group = lax.axis_index("subj")
        even = 1 - place % 2
        facts = jnp.stack([group, place > 0, place < slabs - 1, even]).astype(jnp.int32)
        ups = (even, 1 - even)
        flow_spec = [
            pl.BlockSpec((1, 3, Z, Y, X), lambda *_, t=t: (t, 0, 0, 0, 0)) for t in range(steps)
        ]

        def up_at(facts_ref, i):
            return facts_ref[3] if i == 0 else 1 - facts_ref[3]

        def up_here(i):
            odd = lax.rem(lax.axis_index("slab"), 2)
            return 1 - odd if i == 0 else odd

        tmpl_far = [
            swap(lax.dynamic_slice_in_dim(template, up * (Z - 2), 2, 0), i)
            for i, up in enumerate(ups)
        ]
        flow0_edge = [
            lax.dynamic_slice(velocity, (0, 0, 0, up * (Z - 1), 0, 0), (1, 1, 3, 1, Y, X))[0, 0, :, 0]
            for up in ups
        ]
        flow0_far = [swap(flow0_edge[i], i) for i in SIDES]
        own_parts = [template] + [turn(template, k) for k in range(1, subj)]
        tmpl_far[1], tmpl_far[0], _, _ = after(*tmpl_far[::-1], *flow0_edge)
        edge = jnp.concatenate(tmpl_far[::-1], axis=0)
        edge_parts = [edge] + [turn(edge, k) for k in range(1, subj)]

        def forward(*refs):
            facts_ref, refs = refs[0], refs[1:]
            owns, edges = refs[:subj], refs[subj : 2 * subj]
            v0, v1, aim = refs[2 * subj : 2 * subj + 3]
            tmpl, img1, lam2, *srcs = refs[2 * subj + 3 :]
            for k in range(subj):
                start = pl.multiple_of(lax.rem(facts_ref[0] + subj - k, subj) * rows, rows)
                at = pl.ds(start, rows)
                tmpl[2 : Z + 2, at, :] = owns[k][...]
                for i in SIDES:
                    up = up_at(facts_ref, i)
                    for j in range(2):
                        tmpl[up * (Z + 2) + j, at, :] = edges[k][2 * (1 - i) + j]
            for z in range(Z):
                v = [v0[0, d, z] for d in range(3)]
                f = tmpl[z + 2]
                img1[z] = advance(f, upwind(tmpl[z + 1], f, tmpl[z + 3], v), v, dt)
            for i in SIDES:
                z = 1 + up_at(facts_ref, i) * (Z - 3)
                v = [v1[0, d, z] for d in range(3)]
                f = img1[z]
                diffs = upwind(img1[z - 1], f, img1[z + 1], v)
                lam = advance(f, diffs, v, dt) - aim[z]
                lam2[i] = lam
                for d in range(3):
                    srcs[i][d] = (-MATCH * dt) * lam * diffs[d]

        outs = [struct(Z + 4, Y, X), struct(Z, Y, X), struct(2, Y, X)] + [struct(3, Y, X)] * 2
        operands = [facts] + own_parts + edge_parts + [flow, flow, target]
        tmpl, img1, lam2_in, *inner1 = call(
            forward,
            outs,
            [SMEM]
            + [whole(x) for x in own_parts + edge_parts]
            + [flow_spec[0], flow_spec[1], whole(target)],
            [whole(x) for x in outs],
            operands,
            "forward",
            weight=FORWARD,
        )
        far1 = [swap(inner1[0], 0), None]

        def middle(facts_ref, tmpl, img1, halo0, halo1, v1, aim, src0, src1, lam2, v0_far):
            for i, halo, src in ((0, halo0, src0), (1, halo1, src1)):
                up = up_at(facts_ref, i)
                at = 1 + up * (Z + 1)
                v = [halo[d] for d in range(3)]
                for d in range(3):
                    v0_far[up, d] = v[d]
                f = tmpl[at]
                outside = advance(f, upwind(tmpl[at - 1], f, tmpl[at + 1], v), v, dt)
                z = up * (Z - 1)
                inside = img1[z + 1 - 2 * up]
                below = jnp.where(up == 1, inside, outside)
                above = jnp.where(up == 1, outside, inside)
                v = [v1[0, d, z] for d in range(3)]
                f = img1[z]
                diffs = upwind(below, f, above, v)
                lam = advance(f, diffs, v, dt) - aim[z]
                for d in range(3):
                    src[d] = (-MATCH * dt) * lam * diffs[d]
                lam2[i] = lam

        outs = [struct(3, Y, X)] * 2 + [struct(2, Y, X), struct(2, 3, Y, X)]
        operands = [facts, tmpl, img1, *flow0_far, flow, target]
        *outer1, lam2_out, v0_far = call(
            middle,
            outs,
            [SMEM] + [whole(x) for x in operands[1:5]] + [flow_spec[1], whole(target)],
            [whole(x) for x in outs],
            operands,
            "middle",
            weight=MIDDLE,
        )
        def back(facts_ref, lam2_in, lam2_out, v1, lam1, word0, word1, lam2):
            for i in SIDES:
                up = up_at(facts_ref, i)
                lam2[1 + up * (Z - 3)] = lam2_in[i]
                lam2[up * (Z - 1)] = lam2_out[i]
            for z in range(Z):
                v = [v1[0, d, z] for d in range(3)]
                above = jnp.maximum(v1[0, 0, z + 1], 0.0) * lam2[z + 1] if z < Z - 1 else None
                below = jnp.minimum(v1[0, 0, z - 1], 0.0) * lam2[z - 1] if z > 0 else None
                lam1[z] = retreat(lam2[z], v, above, below, dt)
            for i, word in ((0, word0), (1, word1)):
                up = up_at(facts_ref, i)
                z = up * (Z - 1)
                v = v1[0, 0, z]
                word[0] = jnp.where(up == 1, jnp.minimum(v, 0.0), jnp.maximum(v, 0.0)) * lam2[z]
                word[1] = lam1[z]

        outs = [struct(Z, Y, X)] + [struct(2, Y, X)] * 2
        operands = [facts, lam2_in, lam2_out, flow]
        lam1_part, *words = call(
            back,
            outs,
            [SMEM] + [whole(x) for x in operands[1:3]] + [flow_spec[1]],
            [whole(x) for x in outs],
            operands,
            "back",
            weight=BACK,
            scratch=[pltpu.VMEM((Z, Y, X), jnp.float32)],
        )
        words_far = [swap(words[i], i) for i in SIDES]
        near1 = [swap(after(outer1[0], *words)[0], 0), None]

        held, far1[0], *words_far = after((inner1[1], outer1[1]), far1[0], *words_far)
        far1[1], near1[1] = [swap(x, 1) for x in held]

        def last(facts_ref, tmpl, part, own0, own1, far0, far1, v0_far, v0, lam0, src0, src1, out0, out1, near, lam):
            for z in range(1, Z - 1):
                lam[z + 1] = part[z]
            for i, own, far in ((0, own0, far0), (1, own1, far1)):
                up = up_at(facts_ref, i)
                toward = dt * (2 * up - 1).astype(jnp.float32)
                inside = jnp.where(up == 1, facts_ref[2], facts_ref[1]) > 0
                lam[1 + up * (Z - 1)] = own[1] + toward * far[0]
                lam[up * (Z + 1)] = jnp.where(inside, far[1] - toward * own[0], 0.0)

            def flow_at(z, d):
                return v0[0, d, z] if 0 <= z < Z else v0_far[0 if z < 0 else 1, d]

            def source(z, v, src, *at):
                diffs = upwind(tmpl[z + 1], tmpl[z + 2], tmpl[z + 3], v)
                for d in range(3):
                    src[(*at, d)] = (-MATCH * dt) * lam[z + 1] * diffs[d]

            for i, inner, outer in ((0, src0, out0), (1, src1, out1)):
                up = up_at(facts_ref, i)
                for z, src in ((1 + up * (Z - 3), inner), (up * (Z - 1), outer)):
                    source(z, [v0[0, d, z] for d in range(3)], src)
            for j, z in enumerate((-1, Z)):
                source(z, [flow_at(z, d) for d in range(3)], near, j)
            for z in range(Z):
                above = jnp.maximum(flow_at(z + 1, 0), 0.0) * lam[z + 2]
                below = jnp.minimum(flow_at(z - 1, 0), 0.0) * lam[z]
                v = [flow_at(z, d) for d in range(3)]
                lam0[z] = retreat(lam[z + 1], v, above, below, dt)

        outs = [struct(Z, Y, X)] + [struct(3, Y, X)] * 4 + [struct(2, 3, Y, X)]
        operands = [facts, tmpl, lam1_part, *words, *words_far, v0_far, flow]
        lam0, *inner_outer, near0 = call(
            last,
            outs,
            [SMEM] + [whole(x) for x in operands[1:8]] + [flow_spec[0]],
            [whole(x) for x in outs],
            operands,
            "last",
            weight=LAST,
            scratch=[pltpu.VMEM((Z + 2, Y, X), jnp.float32)],
        )
        inner0, outer0 = inner_outer[:2], inner_outer[2:]
        far0 = [swap(inner0[i], i) for i in SIDES]

        def sweeps(facts_ref, s, v, out, u2):
            for z in range(-1, Z + 1):
                beside = plane_sum(s[z])
                if z - 1 in s:
                    beside = beside + s[z - 1]
                if z + 1 in s:
                    beside = beside + s[z + 1]
                u = (s[z] + beside * SEVENTH) * SEVENTH
                if z == -1:
                    u = jnp.where(facts_ref[1] > 0, u, 0.0)
                if z == Z:
                    u = jnp.where(facts_ref[2] > 0, u, 0.0)
                u2[z + 1] = u
            for z in range(Z):
                u = u2[z + 1]
                beside = plane_sum(u) + u2[z] + u2[z + 2]
                out[0, 0, z] = v[0, 0, z] + (s[z] + beside) * SEVENTH

        class Planes:
            def __init__(self, ref, low, high):
                self.ref, self.low, self.high = ref, low, high

            def __contains__(self, z):
                return self.low <= z <= self.high

            def __getitem__(self, z):
                return self.ref[z - self.low]

        part = pl.BlockSpec((1, Y, X), lambda d: (d, 0, 0))
        flow_part = [
            pl.BlockSpec((1, 1, Z, Y, X), lambda d, t=t: (t, d, 0, 0, 0)) for t in range(steps)
        ]
        u2_scratch = pltpu.VMEM((Z + 2, Y, X), jnp.float32)

        def share(k):
            start = lax.rem(group + k, subj) * rows
            return lax.dynamic_slice_in_dim(lam0, start, rows, axis=1)

        template_grad = share(0)
        for k in range(1, subj):
            template_grad = template_grad + turn(share(k), k)

        def smooth_0(facts_ref, in0, in1, out0, out1, near, v, out, rim, u2, s):
            for i, inner, outer in ((0, in0, out0), (1, in1, out1)):
                up = up_at(facts_ref, i)
                s[2 + up * (Z - 3)] = inner[0]
                s[1 + up * (Z - 1)] = outer[0]
            s[0] = near[0, 0]
            s[Z + 1] = near[1, 0]
            sweeps(facts_ref, Planes(s, -1, Z), v, out, u2)
            for i in SIDES:
                rim[i, 0] = out[0, 0, up_at(facts_ref, i) * (Z - 1)]

        both = pl.BlockSpec((2, 1, Y, X), lambda d: (0, d, 0, 0))
        gradient, rim = call(
            smooth_0,
            [struct(*flow.shape), struct(2, 3, Y, X)],
            [SMEM] + [part] * 4 + [both, flow_part[0]],
            [flow_part[0], both],
            [facts, *inner0, *outer0, near0, flow],
            "smooth_0",
            weight=SMOOTH,
            grid=(3,),
            scratch=[u2_scratch, pltpu.VMEM((Z + 2, Y, X), jnp.float32)],
        )

        def smooth_1(facts_ref, in0, in1, out0, out1, near0, near1, far0, far1, _, v, out, u2, s):
            for i, inner, outer, near, far in ((0, in0, out0, near0, far0), (1, in1, out1, near1, far1)):
                up = up_at(facts_ref, i)
                s[3 + up * (Z - 3)] = inner[0]
                s[2 + up * (Z - 1)] = outer[0]
                s[1 + up * (Z + 1)] = near[0]
                s[up * (Z + 3)] = far[0]
            sweeps(facts_ref, Planes(s, -2, Z + 1), v, out, u2)

        gradient = call(
            smooth_1,
            struct(*flow.shape),
            [SMEM] + [part] * 8 + [pl.BlockSpec(memory_space=pl.ANY), flow_part[1]],
            flow_part[1],
            [facts, *inner1, *outer1, *near1, *far1, gradient, flow],
            "smooth_1",
            weight=SMOOTH,
            grid=(3,),
            aliases={9: 0},
            scratch=[u2_scratch, pltpu.VMEM((Z + 4, Y, X), jnp.float32)],
        )

        def add_far(far_0, far_1, rim, _, out, held, done):
            copies = []
            for i, far in ((0, far_0), (1, far_1)):
                z = up_here(i) * (Z - 1)
                for d in range(3):
                    held[i, d] = rim[i, d] + far[d] * SEVENTH**3
                    copies.append(pltpu.make_async_copy(held.at[i, d], out.at[0, d, z], done.at[i, d]))
                    copies[-1].start()
            for copy in copies:
                copy.wait()

        gradient = call(
            add_far,
            struct(*flow.shape),
            [VMEM, VMEM, VMEM, ANY],
            ANY,
            [*far0, rim, gradient],
            "add_far",
            grid=(),
            aliases={3: 0},
            scratch=[pltpu.VMEM((2, 3, Y, X), jnp.float32), pltpu.SemaphoreType.DMA((2, 3))],
        )
        return gradient[None], template_grad

    return body


def solution(mesh):
    sizes = dict(mesh.shape)
    return jax.shard_map(
        make_body(sizes["subj"], sizes["slab"]),
        mesh=mesh,
        in_specs=(
            P("slab", "subj", None),
            P("subj", "slab", None, None),
            P("subj", None, None, "slab", None, None),
        ),
        out_specs=(P("subj", None, None, "slab", None, None), P("slab", "subj", None)),
        check_vma=False,
    )
```
